32 devices in a mesh: dp: 16 (over z, y, x), pair: 2 (over core).
Axes of the slice: x: 2, y: 2, z: 4, core: 2. Of those that a mesh axis runs over, the one named last changes fastest.
Arguments:
- hidden: bfloat16 [16384, 1024], P('dp'), may hold values from -6 to 6
- doc_lengths: int32 [16, 8], P('dp'), may hold values from 1 to 512, 1024 in all within a row
- ln_gain: float32 [1024], replicated, may hold values from 0.5 to 1.5
- ln_bias: float32 [1024], replicated, may hold values from -3 to 3
- qkv_weight: bfloat16 [1024, 3072], replicated, may hold values from -0.1875 to 0.1875
- qkv_bias: float32 [3072], replicated, may hold values from -3 to 3
- dense_weight: bfloat16 [1024, 1024], replicated, may hold values from -1.5 to 1.5
- dense_bias: float32 [1024], replicated, may hold values from -2 to 2
- fc_in_weight: bfloat16 [1024, 4096], replicated, may hold values from -0.1875 to 0.1875
- fc_in_bias: float32 [4096], replicated, may hold values from -3 to 3
- fc_out_weight: bfloat16 [4096, 1024], replicated, may hold values from -0.09375 to 0.09375
- fc_out_bias: float32 [1024], replicated, may hold values from -2 to 2
- cotangent: bfloat16 [16384, 1024], P('dp'), may hold values from -6 to 6
Outputs:
- output: bfloat16 [16384, 1024], P(('dp', 'pair'))
- input_grad: bfloat16 [16384, 1024], P('dp')
- qkv_weight_grad: float32 [1024, 3072], P(('dp', 'pair'))
- qkv_bias_grad: float32 [3072], P(('dp', 'pair'))
- dense_weight_grad: float32 [1024, 1024], P(('dp', 'pair'))
- dense_bias_grad: float32 [1024], P(('dp', 'pair'))
- fc_in_weight_grad: float32 [1024, 4096], P(('dp', 'pair'))
- fc_in_bias_grad: float32 [4096], P(('dp', 'pair'))
- fc_out_weight_grad: float32 [4096, 1024], P(('dp', 'pair'))
- fc_out_bias_grad: float32 [1024], P(('dp', 'pair'))
- ln_gain_grad: float32 [1024], P(('dp', 'pair'))
- ln_bias_grad: float32 [1024], P(('dp', 'pair'))
The draws below stay inside these ranges and needn't reach their ends.
Inputs may be any that keep to these rules, and one draw needn't show every extreme that they name: `doc_lengths`: each row holds the lengths of the 8 documents packed into one sequence, in order; they sum to 1024, and in every row one document has 512 tokens.
All inputs are finite; a program needn't handle non-finite values.
Results may differ from the reference program's by a relative error of at most 0.011.
Values may be sent and summed in bfloat16 or wider, within the bound.
A program may use at most 448 MiB of HBM per device.

```python
import math
import jax
import jax.numpy as jnp
import numpy as np
from jax import lax

D = 1024
HEADS = 16
HEAD = 64
ROT = 16
FF = 4096
SEQ_LEN = 1024
DOCS = 8
DOC_MOST = 512
SEQS = 16
TOKENS = 16384


def strengthened(result, own_key, source, target, shards_of, factor):
    owner, partner = [(jnp.arange(result.shape[position]) // (result.shape[position] // shards_of)).reshape([-1 if axis == position else 1 for axis in range(result.ndim)]) for position in (source, target)]
    chosen = jax.random.permutation(own_key, shards_of)[partner]
    strong = (owner == chosen) | (owner == (partner + shards_of // 2) % shards_of)
    return jnp.where(strong, factor * result, result)


def levels(own_key, extent, cuts, least, top_value):
    factor_of, own = 1.0, jax.random.fold_in(own_key, 6)
    for axis_at, parts in cuts:
        steps = jnp.exp(jax.random.uniform(jax.random.fold_in(own, axis_at), (parts,), jnp.float32, least / len(cuts), top_value / len(cuts)))
        factor_of = factor_of * jnp.repeat(steps, extent[axis_at] // parts).reshape([-1 if axis == axis_at else 1 for axis in range(len(extent))])
    return factor_of


def split_up(amount, total, reach, slope):
    loads = [(1 << 20) // math.isqrt(standing ** slope) + 1 for standing in range(2, amount + 1)]
    surplus, counts = total - reach - (amount - 1), [1] * (amount - 1)
    while surplus > 0:
        movable = [i for i in range(amount - 1) if counts[i] < reach]
        pool, left = sum([loads[i] for i in movable]), surplus
        for i in movable:
            extra = min(reach - counts[i], max(1, left * loads[i] // pool), surplus)
            counts[i] = counts[i] + extra
            surplus = surplus - extra
    return np.array([reach] + counts)


def uneven(rng, number_of, total, bound, slope):
    if number_of == 2:
        one = jax.random.randint(rng, (), max(1, total - bound), min(bound, total - 1) + 1)
        return jnp.stack([one, total - one])
    sizes = jnp.asarray(split_up(number_of, total, bound, slope), jnp.int32)
    pairs = (number_of - 1) // 2
    source_of, sink = sizes[1:1 + 2 * pairs:2], sizes[2:2 + 2 * pairs:2]
    margin = jnp.minimum(source_of - 1, bound - sink)
    shifted = jax.random.randint(jax.random.fold_in(rng, 1), (pairs,), 0, 1 << 20) % (margin + 1)
    sizes = sizes.at[1:1 + 2 * pairs:2].set(source_of - shifted).at[2:2 + 2 * pairs:2].set(sink + shifted)
    return sizes[jax.random.permutation(jax.random.fold_in(rng, 2), number_of)]


def noise(own_key, dims, width, limit, pieces=(), held_as=jnp.bfloat16):
    entries = jax.random.normal(own_key, dims, jnp.float32) * width
    if len(pieces) > 0:
        entries = levels(own_key, dims, pieces, -0.22, 0.18) * entries
    return jnp.clip(entries, min=-limit, max=limit).astype(held_as)


def gaussian_with(own_key, dims, scale, bound, split, heavy, kind=jnp.bfloat16):
    entries = scale * jax.random.normal(own_key, dims, jnp.float32)
    if split:
        entries = entries * levels(own_key, dims, split, -0.22, 0.18)
    return jnp.clip(strengthened(entries, jax.random.fold_in(own_key, 3), *heavy), -bound, bound).astype(kind)


def setup_inputs(seed: int = 0) -> dict:
    seeds = jax.random.split(jax.random.key(seed), 14)
    hidden = noise(seeds[0], (TOKENS, D), 1.0, 6.0, ((0, 16),))
    doc_lengths = jax.vmap(lambda own: uneven(own, DOCS, SEQ_LEN, DOC_MOST, 2))(jax.random.split(seeds[1], SEQS)).reshape((SEQS, DOCS)).astype(jnp.int32)
    ln_gain = jnp.clip(1.0 + 0.1 * jax.random.normal(seeds[2], (D,), jnp.float32), 0.5, 1.5)
    ln_bias = noise(seeds[3], (D,), 0.5, 3.0, (), jnp.float32)
    qkv_weight = noise(seeds[4], (D, 3 * D), D ** -0.5, 0.1875)
    qkv_bias = noise(seeds[5], (3 * D,), 0.5, 3.0, (), jnp.float32)
    dense_weight = noise(seeds[6], (D, D), (D // 64) ** -0.5, 1.5)
    dense_bias = noise(seeds[7], (D,), 0.3, 2.0, (), jnp.float32)
    fc_in_weight = noise(seeds[8], (D, FF), D ** -0.5, 0.1875)
    fc_in_bias = noise(seeds[9], (FF,), 0.5, 3.0, (), jnp.float32)
    fc_out_weight = noise(seeds[10], (FF, D), FF ** -0.5, 0.09375)
    fc_out_bias = noise(seeds[11], (D,), 0.3, 2.0, (), jnp.float32)
    cotangent = gaussian_with(seeds[12], (TOKENS, D), 1.0, 6.0, ((0, 16),), (0, 1, 16, 2.0))
    return dict(hidden=hidden, doc_lengths=doc_lengths, ln_gain=ln_gain, ln_bias=ln_bias, qkv_weight=qkv_weight, qkv_bias=qkv_bias, dense_weight=dense_weight, dense_bias=dense_bias, fc_in_weight=fc_in_weight, fc_in_bias=fc_in_bias, fc_out_weight=fc_out_weight, fc_out_bias=fc_out_bias, cotangent=cotangent)


@jax.custom_vjp
def low(v):
    return lax.optimization_barrier(v.astype(jnp.bfloat16)).astype(jnp.float32)

@jax.custom_vjp
def low_back(v):
    return v

def low_keep(v):
    return (low(v), None)

def low_pass(kept, grad):
    return (grad,)

def back_keep(v):
    return (v, None)

def back_low(kept, grad):
    return (low(grad),)
low.defvjp(low_keep, low_pass)
low_back.defvjp(back_keep, back_low)
norm_epsilon = 1e-05
highest = lax.Precision.HIGHEST

def token_tables(lengths):
    doc_ends = jnp.cumsum(lengths).astype(jnp.int32)
    doc_starts = (doc_ends - lengths).astype(jnp.int32)
    places = jnp.arange(SEQ_LEN, dtype=jnp.int32)
    doc_of = lax.optimization_barrier(jnp.sum((places[:, None] >= doc_ends[None, :]).astype(jnp.int32), axis=1))
    picked = doc_of[:, None] == jnp.arange(DOCS, dtype=jnp.int32)[None, :]
    start_of = lax.optimization_barrier(jnp.sum(jnp.where(picked, doc_starts[None, :], 0), axis=1)).astype(jnp.int32)
    positions = places - start_of
    inverse = 10000.0 ** (-(jnp.arange(0, ROT, 2, dtype=jnp.float32) / ROT))
    angles = positions.astype(jnp.float32)[:, None] * inverse[None, :]
    cosines = jnp.concatenate([jnp.cos(angles), jnp.cos(angles)], axis=1)
    sines = jnp.concatenate([jnp.sin(angles), jnp.sin(angles)], axis=1)
    allowed = (doc_of[:, None] == doc_of[None, :]) & (places[None, :] <= places[:, None])
    return (allowed, cosines, sines)

def rotate(values, cosines, sines):
    half_rot = ROT // 2
    turned_part = values[..., :ROT]
    swapped = jnp.concatenate([-turned_part[..., half_rot:], turned_part[..., :half_rot]], axis=-1)
    turned = turned_part * cosines[:, None, :] + swapped * sines[:, None, :]
    return jnp.concatenate([turned, values[..., ROT:]], axis=-1)

def layer_seq(inputs, lengths, weights):
    gain, shift, w_qkv, b_qkv, w_dense, b_dense, w_in, b_in, w_out, b_out = weights
    row_mean = lax.optimization_barrier(jnp.mean(inputs, axis=1, keepdims=True))
    centred = inputs - row_mean
    variance = lax.optimization_barrier(jnp.mean(centred * centred, axis=1, keepdims=True))
    normed = low_back(low(centred * lax.rsqrt(variance + norm_epsilon) * gain + shift))
    allowed, cosines, sines = token_tables(lengths)
    raw = low_back(jnp.dot(normed, w_qkv, precision=highest) + b_qkv)
    head_shape = (SEQ_LEN, HEADS, HEAD)
    queries = low(rotate(raw[:, :D].reshape(head_shape), cosines, sines))
    keys_f = low(rotate(raw[:, D:2 * D].reshape(head_shape), cosines, sines))
    values_f = low(raw[:, 2 * D:].reshape(head_shape))
    scores = low_back(jnp.einsum('qhd,khd->hqk', queries, keys_f, precision=highest) * HEAD ** (-0.5))
    scores = jnp.where(allowed[None], scores, -1000000000.0)
    probs = low(jax.nn.softmax(scores, axis=2))
    context = jnp.einsum('hqk,khd->qhd', probs, values_f, precision=highest).reshape(SEQ_LEN, D)
    context = low_back(low(context))
    attention = low_back(low(jnp.dot(context, w_dense, precision=highest) + b_dense))
    pre_act = low_back(jnp.dot(normed, w_in, precision=highest) + b_in)
    act = low(jax.nn.gelu(pre_act, approximate=False))
    mlp_out = low_back(low(jnp.dot(act, w_out, precision=highest) + b_out))
    return inputs + attention + mlp_out

def reference(hidden, doc_lengths, ln_gain, ln_bias, qkv_weight, qkv_bias, dense_weight, dense_bias, fc_in_weight, fc_in_bias, fc_out_weight, fc_out_bias, cotangent):
    params = tuple((item.astype(jnp.float32) for item in (ln_gain, ln_bias, qkv_weight, qkv_bias, dense_weight, dense_bias, fc_in_weight, fc_in_bias, fc_out_weight, fc_out_bias)))
    inputs = hidden.astype(jnp.float32).reshape(SEQS, SEQ_LEN, D)
    grads_in = cotangent.astype(jnp.float32).reshape(SEQS, SEQ_LEN, D)

    def forward(inputs_all, *weights):

        def step(running, item):
            seq_inputs, lengths = item
            return (running, layer_seq(seq_inputs, lengths, weights))
        unused, outputs = lax.scan(jax.checkpoint(step), jnp.zeros((), jnp.float32), (inputs_all, doc_lengths))
        return outputs
    outputs, pullback = jax.vjp(forward, inputs, *params)
    grads = pullback(grads_in)
    return (outputs.reshape(TOKENS, D).astype(jnp.bfloat16), grads[0].reshape(TOKENS, D).astype(jnp.bfloat16), grads[3], grads[4], grads[5], grads[6], grads[7], grads[8], grads[9], grads[10], grads[1], grads[2])
```

```python
from functools import partial

import jax
import jax.numpy as jnp
import numpy as np
from jax import lax
from jax.experimental import pallas as pl
from jax.experimental.pallas import tpu as pltpu
from jax.sharding import PartitionSpec as P

F32, BF = jnp.float32, jnp.bfloat16
MESH = pl.DeviceIdType.MESH
EPS = 1e-05
SEQ, D, FF, HEAD, ROT, DOCS = 1024, 1024, 4096, 64, 16, 8
INNER = 16
ORDER_A, ORDER_B = (0, 2, 1, 3), (1, 2, 0, 3)
LAGS = (1, 2, 3, 4)


def dot(a, b):
    return lax.dot_general(a, b, (((1,), (0,)), ((), ())), preferred_element_type=F32)


def dot_t(a, b):
    return lax.dot_general(a, b, (((1,), (1,)), ((), ())), preferred_element_type=F32)


def t_dot(a, b):
    return lax.dot_general(a, b, (((0,), (0,)), ((), ())), preferred_element_type=F32)


def loop(n, body, first=0):
    def step(i, c):
        body(i)
        return c

    lax.fori_loop(first, n, step, 0)


def at_multiple(start, size, of=None):
    return pl.ds(pl.multiple_of(start, of or size), size)


class Scope:
    pass


SCRATCH = (
    ("A", (3, SEQ, D), BF),
    ("ACC", (2, SEQ, D), F32),
    ("WA", (2, D, 768), BF),
    ("WB", (D, D), BF),
    ("PD", (SEQ, 512), F32),
    ("QKV", (SEQ, 768), BF),
    ("DR", (SEQ, 768), BF),
    ("GW", (16, 2, 2, 2, 2, 64, 256), BF),
    ("RW1", (16, 2, 2, 2, 64, 256), BF),
    ("RW2", (16, 2, 2, 64, 256), BF),
    ("RW3", (16, 2, 64, 256), BF),
    ("RW4", (16, 64, 256), BF),
    ("GO", (16, 256, D), BF),
    ("RO1A", (8, 256, 512), BF),
    ("RO2A", (4, 256, 512), BF),
    ("RO3A", (2, 256, 512), BF),
    ("RO4A", (256, 512), BF),
    ("RO1B", (4, 2, 256, 512), BF),
    ("RO2B", (2, 2, 256, 512), BF),
    ("RO3B", (2, 256, 512), BF),
    ("RO4B", (256, 512), BF),
    ("bcol", (8, 4096), F32),
    ("bsum", (8, D), F32),
    ("lnsum", (2, 8, D), F32),
    ("VEC", (8, D), F32),
    ("VRECV", (4, 8, D), F32),
    ("VPART", (8, D), F32),
)
SEMS = (
    ("lsem", (2, 2)),
    ("hsem", (6,)),
    ("qsem", (2, 3)),
    ("ws", (16, 4)),
    ("wr", (16, 4)),
    ("os", (8, 2, 4)),
    ("orr", (8, 2, 4)),
    ("vs", (5,)),
    ("vr", (5,)),
    ("xs", (4,)),
    ("xr", (4,)),
    ("fs", (5,)),
    ("fr", (5,)),
    ("fl", (7,)),
)
INPUTS = ("hidden", "lens", "gain", "shift", "w_qkv", "b_qkv", "w_dense", "b_dense", "w_in", "b_in", "w_out", "b_out", "cot")
OUTPUTS = ("o_out", "o_ig", "o_qkv", "o_dense", "o_in", "o_outw", "o_vec")


class Reducer:
    def __init__(self, s, extra):
        self.s, self.extra = s, extra
        dp = lax.axis_index("dp")
        inner = dp // extra
        self.dp, self.pr = dp, lax.axis_index("pair")
        self.bits = [inner % 2, (inner // 2) % 2, (inner // 4) % 2, inner // 8]
        self.partner = [dp + (1 - 2 * self.bits[b]) * (extra << b) for b in range(4)]

    def to(self, src, dst, ss, rs, b):
        return pltpu.make_async_remote_copy(
            src_ref=src, dst_ref=dst, send_sem=ss, recv_sem=rs, device_id=(self.partner[b], self.pr), device_id_type=MESH
        )

    def w_half(self, order, st, u, bit):
        s = self.s
        if st == 0:
            return s.GW.at[u, :, :, :, bit] if order == ORDER_A else s.GW.at[u, :, :, bit]
        if st == 1:
            return s.RW1.at[u, :, bit]
        if st == 2:
            return s.RW2.at[u, :, bit]
        return s.RW3.at[u, bit]

    def w_copy(self, order, st, u):
        s, b = self.s, order[st]
        dst = (s.RW1, s.RW2, s.RW3, s.RW4)[st].at[u]
        return self.to(self.w_half(order, st, u, 1 - self.bits[b]), dst, s.ws.at[u, st], s.wr.at[u, st], b)

    def w_finish(self, order, st, u, col):
        s, b = self.s, order[st]
        self.w_copy(order, st, u).wait_recv()
        kept = self.w_half(order, st, u, self.bits[b])
        got = (s.RW1, s.RW2, s.RW3, s.RW4)[st].at[u]
        if st < 3:
            lead = got.shape[0]
            for i in range(lead):
                got[i] = (got[i].astype(F32) + kept[i].astype(F32)).astype(BF)
            self.w_copy(order, st + 1, u).start()
        else:
            rows, lanes = at_multiple(64 * (col // 1024), 64), at_multiple(lax.rem(col, 1024), 256)
            s.ACC[0, rows, lanes] = got[...].astype(F32) + kept[...].astype(F32)

    def o_bits(self, c):
        return {1: c % 2, 2: (c // 2) % 2, 3: c // 4}

    def o_plan(self, order, st, c):
        s, x = self.s, self.bits[0]
        own = self.o_bits(c)
        same = {b: self.bits[b] == own[b] for b in (1, 2, 3)}
        zc, yc, hc = (c // 2) % 2, c % 2, c // 4
        n = 0 if order == ORDER_A else 1
        sems = (s.os.at[c, n, st], s.orr.at[c, n, st])
        everyone = c >= 0
        if order == ORDER_A:
            lanes = pl.ds(0, 512)
            if st == 0:
                return everyone, everyone, self.to(s.GO.at[2 * c + 1 - x, :, lanes], s.RO1A.at[c], *sems, 0), s.RO1A.at[c]
            if st == 1:
                dst = s.RO2A.at[2 * hc + yc]
                return everyone, same[2], self.to(s.RO1A.at[c], dst, *sems, 2), dst
            if st == 2:
                dst = s.RO3A.at[hc]
                return same[2], same[2] & same[1], self.to(s.RO2A.at[2 * hc + yc], dst, *sems, 1), dst
            part = same[2] & same[1]
            return part, part & same[3], self.to(s.RO3A.at[hc], s.RO4A, *sems, 3), s.RO4A
        lanes = pl.ds(512, 512)
        if st == 0:
            dst = s.RO1B.at[c // 2]
            return everyone, same[1], self.to(s.GO.at[pl.ds(2 * c, 2), :, lanes], dst, *sems, 1), dst
        if st == 1:
            dst = s.RO2B.at[hc]
            return same[1], same[1] & same[2], self.to(s.RO1B.at[c // 2], dst, *sems, 2), dst
        part = same[1] & same[2]
        if st == 2:
            dst = s.RO3B.at[hc]
            return part, part, self.to(s.RO2B.at[hc, 1 - x], dst, *sems, 0), dst
        return part, part & same[3], self.to(s.RO3B.at[hc], s.RO4B, *sems, 3), s.RO4B

    def o_sends(self, order, st):
        return (order == ORDER_A and st == 0) or (order == ORDER_B and st == 2)

    def o_start(self, order, st, c):
        part, takes, copy, _ = self.o_plan(order, st, c)
        if self.o_sends(order, st):
            pl.when(part)(lambda: copy.start())
        else:
            pl.when(part & jnp.logical_not(takes))(lambda: copy.start())

    def o_wait_sent(self, order, st, c):
        part, takes, copy, _ = self.o_plan(order, st, c)
        if self.o_sends(order, st):
            pl.when(part)(lambda: copy.wait_send())
        else:
            pl.when(part & jnp.logical_not(takes))(lambda: copy.wait_send())

    def o_finish(self, order, st, c):
        s, x = self.s, self.bits[0]
        _, takes, copy, got = self.o_plan(order, st, c)
        zc, yc, hc = (c // 2) % 2, c % 2, c // 4
        lanes = pl.ds(0, 512) if order == ORDER_A else pl.ds(512, 512)
        if order == ORDER_A:
            kept = (s.GO.at[2 * c + x, :, lanes], s.RO1A.at[c], s.RO2A.at[2 * hc + yc], s.RO3A.at[hc])[st]
        else:
            kept = (s.GO.at[pl.ds(2 * c, 2), :, lanes], s.RO1B.at[c // 2], s.RO2B.at[hc, x], s.RO3B.at[hc])[st]

        @pl.when(takes)
        def _():
            copy.wait_recv()
            if st == 3:
                s.ACC[0, 256:512, lanes] = got[...].astype(F32) + kept[...].astype(F32)
            elif len(got.shape) == 3:
                for i in range(2):
                    got[i] = (got[i].astype(F32) + kept[i].astype(F32)).astype(BF)
            else:
                got[...] = (got[...].astype(F32) + kept[...].astype(F32)).astype(BF)

        if st < 3:
            self.o_start(order, st + 1, c)


def layer_norm(load_rows, gain, shift, nb):
    def tile(i):
        x = load_rows(i).astype(F32)
        mean = jnp.mean(x, axis=1, keepdims=True)
        cen = x - mean
        inv = lax.rsqrt(jnp.mean(cen * cen, axis=1, keepdims=True) + EPS)
        nb[at_multiple(i * 128, 128), :] = (cen * inv * gain + shift).astype(BF)

    loop(8, tile)


A1, A2, A3, A4, A5 = 0.254829592, -0.284496736, 1.421413741, -1.453152027, 1.061405429


def gelu_both(x):
    e = jnp.exp(-0.5 * (x * x))
    t = 1.0 / (1.0 + (0.3275911 * 0.7071067811865476) * jnp.abs(x))
    poly = ((((0.5 * A5) * t + (0.5 * A4)) * t + (0.5 * A3)) * t + (0.5 * A2)) * t + (0.5 * A1)
    q = poly * t * e
    cdf = jnp.where(x >= 0, 1.0 - q, q)
    return cdf, x * (e * 0.3989422804014327)


def load_inputs(s):
    hc = [pltpu.make_async_copy(s.hidden.at[pl.ds(256 * j, 256)], s.GO.at[12 + j], s.hsem.at[j]) for j in range(4)]
    gc = pltpu.make_async_copy(s.cot, s.A.at[1], s.hsem.at[4])
    for cp in hc:
        cp.start()
    gc.start()
    return hc, gc


def staged_rows(s):
    return lambda i: s.GO[12 + i // 2, at_multiple(128 * lax.rem(i, 2), 128), :]


def feed_role(s, rs, enter):
    nb, g = s.A.at[0], s.A.at[1]
    dn, out = s.ACC.at[0], s.ACC.at[1]

    def weights(c, slot):
        cols = at_multiple(c * 512, 512)
        return (
            pltpu.make_async_copy(s.w_in.at[:, cols], s.WA.at[slot, :, pl.ds(0, 512)], s.lsem.at[0, slot]),
            pltpu.make_async_copy(s.w_out.at[cols, :], s.WB.at[at_multiple(512 * slot, 512)], s.lsem.at[1, slot]),
        )

    hc, gc = load_inputs(s)
    for cp in weights(0, 0):
        cp.start()
    for cp in hc:
        cp.wait()
    layer_norm(staged_rows(s), s.gain[...], s.shift[...], nb)
    gc.wait()
    s.bsum[...] = jnp.zeros((8, D), F32)

    def prepare(i):
        at = at_multiple(i * 128, 128)
        s.bsum[...] += jnp.sum(g[at, :].astype(F32).reshape(16, 8, D), axis=0)
        dn[at, :] = jnp.zeros((128, D), F32)
        out[at, :] = jnp.zeros((128, D), F32)

    loop(8, prepare)
    enter()

    def progress(t):
        @pl.when(t < 8)
        def _():
            rs.w_copy(ORDER_A, 0, 2 * t).start()
            rs.w_copy(ORDER_B, 0, 2 * t + 1).start()
            rs.o_start(ORDER_A, 0, t)
            rs.o_start(ORDER_B, 0, t)

        for st in range(3):
            c = t - LAGS[st]

            @pl.when((c >= 0) & (c < 8))
            def _(st=st, c=c):
                rs.w_finish(ORDER_A, st, 2 * c, 512 * c)
                rs.w_finish(ORDER_B, st, 2 * c + 1, 512 * c + 256)
                rs.o_finish(ORDER_A, st, c)
                rs.o_finish(ORDER_B, st, c)

    def chunk(c):
        slot = lax.rem(c, 2)

        @pl.when(c < 7)
        def _():
            for cp in weights(c + 1, 1 - slot):
                cp.start()

        for cp in weights(c, slot):
            cp.wait()
        win, wout = s.WA.at[slot, :, pl.ds(0, 512)], s.WB.at[at_multiple(512 * slot, 512)]
        cols = at_multiple(c * 512, 512)
        bias = s.b_in[:, cols]
        bacc = jnp.zeros((8, 512), F32)
        for rt in range(2):
            rows = pl.ds(512 * rt, 512)
            s.PD[0:512, :] = dot(nb[rows, :], win[...]) + bias
            s.PD[512:1024, :] = dot_t(g[rows, :], wout[...])
            for q in range(4):
                r, r2, ro = pl.ds(128 * q, 128), pl.ds(512 + 128 * q, 128), pl.ds(512 * rt + 128 * q, 128)
                pre = s.PD[r, :]
                cdf, xphi = gelu_both(pre)
                s.QKV[ro, 0:512] = (pre * cdf).astype(BF)
                dp = (s.PD[r2, :] * (cdf + xphi)).astype(BF)
                s.DR[ro, 0:512] = dp
                bacc = bacc + jnp.sum(dp.astype(F32).reshape(16, 8, 512), axis=0)
            for h in range(2):
                part = pl.ds(512 * rt + 256 * h, 256)
                out[part, :] += dot(s.QKV[part, 0:512], wout[...])
                dn[part, :] += dot_t(s.DR[part, 0:512], win[...])
        s.bcol[:, cols] = bacc
        for q in range(4):
            tile = t_dot(nb[:, pl.ds(256 * q, 256)], s.DR[:, 0:512]).astype(BF)
            for i in range(2):
                s.GW[2 * c + i, q // 2, q % 2] = tile[:, 256 * i : 256 * i + 256].reshape(2, 2, 64, 256)
        for i in range(2):
            s.GO[2 * c + i] = t_dot(s.QKV[:, 256 * i : 256 * i + 256], g[...]).astype(BF)
        progress(c)

    loop(8, chunk)
    for j in range(4):
        s.VEC[j : j + 1, :] = jnp.sum(s.bcol[:, 1024 * j : 1024 * j + 1024], axis=0, keepdims=True)
    s.VEC[4:5, :] = jnp.sum(s.bsum[...], axis=0, keepdims=True)
    s.VEC[5:8, :] = jnp.zeros((3, D), F32)

    def finish_all():
        def units(c):
            rs.w_finish(ORDER_A, 3, 2 * c, 512 * c)
            rs.w_finish(ORDER_B, 3, 2 * c + 1, 512 * c + 256)
            rs.o_finish(ORDER_A, 3, c)
            rs.o_finish(ORDER_B, 3, c)

        loop(8, units)

    def wait_sent():
        def units(c):
            for st in range(4):
                rs.w_copy(ORDER_A, st, 2 * c).wait_send()
                rs.w_copy(ORDER_B, st, 2 * c + 1).wait_send()
                rs.o_wait_sent(ORDER_A, st, c)
                rs.o_wait_sent(ORDER_B, st, c)

        loop(8, units)

    return progress, finish_all, wait_sent


def attention_role(s, rs, enter):
    nb, g, dcT = s.A.at[0], s.A.at[1], s.A.at[2]
    dn, S1 = s.ACC.at[0], s.ACC.at[1]

    def weights(gr, slot):
        return [
            pltpu.make_async_copy(
                s.w_qkv.at[:, at_multiple(j * 1024 + gr * 256, 256)], s.WA.at[slot, :, pl.ds(256 * j, 256)], s.qsem.at[slot, j]
            )
            for j in range(3)
        ]

    hc, gc = load_inputs(s)
    for cp in weights(0, 0):
        cp.start()
    dc = pltpu.make_async_copy(s.w_dense, s.WB, s.lsem.at[1, 0])
    dc.start()
    place = lax.broadcasted_iota(jnp.int32, (8, SEQ), 1)
    start = jnp.zeros((8, SEQ), jnp.int32)
    end = jnp.int32(0)
    for d in range(DOCS - 1):
        end = end + s.lens[0, d]
        start = jnp.where(place >= end, end, start)
    inv = np.float32(10000.0) ** (-(np.arange(0, ROT, 2, dtype=np.float32) / np.float32(ROT)))
    row = lax.broadcasted_iota(jnp.int32, (8, SEQ), 0)
    freq = jnp.zeros((8, SEQ), F32)
    for j in range(8):
        freq = jnp.where(row == j, float(inv[j]), freq)
    ang = (place - start).astype(F32) * freq
    co, si = jnp.cos(ang), jnp.sin(ang)
    one, zero = jnp.ones((48, SEQ), F32), jnp.zeros((48, SEQ), F32)
    for j, parts in enumerate(([co, co, one, co, co, one], [-si, si, zero, -si, si, zero])):
        table = jnp.concatenate(parts, axis=0).T
        for i in range(4):
            S1[768:1024, 256 * i + 128 * j : 256 * i + 128 * j + 128] = table[256 * i : 256 * i + 256]
    blocks = [(qb, kb) for qb in range(4) for kb in range(max(0, qb - 2), qb + 1)]

    def mask_at(qb, kb):
        n = blocks.index((qb, kb))
        return s.GO.at[8 + n // 4, :, pl.ds(256 * (n % 4), 256)]

    for qb, kb in blocks:
        kidx = lax.broadcasted_iota(jnp.int32, (256, 256), 0) + 256 * kb
        qidx = lax.broadcasted_iota(jnp.int32, (256, 256), 1) + 256 * qb
        st = start[0:1, 256 * qb : 256 * qb + 256]
        mask_at(qb, kb)[...] = jnp.where((kidx >= st) & (kidx <= qidx), 0.0, -1e9).astype(BF)
    for cp in hc:
        cp.wait()
    layer_norm(staged_rows(s), s.gain[...], s.shift[...], nb)
    gc.wait()
    dc.wait()
    s.bsum[...] = jnp.zeros((8, D), F32)

    def d_context(i):
        at = at_multiple(i * 512, 512)
        for q in range(4):
            dcT[pl.ds(256 * q, 256), at] = dot_t(s.WB[pl.ds(256 * q, 256), :], g[at, :]).astype(BF)
        s.bsum[...] += jnp.sum(g[at, :].astype(F32).reshape(64, 8, D), axis=0)
        dn[at, :] = jnp.zeros((512, D), F32)

    loop(2, d_context)
    enter()
    E = lambda n: s.GO.at[n]
    DS = lambda n: s.GO.at[3 + n]
    kT, vT = s.GO.at[6], s.GO.at[7]
    ones = jnp.ones((16, SEQ), BF)
    lane = lax.broadcasted_iota(jnp.int32, (256, 256), 1)

    def turn(x, i, sign):
        cosines, sines = (S1[768:1024, at_multiple(256 * i + 128 * j, 128)] for j in range(2))
        low = lax.broadcasted_iota(jnp.int32, (256, 128), 1) % 64 < 8
        parts = []
        for j in range(x.shape[1] // 128):
            u = x[:, 128 * j : 128 * j + 128]
            a = jnp.where(low, pltpu.roll(u, 120, 1), pltpu.roll(u, 8, 1)) * sines
            parts.append(u * cosines + a if sign > 0 else u * cosines - a)
        return jnp.concatenate(parts, axis=1)

    def stack(x):
        zb = jnp.zeros_like(x)
        return jnp.concatenate([jnp.where((lane >= 64 * h) & (lane < 64 * h + 64), x, zb) for h in range(4)], axis=0)

    def diag(x):
        return jnp.concatenate([x[64 * h : 64 * h + 64, 256 * h : 256 * h + 256] for h in range(4)], axis=0)

    def rows4(x):
        return jnp.concatenate([jnp.broadcast_to(x[:, 256 * h : 256 * h + 256], (64, 256)) for h in range(4)], axis=0)

    def sum4(x):
        return jnp.concatenate([jnp.sum(x[64 * h : 64 * h + 64], axis=0, keepdims=True) for h in range(4)], axis=1)

    def finish(gr, st):
        @pl.when(gr >= 0)
        def _():
            rs.w_finish(ORDER_A, st, 3 * gr, 256 * gr)
            rs.w_finish(ORDER_B, st, 3 * gr + 1, 1024 + 256 * gr)
            rs.w_finish(ORDER_A, st, 3 * gr + 2, 2048 + 256 * gr)

    def group(gr):
        slot = lax.rem(gr, 2)

        @pl.when(gr < 3)
        def _():
            for cp in weights(gr + 1, 1 - slot):
                cp.start()

        for cp in weights(gr, slot):
            cp.wait()
        w = s.WA.at[slot]
        bq = jnp.concatenate([s.b_qkv[:, at_multiple(1024 * j + gr * 256, 256)] for j in range(3)], axis=1)

        def project(i):
            for h in range(2):
                at = at_multiple(i * 512 + 256 * h, 256)
                part = dot(nb[at, :], w[...]) + bq
                s.QKV[at, 0:256] = turn(part[:, 0:256], 2 * i + h, 1).astype(BF) * BF(0.125)
                s.QKV[at, 256:512] = turn(part[:, 256:512], 2 * i + h, 1).astype(BF)
                s.QKV[at, 512:768] = part[:, 512:768].astype(BF)

        loop(2, project)
        crow = at_multiple(gr * 256, 256)
        for i in range(4):
            at = pl.ds(256 * i, 256)
            kT[:, at] = s.QKV[at, 256:512].astype(F32).T.astype(BF)
            vT[:, at] = s.QKV[at, 512:768].astype(F32).T.astype(BF)
        s.PD[...] = jnp.zeros((SEQ, 512), F32)
        for qb in range(4):
            if qb < 3:
                finish(gr - 1, qb)
            qs = pl.ds(256 * qb, 256)
            kbs = list(range(max(0, qb - 2), qb + 1))
            nk = len(kbs)
            win = pl.ds(256 * kbs[0], 256 * nk)
            qst = stack(s.QKV[qs, 0:256])
            m = None
            for n, kb in enumerate(kbs):
                b = mask_at(qb, kb)[...].astype(F32)
                sc = dot_t(s.QKV[pl.ds(256 * kb, 256), 256:512], qst) + jnp.concatenate([b] * 4, axis=1)
                S1[pl.ds(256 * n, 256), :] = sc
                top = jnp.max(sc, axis=0, keepdims=True)
                m = top if m is None else jnp.maximum(m, top)
            for n in range(nk):
                E(n)[...] = jnp.exp(S1[pl.ds(256 * n, 256), :] - m).astype(BF)
            ev = s.GO[0:nk].reshape(256 * nk, D)
            cx = dot(jnp.concatenate([vT[:, win], ones[:, 0 : 256 * nk]], axis=0), ev)
            li = 1.0 / cx[256:257, :]
            lsel = rows4(li)
            cT = diag(cx) * lsel
            dcs = (dcT[crow, qs].astype(F32) * lsel).astype(BF).astype(F32)
            dcT[crow, qs] = cT.astype(BF)
            inner = sum4(cT * dcs)
            dst = stack(dcs.T.astype(BF))
            for n, kb in enumerate(kbs):
                ks = pl.ds(256 * kb, 256)
                dP = dot_t(s.QKV[ks, 512:768], dst)
                DS(n)[...] = (E(n)[...].astype(F32) * (dP - inner)).astype(BF)
                s.PD[ks, 0:256] += dot(DS(n)[...], qst)
                s.PD[ks, 256:512] += dot(E(n)[...], dst)
            dq = diag(dot(kT[:, win], s.GO[3 : 3 + nk].reshape(256 * nk, D)))
            s.DR[qs, 0:256] = turn(dq.T * 0.125, qb, -1).astype(BF)
        for i in range(4):
            at = pl.ds(256 * i, 256)
            s.DR[at, 256:512] = turn(s.PD[at, 0:256], i, -1).astype(BF)
        s.DR[:, 512:768] = s.PD[:, 256:512].astype(BF)
        for q in range(4):
            tile = t_dot(nb[:, pl.ds(256 * q, 256)], s.DR[...]).astype(BF)
            for j in range(3):
                s.GW[3 * gr + j, q // 2, q % 2] = tile[:, 256 * j : 256 * j + 256].reshape(2, 2, 64, 256)
        rs.w_copy(ORDER_A, 0, 3 * gr).start()
        rs.w_copy(ORDER_B, 0, 3 * gr + 1).start()
        rs.w_copy(ORDER_A, 0, 3 * gr + 2).start()
        for j in range(3):
            s.bcol[:, at_multiple(1024 * j + gr * 256, 256)] = jnp.sum(
                s.DR[:, 256 * j : 256 * j + 256].astype(F32).reshape(128, 8, 256), axis=0
            )

        def d_normed(i):
            for h in range(2):
                at = at_multiple(i * 512 + 256 * h, 256)
                dn[at, :] += dot_t(s.DR[at, :], w[...])

        loop(2, d_normed)

    loop(4, group)

    for q in range(4):
        tile = dot(dcT[pl.ds(256 * q, 256), :], g[...]).astype(BF)
        for j in range(4):
            s.GW[12 + j, q // 2, q % 2] = tile[:, 256 * j : 256 * j + 256].reshape(2, 2, 64, 256)
    for j in range(4):
        rs.w_copy(ORDER_B, 0, 12 + j).start()

    def context_rows(i):
        at = at_multiple(i * 128, 128)
        nb[:, at] = dcT[at, :].astype(F32).T.astype(BF)

    loop(8, context_rows)
    for i in range(4):
        at = pl.ds(256 * i, 256)
        S1[at, :] = dot(nb[at, :], s.WB[...])
    for j in range(3):
        s.VEC[j : j + 1, :] = jnp.sum(s.bcol[:, 1024 * j : 1024 * j + 1024], axis=0, keepdims=True)
    s.VEC[3:4, :] = jnp.sum(s.bsum[...], axis=0, keepdims=True)
    s.VEC[6:8, :] = jnp.zeros((2, D), F32)

    def progress(t):
        if t < 11:
            finish(3, t - 8)
            for j in range(4):
                rs.w_finish(ORDER_B, t - 8, 12 + j, 3072 + 256 * j)

    def finish_all():
        def units(gr):
            finish(gr, 3)
            rs.w_finish(ORDER_B, 3, 12 + gr, 3072 + 256 * gr)

        loop(4, units)

    def wait_sent():
        def units(gr):
            for st in range(4):
                rs.w_copy(ORDER_A, st, 3 * gr).wait_send()
                rs.w_copy(ORDER_B, st, 3 * gr + 1).wait_send()
                rs.w_copy(ORDER_A, st, 3 * gr + 2).wait_send()
                rs.w_copy(ORDER_B, st, 12 + gr).wait_send()

        loop(4, units)

    return progress, finish_all, wait_sent


def kernel(extra, *refs):
    s = Scope()
    names = INPUTS + OUTPUTS + tuple(n for n, *_ in SCRATCH) + tuple(n for n, *_ in SEMS) + ("ready",)
    for n, r in zip(names, refs, strict=True):
        setattr(s, n, r)
    rs = Reducer(s, extra)
    pr, dp = rs.pr, rs.dp
    other = (dp, 1 - pr)
    barrier = pltpu.get_barrier_semaphore()
    for b in range(4):
        pl.semaphore_signal(barrier, inc=1, device_id=(rs.partner[b], pr), device_id_type=MESH)
    pl.semaphore_signal(barrier, inc=1, device_id=other, device_id_type=MESH)
    enter = lambda: pl.semaphore_wait(barrier, 5)

    def to_other(src, dst, ss, sr):
        return pltpu.make_async_remote_copy(src_ref=src, dst_ref=dst, send_sem=ss, recv_sem=sr, device_id=other, device_id_type=MESH)

    def role(is_attention, run, bias):
        progress, finish_all, wait_sent = run(s, rs, enter)
        own_half = 0 if is_attention else 1
        mine, theirs = pl.ds(512 * own_half, 512), pl.ds(512 * (1 - own_half), 512)
        pl.semaphore_signal(s.ready, inc=1, device_id=other, device_id_type=MESH)
        hc = pltpu.make_async_copy(s.hidden, s.A.at[2], s.hsem.at[5])
        hc.start()
        branch = s.A.at[0]

        def pack(i):
            at = at_multiple(i * 128, 128)
            branch[at, :] = (s.ACC[1, at, :] + bias[...]).astype(BF)

        loop(8, pack)

        def pack_dn(i):
            at = at_multiple(i * 128, 128)
            s.WB[at, :] = s.ACC[0, at, :].astype(BF)

        loop(8, pack_dn)
        progress(8)
        pl.semaphore_wait(s.ready, 1)
        moves = [
            to_other(branch.at[theirs, pl.ds(0, 512)], s.WA.at[1, pl.ds(0, 512), pl.ds(256, 512)], s.xs.at[0], s.xr.at[0]),
            to_other(branch.at[theirs, pl.ds(512, 512)], s.WA.at[1, pl.ds(512, 512), pl.ds(256, 512)], s.xs.at[1], s.xr.at[1]),
            to_other(s.WB.at[:, pl.ds(0, 768)], s.WA.at[0], s.xs.at[2], s.xr.at[2]),
            to_other(s.WB.at[:, pl.ds(768, 256)], s.WA.at[1, :, pl.ds(0, 256)], s.xs.at[3], s.xr.at[3]),
        ]
        for cp in moves:
            cp.start()
        progress(9)
        hc.wait()
        for cp in moves:
            cp.wait_recv()
        s.lnsum[...] = jnp.zeros((2, 8, D), F32)

        def last(i):
            at = at_multiple(i * 64, 64)
            x = s.A[2, at, :].astype(F32)
            mean = jnp.mean(x, axis=1, keepdims=True)
            cen = x - mean
            inv = lax.rsqrt(jnp.mean(cen * cen, axis=1, keepdims=True) + EPS)
            x_hat = cen * inv
            a = s.WB[at, :].astype(F32)
            b = jnp.concatenate([s.WA[0, at, :], s.WA[1, at, 0:256]], axis=1).astype(F32)
            dnv = (a + b).astype(BF).astype(F32)
            e = dnv * s.gain[...]
            grad = s.A[1, at, :].astype(F32) + inv * (
                e - jnp.mean(e, axis=1, keepdims=True) - x_hat * jnp.mean(e * x_hat, axis=1, keepdims=True)
            )
            if is_attention:
                s.lnsum[0] += jnp.sum((dnv * x_hat).reshape(8, 8, D), axis=0)
                s.lnsum[1] += jnp.sum(dnv.reshape(8, 8, D), axis=0)

            @pl.when(i // 8 == own_half)
            def _():
                here = 64 * lax.rem(i, 8)
                got = jnp.concatenate([s.WA[1, at_multiple(here, 64), 256:768], s.WA[1, at_multiple(512 + here, 64), 256:768]], axis=1)
                attn, mlp = (branch[at, :], got) if is_attention else (got, branch[at, :])
                branch[at, :] = (x + attn.astype(F32) + mlp.astype(F32)).astype(BF)

            s.A[2, at, :] = grad.astype(BF)

        loop(16, last)
        outs = [
            pltpu.make_async_copy(branch.at[mine], s.o_out, s.fl.at[0]),
            pltpu.make_async_copy(s.A.at[2], s.o_ig, s.fl.at[1]),
        ]
        for cp in outs:
            cp.start()
        if is_attention:
            for j in range(2):
                s.VEC[4 + j : 5 + j, :] = jnp.sum(s.lnsum[j], axis=0, keepdims=True)
        vecs = []
        for b in range(4):
            cp = rs.to(s.VEC, s.VRECV.at[b], s.vs.at[b], s.vr.at[b], b)
            cp.start()
            progress(10 + b)
            cp.wait()
            s.VEC[...] += s.VRECV[b]
        vx = to_other(s.VEC, s.VPART, s.vs.at[4], s.vr.at[4])
        vx.start()
        finish_all()

        def split(first, size, half):
            return pl.ds(first, size) if extra > 1 else pl.ds(first + half * (size // 2), size // 2)

        def pieces(attention, half):
            wide = [s.o_qkv.at[:, pl.ds(1024 * k, 1024)] for k in range(3)] + [s.o_dense]
            if not attention:
                wide = [s.o_in.at[:, pl.ds(1024 * k, 1024)] for k in range(4)]
            parts = [(s.ACC.at[0, split(64 * k, 64, half)], to) for k, to in enumerate(wide)]
            return parts if attention else parts + [(s.ACC.at[0, split(256, 256, half)], s.o_outw)]

        sent, local = [], []
        for n, (src, dst) in enumerate(pieces(is_attention, 1 - own_half)):
            cp = to_other(src, dst, s.fs.at[n], s.fr.at[n])
            cp.start()
            sent.append(cp)
        for n, (src, dst) in enumerate(pieces(is_attention, own_half)):
            cp = pltpu.make_async_copy(src, dst, s.fl.at[2 + n])
            cp.start()
            local.append(cp)
        vx.wait()
        s.o_vec[0 if is_attention else 1] = s.VEC[...]
        s.o_vec[1 if is_attention else 0] = s.VPART[...]
        wait_sent()
        for cp in moves:
            cp.wait_send()
        for cp in outs + local:
            cp.wait()
        for cp in sent:
            cp.wait_send()
        for n, (src, dst) in enumerate(pieces(not is_attention, own_half)):
            to_other(src, dst, s.fs.at[n], s.fr.at[n]).wait_recv()

    pl.when(pr == 0)(lambda: role(True, attention_role, s.b_dense))
    pl.when(pr == 1)(lambda: role(False, feed_role, s.b_out))


def call(extra, *args):
    rows = 32 if extra == 1 else 64
    outw = 128 if extra == 1 else 256
    anywhere, vmem, smem = (pl.BlockSpec(memory_space=m) for m in (pl.ANY, pltpu.VMEM, pltpu.SMEM))
    shapes = [
        ((512, D), BF), ((SEQ, D), BF), ((rows, 3072), F32), ((rows, D), F32), ((rows, FF), F32), ((outw, D), F32), ((2, 8, D), F32),
    ]
    return pl.pallas_call(
        partial(kernel, extra),
        out_shape=[jax.ShapeDtypeStruct(*x) for x in shapes],
        in_specs=[anywhere, smem, vmem, vmem, anywhere, vmem, anywhere, vmem, anywhere, vmem, anywhere, vmem, anywhere],
        out_specs=[anywhere] * 6 + [vmem],
        scratch_shapes=[pltpu.VMEM(shape, kind) for _, shape, kind in SCRATCH]
        + [pltpu.SemaphoreType.DMA(shape) for _, shape in SEMS]
        + [pltpu.SemaphoreType.REGULAR],
        compiler_params=pltpu.CompilerParams(collective_id=0, has_side_effects=True, vmem_limit_bytes=VMEM_LIMIT),
        cost_estimate=pl.CostEstimate(flops=50 * 10**9, bytes_accessed=40 * 10**6, transcendentals=10**7),
    )(*args)


VMEM_LIMIT = 62 * 2**20


def swap(x, bit):
    return lax.ppermute(x, "dp", [(i, i ^ bit) for i in range(lax.axis_size("dp"))])


def halve(x, bit):
    half = x.shape[0] // 2
    up = (lax.axis_index("dp") // bit) % 2
    keep = lax.dynamic_slice_in_dim(x, up * half, half, 0)
    give = lax.dynamic_slice_in_dim(x, (1 - up) * half, half, 0)
    return keep + swap(give, bit)


def body(hidden, doc_lengths, ln_gain, ln_bias, qkv_weight, qkv_bias, dense_weight, dense_bias, fc_in_weight, fc_in_bias, fc_out_weight, fc_out_bias, cotangent):
    extra = lax.axis_size("dp") // INNER
    output, input_grad, qkv, dense, w_in, w_out, vec = call(
        extra, hidden, doc_lengths, ln_gain[None], ln_bias[None], qkv_weight, qkv_bias[None], dense_weight, dense_bias[None],
        fc_in_weight, fc_in_bias[None], fc_out_weight, fc_out_bias[None], cotangent,
    )
    dp, pair = lax.axis_index("dp"), lax.axis_index("pair")
    if extra > 1:
        bit = extra // 2
        while bit:
            qkv, dense, w_in, w_out = (halve(x, bit) for x in (qkv, dense, w_in, w_out))
            vec = vec + swap(vec, bit)
            bit //= 2
        qkv, dense, w_in, w_out = (
            lax.dynamic_slice_in_dim(x, pair * (x.shape[0] // 2), x.shape[0] // 2, 0) for x in (qkv, dense, w_in, w_out)
        )
    place = dp * 2 + pair
    count = lax.axis_size("dp") * 2

    def own(x):
        x = x.reshape(-1)
        size = x.shape[0] // count
        return lax.dynamic_slice_in_dim(x, place * size, size, 0)

    return (
        output, input_grad, qkv, own(vec[0, 0:3]), dense, own(vec[0, 3]), w_in, own(vec[1, 0:4]), w_out, own(vec[1, 4]),
        own(vec[0, 4]), own(vec[0, 5]),
    )


def solution(mesh):
    rows = P("dp", None)
    shard, shard1 = P(("dp", "pair"), None), P(("dp", "pair"))
    return jax.shard_map(
        body,
        mesh=mesh,
        in_specs=(rows, rows) + (P(),) * 10 + (rows,),
        out_specs=(shard, rows, shard, shard1, shard, shard1, shard, shard1, shard, shard1, shard1, shard1),
        check_vma=False,
    )
```

```python
from functools import partial

import jax
import jax.numpy as jnp
import numpy as np
from jax import lax
from jax.experimental import pallas as pl
from jax.experimental.pallas import tpu as pltpu
from jax.sharding import PartitionSpec as P

F32, BF = jnp.float32, jnp.bfloat16
MESH = pl.DeviceIdType.MESH
EPS = 1e-05
SEQ, D, FF, HEAD, ROT, DOCS = 1024, 1024, 4096, 64, 16, 8
INNER = 16
X_FIRST, Y_FIRST, Z_FIRST, X_THEN_Z = (0, 1, 2, 3), (1, 0, 2, 3), (2, 1, 0, 3), (0, 2, 1, 3)
W_ORDERS = (X_FIRST, Y_FIRST)
O_ORDERS = (Z_FIRST, X_THEN_Z)
QKV_ORDERS = (X_FIRST, Y_FIRST, Z_FIRST)
DENSE_ORDERS = (Y_FIRST, Y_FIRST, Z_FIRST, X_FIRST)
LAGS = (1, 2, 3)


def dot(a, b):
    return lax.dot_general(a, b, (((1,), (0,)), ((), ())), preferred_element_type=F32)


def dot_t(a, b):
    return lax.dot_general(a, b, (((1,), (1,)), ((), ())), preferred_element_type=F32)


def t_dot(a, b):
    return lax.dot_general(a, b, (((0,), (0,)), ((), ())), preferred_element_type=F32)


def scoped(name, f):
    def g(*a, **k):
        with jax.named_scope(name):
            return f(*a, **k)
    return g


def loop(n, body, first=0):
    def step(i, c):
        body(i)
        return c

    lax.fori_loop(first, n, step, 0)


def at_multiple(start, size, of=None):
    return pl.ds(pl.multiple_of(start, of or size), size)


def xor(a, b):
    return a + b - 2 * a * b


class Scope:
    pass


SCRATCH = (
    ("A", (3, SEQ, D), BF),
    ("ACC", (2, SEQ, D), F32),
    ("WA", (2, D, 768), BF),
    ("WB", (D, D), BF),
    ("PD", (SEQ, 512), F32),
    ("GW", (16, 2, 2, 2, 2, 64, 256), BF),
    ("RW1", (16, 2, 2, 2, 64, 256), BF),
    ("RW2", (16, 2, 2, 64, 256), BF),
    ("RW3", (16, 2, 64, 256), BF),
    ("RW4", (16, 64, 256), BF),
    ("GO", (16, 256, D), BF),
    ("RO1", (2, 8, 2, 128, 512), BF),
    ("RO2", (2, SEQ, 512), BF),
    ("RO3", (SEQ, 512), BF),
    ("RO4", (2, 2, 128, 512), BF),
    ("bcol", (8, 4096), F32),
    ("bsum", (8, D), F32),
    ("lnsum", (2, 8, D), F32),
    ("VEC", (8, D), F32),
    ("VRECV", (6, 8, D), F32),
    ("VPART", (8, D), F32),
)
SEMS = (
    ("lsem", (2, 8)),
    ("hsem", (6,)),
    ("qsem", (2, 3)),
    ("ws", (16, 4)),
    ("wr", (16, 4)),
    ("os", (2, 8, 5)),
    ("orr", (2, 8, 5)),
    ("vs", (7,)),
    ("vr", (7,)),
    ("xs", (24,)),
    ("xr", (24,)),
    ("fs", (5,)),
    ("fr", (5,)),
    ("fl", (7,)),
)
INPUTS = ("hidden", "lens", "gain", "shift", "w_qkv", "b_qkv", "w_dense", "b_dense", "w_in", "b_in", "w_out", "b_out", "cot")
OUTPUTS = ("o_out", "o_ig", "o_qkv", "o_dense", "o_in", "o_outw", "o_vec")


class Reducer:
    def __init__(self, s, extra):
        self.s, self.extra = s, extra
        dp = lax.axis_index("dp")
        inner = dp // extra
        self.dp, self.pr = dp, lax.axis_index("pair")
        self.bits = [inner % 2, (inner // 2) % 2, (inner // 4) % 2, inner // 8]
        step = [(1 - 2 * self.bits[b]) * (extra << b) for b in range(4)]
        self.partner = [dp + step[b] for b in range(4)]
        self.lines = ((self.partner[2], self.partner[3], dp + step[2] + step[3]), (self.partner[0], self.partner[1], dp + step[0] + step[1]))

    def to(self, src, dst, ss, rs, b):
        return pltpu.make_async_remote_copy(
            src_ref=src, dst_ref=dst, send_sem=ss, recv_sem=rs, device_id=(self.partner[b], self.pr), device_id_type=MESH
        )

    def w_half(self, order, st, u, bit):
        s = self.s
        left = [b for b in (3, 2, 1, 0) if b not in order[:st]]
        ref = (s.GW, s.RW1, s.RW2, s.RW3)[st]
        return ref.at[(u,) + (slice(None),) * left.index(order[st]) + (bit,)]

    def w_copy(self, order, st, u):
        s, b = self.s, order[st]
        dst = (s.RW1, s.RW2, s.RW3, s.RW4)[st].at[u]
        return self.to(self.w_half(order, st, u, 1 - self.bits[b]), dst, s.ws.at[u, st], s.wr.at[u, st], b)

    def w_finish(self, order, st, u, cols):
        s, b = self.s, order[st]
        self.w_copy(order, st, u).wait_recv()
        kept = self.w_half(order, st, u, self.bits[b])
        got = (s.RW1, s.RW2, s.RW3, s.RW4)[st].at[u]
        if st < 3:
            lead = got.shape[0]
            for i in range(lead):
                got[i] = (got[i].astype(F32) + kept[i].astype(F32)).astype(BF)
            self.w_copy(order, st + 1, u).start()
        else:
            total = got[...].astype(F32) + kept[...].astype(F32)
            for i, at in enumerate(cols):
                s.ACC[0, at_multiple(64 * (at // 1024), 64), at_multiple(lax.rem(at, 1024), 128)] = total[:, 128 * i : 128 * i + 128]

    def chunk_of(self, c):
        return c % 2, (c // 2) % 2, c // 4

    def shard(self, c, x, y):
        a, b, _ = self.chunk_of(c)
        return x + 2 * y + 4 * xor(a, xor(x, y)) + 8 * xor(b, x)

    def ro2(self, n, c):
        return self.s.RO2.at[n, at_multiple(128 * c, 128)]

    def ro3(self, n, c):
        return self.s.RO3.at[at_multiple(512 * n + 128 * (c // 2), 128)]

    def o_shard(self, n, c, first, second):
        a, _, _ = self.chunk_of(c)
        p, q, r, _ = O_ORDERS[n]
        bit = {p: first, q: second, r: xor(a, xor(first, second))}
        return self.shard(c, bit[0], bit[1])

    def o_copies(self, n, st, c):
        s, own = self.s, self.bits
        a, b, h = self.chunk_of(c)
        p, q, r, _ = O_ORDERS[n]
        here = xor(a, xor(own[p], own[q])) == own[r]
        mine = here & (xor(b, own[0]) == own[3])

        def copy(src, dst, k, bit):
            return self.to(src, dst, s.os.at[n, c, k], s.orr.at[n, c, k], bit)

        if st == 0:
            copies = []
            for k in range(2):
                src = s.GO.at[self.o_shard(n, c, 1 - own[p], k), at_multiple(128 * h, 128), pl.ds(512 * n, 512)]
                copies.append(copy(src, s.RO1.at[n, c, k], k, p))
            return True, True, copies
        if st == 1:
            return True, True, [copy(s.RO1.at[n, c, 1 - own[q]], self.ro2(n, c), 2, q)]
        if st == 2:
            return jnp.logical_not(here), here, [copy(self.ro2(n, c), self.ro3(n, c), 3, r)]
        return here & jnp.logical_not(mine), mine, [copy(self.ro3(n, c), s.RO4.at[n, h], 4, 3)]

    def o_start(self, n, st, c):
        sends, _, copies = self.o_copies(n, st, c)

        @pl.when(sends)
        def _():
            for cp in copies:
                cp.start()

    def o_wait_sent(self, n, st, c):
        sends, _, copies = self.o_copies(n, st, c)

        @pl.when(sends)
        def _():
            for cp in copies:
                cp.wait_send()

    def o_finish(self, n, st, c):
        s, own = self.s, self.bits
        _, _, h = self.chunk_of(c)
        p, q, _, _ = O_ORDERS[n]
        lanes = pl.ds(512 * n, 512)
        _, takes, copies = self.o_copies(n, st, c)

        @pl.when(takes)
        def _():
            for cp in copies:
                cp.wait_recv()
            if st == 0:
                for k in range(2):
                    kept = s.GO[self.o_shard(n, c, own[p], k), at_multiple(128 * h, 128), lanes]
                    s.RO1[n, c, k] = (s.RO1[n, c, k].astype(F32) + kept.astype(F32)).astype(BF)
            elif st == 1:
                got = self.ro2(n, c)
                got[...] = (got[...].astype(F32) + s.RO1[n, c, own[q]].astype(F32)).astype(BF)
            elif st == 2:
                got = self.ro3(n, c)
                got[...] = (got[...].astype(F32) + self.ro2(n, c)[...].astype(F32)).astype(BF)
            else:
                s.ACC[0, at_multiple(256 + 128 * h, 128), lanes] = s.RO4[n, h].astype(F32) + self.ro3(n, c)[...].astype(F32)

        if st < 3:
            self.o_start(n, st + 1, c)


def layer_norm(load_rows, gain, shift, nb):
    def tile(i):
        x = load_rows(i).astype(F32)
        mean = jnp.mean(x, axis=1, keepdims=True)
        cen = x - mean
        inv = lax.rsqrt(jnp.mean(cen * cen, axis=1, keepdims=True) + EPS)
        nb[at_multiple(i * 128, 128), :] = (cen * inv * gain + shift).astype(BF)

    loop(8, tile)


A1, A2, A3, A4, A5 = 0.254829592, -0.284496736, 1.421413741, -1.453152027, 1.061405429


def gelu_both(x):
    e = jnp.exp(-0.5 * (x * x))
    t = 1.0 / (1.0 + (0.3275911 * 0.7071067811865476) * jnp.abs(x))
    poly = ((((0.5 * A5) * t + (0.5 * A4)) * t + (0.5 * A3)) * t + (0.5 * A2)) * t + (0.5 * A1)
    q = poly * t * e
    cdf = jnp.where(x >= 0, 1.0 - q, q)
    return cdf, x * (e * 0.3989422804014327)


def load_inputs(s):
    hc = [pltpu.make_async_copy(s.hidden.at[pl.ds(256 * j, 256)], s.GO.at[12 + j], s.hsem.at[j]) for j in range(4)]
    gc = pltpu.make_async_copy(s.cot, s.A.at[1], s.hsem.at[4])
    for cp in hc:
        cp.start()
    gc.start()
    return hc, gc


def staged_rows(s):
    return lambda i: s.GO[12 + i // 2, at_multiple(128 * lax.rem(i, 2), 128), :]


def feed_role(s, rs, enter):
    nb, g = s.A.at[0], s.A.at[1]
    dn, out = s.ACC.at[0], s.ACC.at[1]
    act, dpre = s.A.at[2, :, pl.ds(0, 512)], s.A.at[2, :, pl.ds(512, 512)]

    def units_at(c):
        return [256 * rs.shard(c, p % 2, p // 2) + 128 * (c // 4) for p in range(4)]

    def weights(c, slot):
        copies = []
        for p, at in enumerate(units_at(c)):
            cols, k = at_multiple(at, 128), 4 * slot + p
            copies.append(pltpu.make_async_copy(s.w_in.at[:, cols], s.WA.at[slot, :, pl.ds(128 * p, 128)], s.lsem.at[0, k]))
            copies.append(pltpu.make_async_copy(s.w_out.at[cols, :], s.WB.at[at_multiple(512 * slot + 128 * p, 128)], s.lsem.at[1, k]))
        return copies

    hc, gc = load_inputs(s)
    for cp in weights(0, 0):
        cp.start()
    for cp in hc:
        cp.wait()
    scoped('norm', layer_norm)(staged_rows(s), s.gain[...], s.shift[...], nb)
    gc.wait()
    s.bsum[...] = jnp.zeros((8, D), F32)

    def prepare(i):
        at = at_multiple(i * 128, 128)
        s.bsum[...] += jnp.sum(g[at, :].astype(F32).reshape(16, 8, D), axis=0)
        dn[at, :] = jnp.zeros((128, D), F32)
        out[at, :] = jnp.zeros((128, D), F32)

    scoped('prepare', loop)(8, prepare)
    enter()

    def progress(t):
        for st in (2, 1, 0):
            c = t - LAGS[st]

            @pl.when((c >= 0) & (c < 8))
            def _(st=st, c=c):
                rs.w_finish(W_ORDERS[0], st, 2 * c, None)
                rs.w_finish(W_ORDERS[1], st, 2 * c + 1, None)
                rs.o_finish(0, st, c)
                rs.o_finish(1, st, c)

    def chunk(c):
        slot = lax.rem(c, 2)

        @pl.when(c < 7)
        def _():
            for cp in weights(c + 1, 1 - slot):
                cp.start()

        for cp in weights(c, slot):
            cp.wait()
        win, wout = s.WA.at[slot, :, pl.ds(0, 512)], s.WB.at[at_multiple(512 * slot, 512)]
        places = units_at(c)
        bias = jnp.concatenate([s.b_in[:, at_multiple(at, 128)] for at in places], axis=1)
        bacc = jnp.zeros((8, 512), F32)
        for rt in range(2):
            rows = pl.ds(512 * rt, 512)
            s.PD[0:512, :] = dot(nb[rows, :], win[...]) + bias
            s.PD[512:1024, :] = dot_t(g[rows, :], wout[...])
            for q in range(4):
                r, r2, ro = pl.ds(128 * q, 128), pl.ds(512 + 128 * q, 128), pl.ds(512 * rt + 128 * q, 128)
                pre = s.PD[r, :]
                cdf, xphi = gelu_both(pre)
                act[ro, :] = (pre * cdf).astype(BF)
                dp = (s.PD[r2, :] * (cdf + xphi)).astype(BF)
                dpre[ro, :] = dp
                bacc = bacc + jnp.sum(dp.astype(F32).reshape(16, 8, 512), axis=0)
        for p, at in enumerate(places):
            s.bcol[:, at_multiple(at, 128)] = bacc[:, 128 * p : 128 * p + 128]
        for i in range(2):
            tile = t_dot(act[:, 256 * i : 256 * i + 256], g[...]).astype(BF)
            for p in range(2 * i, 2 * i + 2):
                s.GO[rs.shard(c, p % 2, p // 2), at_multiple(128 * (c // 4), 128), :] = tile[128 * (p % 2) : 128 * (p % 2) + 128]
        rs.o_start(0, 0, c)
        rs.o_start(1, 0, c)
        for q in range(4):
            tile = t_dot(nb[:, pl.ds(256 * q, 256)], dpre[...]).astype(BF)
            for i in range(2):
                s.GW[2 * c + i, q // 2, q % 2] = tile[:, 256 * i : 256 * i + 256].reshape(2, 2, 64, 256)
        rs.w_copy(W_ORDERS[0], 0, 2 * c).start()
        rs.w_copy(W_ORDERS[1], 0, 2 * c + 1).start()
        for h in range(4):
            part = pl.ds(256 * h, 256)
            out[part, :] += dot(act[part, :], wout[...])
            dn[part, :] += dot_t(dpre[part, :], win[...])
        scoped('reduce', progress)(c)

    loop(8, scoped('chunk', chunk))
    for j in range(4):
        s.VEC[j : j + 1, :] = jnp.sum(s.bcol[:, 1024 * j : 1024 * j + 1024], axis=0, keepdims=True)
    s.VEC[4:5, :] = jnp.sum(s.bsum[...], axis=0, keepdims=True)
    s.VEC[5:8, :] = jnp.zeros((3, D), F32)

    def finish_all():
        def units(c):
            places = units_at(c)
            rs.w_finish(W_ORDERS[0], 3, 2 * c, places[:2])
            rs.w_finish(W_ORDERS[1], 3, 2 * c + 1, places[2:])
            rs.o_finish(0, 3, c)
            rs.o_finish(1, 3, c)

        loop(8, units)

    def wait_sent():
        def units(c):
            for st in range(4):
                rs.w_copy(W_ORDERS[0], st, 2 * c).wait_send()
                rs.w_copy(W_ORDERS[1], st, 2 * c + 1).wait_send()
                rs.o_wait_sent(0, st, c)
                rs.o_wait_sent(1, st, c)

        loop(8, units)

    return progress, finish_all, wait_sent


def attention_role(s, rs, enter):
    nb, g, dcT = s.A.at[0], s.A.at[1], s.A.at[2]
    dn, S1 = s.ACC.at[0], s.ACC.at[1]

    def weights(gr, slot):
        return [
            pltpu.make_async_copy(
                s.w_qkv.at[:, at_multiple(j * 1024 + gr * 256, 256)], s.WA.at[slot, :, pl.ds(256 * j, 256)], s.qsem.at[slot, j]
            )
            for j in range(3)
        ]

    hc, gc = load_inputs(s)
    for cp in weights(0, 0):
        cp.start()
    dc = pltpu.make_async_copy(s.w_dense, s.WB, s.lsem.at[1, 0])
    dc.start()
    place = lax.broadcasted_iota(jnp.int32, (8, SEQ), 1)
    start = jnp.zeros((8, SEQ), jnp.int32)
    end = jnp.int32(0)
    for d in range(DOCS - 1):
        end = end + s.lens[0, d]
        start = jnp.where(place >= end, end, start)
    inv = np.float32(10000.0) ** (-(np.arange(0, ROT, 2, dtype=np.float32) / np.float32(ROT)))
    row = lax.broadcasted_iota(jnp.int32, (8, SEQ), 0)
    freq = jnp.zeros((8, SEQ), F32)
    for j in range(8):
        freq = jnp.where(row == j, float(inv[j]), freq)
    ang = (place - start).astype(F32) * freq
    co, si = jnp.cos(ang), jnp.sin(ang)
    one, zero = jnp.ones((48, SEQ), F32), jnp.zeros((48, SEQ), F32)
    for j, parts in enumerate(([co, co, one, co, co, one], [-si, si, zero, -si, si, zero])):
        table = jnp.concatenate(parts, axis=0).T
        for i in range(4):
            S1[768:1024, 256 * i + 128 * j : 256 * i + 128 * j + 128] = table[256 * i : 256 * i + 256]
    blocks = [(qb, kb) for qb in range(4) for kb in range(max(0, qb - 2), qb + 1)]

    def mask_at(qb, kb):
        n = blocks.index((qb, kb))
        return s.GO.at[8 + n // 4, :, pl.ds(256 * (n % 4), 256)]

    for qb, kb in blocks:
        kidx = lax.broadcasted_iota(jnp.int32, (256, 256), 0) + 256 * kb
        qidx = lax.broadcasted_iota(jnp.int32, (256, 256), 1) + 256 * qb
        st = start[0:1, 256 * qb : 256 * qb + 256]
        mask_at(qb, kb)[...] = jnp.where((kidx >= st) & (kidx <= qidx), 0.0, -1e9).astype(BF)
    for cp in hc:
        cp.wait()
    scoped('norm', layer_norm)(staged_rows(s), s.gain[...], s.shift[...], nb)
    gc.wait()
    dc.wait()
    s.bsum[...] = jnp.zeros((8, D), F32)

    def d_context(i):
        at = at_multiple(i * 512, 512)
        for q in range(4):
            dcT[pl.ds(256 * q, 256), at] = dot_t(s.WB[pl.ds(256 * q, 256), :], g[at, :]).astype(BF)
        s.bsum[...] += jnp.sum(g[at, :].astype(F32).reshape(64, 8, D), axis=0)
        dn[at, :] = jnp.zeros((512, D), F32)

    scoped('dctx', loop)(2, d_context)
    enter()
    E = lambda qb, n: s.GO.at[n + 3 * (qb % 2)]
    DS = lambda n: s.GO.at[11 + n]
    kT, vT = s.GO.at[6], s.GO.at[7]
    query, key, value, d_query = (s.RO2.at[n, :, pl.ds(256 * k, 256)] for n in range(2) for k in range(2))
    ones = jnp.ones((16, SEQ), BF)
    lane = lax.broadcasted_iota(jnp.int32, (256, 256), 1)

    def turn(x, i, sign):
        cosines, sines = (S1[768:1024, at_multiple(256 * i + 128 * j, 128)] for j in range(2))
        low = lax.broadcasted_iota(jnp.int32, (256, 128), 1) % 64 < 8
        parts = []
        for j in range(x.shape[1] // 128):
            u = x[:, 128 * j : 128 * j + 128]
            a = jnp.where(low, pltpu.roll(u, 120, 1), pltpu.roll(u, 8, 1)) * sines
            parts.append(u * cosines + a if sign > 0 else u * cosines - a)
        return jnp.concatenate(parts, axis=1)

    def stack(x):
        zb = jnp.zeros_like(x)
        return jnp.concatenate([jnp.where((lane >= 64 * h) & (lane < 64 * h + 64), x, zb) for h in range(4)], axis=0)

    def diag(x):
        return jnp.concatenate([x[64 * h : 64 * h + 64, 256 * h : 256 * h + 256] for h in range(4)], axis=0)

    def rows4(x):
        return jnp.concatenate([jnp.broadcast_to(x[:, 256 * h : 256 * h + 256], (64, 256)) for h in range(4)], axis=0)

    def sum4(x):
        return jnp.concatenate([jnp.sum(x[64 * h : 64 * h + 64], axis=0, keepdims=True) for h in range(4)], axis=1)

    def finish(gr, st):
        @pl.when(gr >= 0)
        def _():
            for j, order in enumerate(QKV_ORDERS):
                at = 1024 * j + 256 * gr
                rs.w_finish(order, st, 3 * gr + j, (at, at + 128))

    def group(gr):
        slot = lax.rem(gr, 2)

        @pl.when(gr < 3)
        def _():
            for cp in weights(gr + 1, 1 - slot):
                cp.start()

        for cp in weights(gr, slot):
            cp.wait()
        w = s.WA.at[slot]
        bq = jnp.concatenate([s.b_qkv[:, at_multiple(1024 * j + gr * 256, 256)] for j in range(3)], axis=1)

        with jax.named_scope("project"):
            for i in range(4):
                at = pl.ds(256 * i, 256)
                raw = dot(nb[at, :], w[...]) + bq
                query[at, :] = turn(raw[:, 0:256], i, 1).astype(BF) * BF(0.125)
                turned = turn(raw[:, 256:512], i, 1)
                key[at, :] = turned.astype(BF)
                kT[:, at] = turned.T.astype(BF)
                value[at, :] = raw[:, 512:768].astype(BF)
                vT[:, at] = raw[:, 512:768].T.astype(BF)
        crow = at_multiple(gr * 256, 256)
        s.PD[...] = jnp.zeros((SEQ, 512), F32)

        def keys_of(qb):
            return list(range(max(0, qb - 2), qb + 1))

        def score(qb, n, kb, q4):
            b = mask_at(qb, kb)[...].astype(F32)
            sc = dot_t(key[pl.ds(256 * kb, 256), :], q4) + jnp.concatenate([b] * 4, axis=1)
            S1[pl.ds(256 * n, 256), :] = sc
            return jnp.max(sc, axis=0, keepdims=True)

        def weigh(qb, n, m):
            E(qb, n)[...] = jnp.exp(S1[pl.ds(256 * n, 256), :] - m).astype(BF)

        def context(qb):
            kbs = keys_of(qb)
            nk = len(kbs)
            win, qs = pl.ds(256 * kbs[0], 256 * nk), pl.ds(256 * qb, 256)
            ev = s.GO[3 * (qb % 2) : 3 * (qb % 2) + nk].reshape(256 * nk, D)
            cx = dot(jnp.concatenate([vT[:, win], ones[:, 0 : 256 * nk]], axis=0), ev)
            li = 1.0 / cx[256:257, :]
            lsel = rows4(li)
            cT = diag(cx) * lsel
            dcs = (dcT[crow, qs].astype(F32) * lsel).astype(BF).astype(F32)
            dcT[crow, qs] = cT.astype(BF)
            return sum4(cT * dcs), stack(dcs.T.astype(BF))

        def back(qb, n, kb, q4, inner, dst):
            ks = pl.ds(256 * kb, 256)
            dP = dot_t(value[ks, :], dst)
            DS(n)[...] = (E(qb, n)[...].astype(F32) * (dP - inner)).astype(BF)
            s.PD[ks, 256:512] += dot(E(qb, n)[...], dst)
            s.PD[ks, 0:256] += dot(DS(n)[...], q4)

        def back_queries(qb):
            kbs = keys_of(qb)
            nk = len(kbs)
            dq = diag(dot(kT[:, pl.ds(256 * kbs[0], 256 * nk)], s.GO[11 : 11 + nk].reshape(256 * nk, D)))
            d_query[pl.ds(256 * qb, 256), :] = turn(dq.T * 0.125, qb, -1).astype(BF)

        with jax.named_scope("heads"):
            q4 = stack(query[0:256, :])
            m = score(0, 0, 0, q4)
            weigh(0, 0, m)
            inner, dst = context(0)
            for qb in range(4):
                kbs, after = keys_of(qb), keys_of(qb + 1) if qb < 3 else []
                q4_after = stack(query[256 * qb + 256 : 256 * qb + 512, :]) if after else None
                m = None
                for n in range(max(len(kbs), len(after))):
                    if n < len(after):
                        top = score(qb + 1, n, after[n], q4_after)
                        m = top if m is None else jnp.maximum(m, top)
                    if n < len(kbs):
                        back(qb, n, kbs[n], q4, inner, dst)
                for n in range(len(after)):
                    weigh(qb + 1, n, m)
                back_queries(qb)
                if after:
                    inner, dst = context(qb + 1)
                q4 = q4_after
        scoped('reduce', finish)(gr - 2, 1)
        for i in range(4):
            at = pl.ds(256 * i, 256)
            s.RO3[at, 0:256] = turn(s.PD[at, 0:256], i, -1).astype(BF)
        s.RO3[:, 256:512] = s.PD[:, 256:512].astype(BF)
        for q in range(4):
            tile = t_dot(nb[:, pl.ds(256 * q, 256)], jnp.concatenate([d_query[...], s.RO3[...]], axis=1)).astype(BF)
            for j in range(3):
                s.GW[3 * gr + j, q // 2, q % 2] = tile[:, 256 * j : 256 * j + 256].reshape(2, 2, 64, 256)
        for j, order in enumerate(QKV_ORDERS):
            rs.w_copy(order, 0, 3 * gr + j).start()
        for j in range(3):
            s.bcol[:, at_multiple(1024 * j + gr * 256, 256)] = jnp.sum(
                (d_query[...] if j == 0 else s.RO3[:, 256 * j - 256 : 256 * j]).astype(F32).reshape(128, 8, 256), axis=0
            )

        with jax.named_scope("dnormed"):
            for i in range(4):
                at = pl.ds(256 * i, 256)
                dn[at, :] += dot_t(jnp.concatenate([d_query[at, :], s.RO3[at, :]], axis=1), w[...])
        scoped('reduce', finish)(gr - 2, 2)
        scoped('reduce', finish)(gr - 1, 0)

    loop(4, scoped('group', group))

    for q in range(4):
        tile = dot(dcT[pl.ds(256 * q, 256), :], g[...]).astype(BF)
        for j in range(4):
            s.GW[12 + j, q // 2, q % 2] = tile[:, 256 * j : 256 * j + 256].reshape(2, 2, 64, 256)
    for j in range(4):
        rs.w_copy(DENSE_ORDERS[j], 0, 12 + j).start()

    for i in range(4):
        at = pl.ds(256 * i, 256)
        S1[at, :] = t_dot(dcT[:, at], s.WB[...])
    for j in range(3):
        s.VEC[j : j + 1, :] = jnp.sum(s.bcol[:, 1024 * j : 1024 * j + 1024], axis=0, keepdims=True)
    s.VEC[3:4, :] = jnp.sum(s.bsum[...], axis=0, keepdims=True)
    s.VEC[6:8, :] = jnp.zeros((2, D), F32)

    def progress(t):
        if t == 7:
            finish(2, 1)
        if t == 9:
            finish(2, 2)
        if 8 <= t < 11:
            finish(3, t - 8)
            for j in range(4):
                rs.w_finish(DENSE_ORDERS[j], t - 8, 12 + j, None)

    def finish_all():
        def units(gr):
            finish(gr, 3)

        loop(4, units)
        for j in range(4):
            rs.w_finish(DENSE_ORDERS[j], 3, 12 + j, (3072 + 256 * j, 3200 + 256 * j))

    def wait_sent():
        def units(gr):
            for st in range(4):
                for j, order in enumerate(QKV_ORDERS):
                    rs.w_copy(order, st, 3 * gr + j).wait_send()

        loop(4, units)
        for j in range(4):
            for st in range(4):
                rs.w_copy(DENSE_ORDERS[j], st, 12 + j).wait_send()

    return progress, finish_all, wait_sent


def kernel(extra, *refs):
    s = Scope()
    names = INPUTS + OUTPUTS + tuple(n for n, *_ in SCRATCH) + tuple(n for n, *_ in SEMS) + ("ready",)
    for n, r in zip(names, refs, strict=True):
        setattr(s, n, r)
    rs = Reducer(s, extra)
    pr, dp = rs.pr, rs.dp
    other = (dp, 1 - pr)
    barrier = pltpu.get_barrier_semaphore()
    for b in range(4):
        pl.semaphore_signal(barrier, inc=1, device_id=(rs.partner[b], pr), device_id_type=MESH)
    for line in rs.lines:
        pl.semaphore_signal(barrier, inc=1, device_id=(line[2], pr), device_id_type=MESH)
    pl.semaphore_signal(barrier, inc=1, device_id=other, device_id_type=MESH)
    enter = lambda: pl.semaphore_wait(barrier, 7)

    def to_other(src, dst, ss, sr):
        return pltpu.make_async_remote_copy(src_ref=src, dst_ref=dst, send_sem=ss, recv_sem=sr, device_id=other, device_id_type=MESH)

    def role(is_attention, run, bias):
        progress, finish_all, wait_sent = run(s, rs, enter)
        own_half = 0 if is_attention else 1
        mine, theirs = pl.ds(512 * own_half, 512), pl.ds(512 * (1 - own_half), 512)
        if not is_attention:
            pl.semaphore_signal(s.ready, inc=1, device_id=other, device_id_type=MESH)
        hc = pltpu.make_async_copy(s.hidden, s.A.at[2], s.hsem.at[5])
        hc.start()
        branch = s.A.at[0]

        def pack(i):
            at = at_multiple(i * 128, 128)
            branch[at, :] = (s.ACC[1, at, :] + bias[...]).astype(BF)
            s.WB[at, :] = s.ACC[0, at, :].astype(BF)

        scoped('pack', loop)(8, pack)
        if is_attention:
            pl.semaphore_wait(s.ready, 1)
        to_feed = (s.WA.at[1, pl.ds(0, 512), pl.ds(256, 512)], s.WA.at[1, pl.ds(512, 512), pl.ds(256, 512)], s.WA.at[0], s.WA.at[1, :, pl.ds(0, 256)])
        to_attention = tuple(s.RO1.at[n // 16, n // 2 % 8, n % 2] for n in range(24))
        give_feed = (branch.at[theirs, pl.ds(0, 512)], branch.at[theirs, pl.ds(512, 512)], s.WB.at[:, pl.ds(0, 768)], s.WB.at[:, pl.ds(768, 256)])
        give_attention = tuple(s.WB.at[pl.ds(128 * (n // 2), 128), pl.ds(512 * (n % 2), 512)] for n in range(16)) + tuple(
            branch.at[pl.ds(512 * (1 - own_half) + 128 * (n // 2), 128), pl.ds(512 * (n % 2), 512)] for n in range(8)
        )
        give, land = (give_feed, to_feed) if is_attention else (give_attention, to_attention)
        moves = [to_other(src, dst, s.xs.at[n], s.xr.at[n]) for n, (src, dst) in enumerate(zip(give, land))]
        for cp in moves:
            cp.start()
        def start_vectors(hop):
            copies = [
                pltpu.make_async_remote_copy(
                    src_ref=s.VEC, dst_ref=s.VRECV.at[3 * hop + k], send_sem=s.vs.at[3 * hop + k], recv_sem=s.vr.at[3 * hop + k],
                    device_id=(to, pr), device_id_type=MESH,
                )
                for k, to in enumerate(rs.lines[hop])
            ]
            for cp in copies:
                cp.start()
            return copies

        def end_vectors(hop, copies):
            for cp in copies:
                scoped('vec', cp.wait)()
            s.VEC[...] += s.VRECV[3 * hop] + s.VRECV[3 * hop + 1] + s.VRECV[3 * hop + 2]

        if not is_attention:
            copies = start_vectors(0)
            for t in range(8, 8 + LAGS[2]):
                scoped(f'reduce{t}', progress)(t)
                if t == 9:
                    end_vectors(0, copies)
                    copies = start_vectors(1)
            end_vectors(1, copies)
        else:
            progress(7)
        hc.wait()
        give, land = (give_attention, to_attention) if is_attention else (give_feed, to_feed)
        for n, (src, dst) in enumerate(zip(give, land)):
            scoped('moves', to_other(src, dst, s.xs.at[n], s.xr.at[n]).wait_recv)()
        s.lnsum[...] = jnp.zeros((2, 8, D), F32)

        def last(i):
            at = at_multiple(i * 128, 128)
            x = s.A[2, at, :].astype(F32)
            mean = jnp.mean(x, axis=1, keepdims=True)
            cen = x - mean
            inv = lax.rsqrt(jnp.mean(cen * cen, axis=1, keepdims=True) + EPS)
            x_hat = cen * inv
            a = s.WB[at, :].astype(F32)
            if is_attention:
                b = jnp.concatenate([s.RO1[0, i, n] for n in range(2)], axis=1).astype(F32)
            else:
                b = jnp.concatenate([s.WA[0, at, :], s.WA[1, at, 0:256]], axis=1).astype(F32)
            dnv = (a + b).astype(BF).astype(F32)
            e = dnv * s.gain[...]
            grad = s.A[1, at, :].astype(F32) + inv * (
                e - jnp.mean(e, axis=1, keepdims=True) - x_hat * jnp.mean(e * x_hat, axis=1, keepdims=True)
            )
            if is_attention:
                s.lnsum[0] += jnp.sum((dnv * x_hat).reshape(16, 8, D), axis=0)
                s.lnsum[1] += jnp.sum(dnv.reshape(16, 8, D), axis=0)

            @pl.when(i // 4 == own_half)
            def _():
                if is_attention:
                    got = jnp.concatenate([s.RO1[1, lax.rem(i, 4), n] for n in range(2)], axis=1)
                else:
                    here = 128 * lax.rem(i, 4)
                    got = jnp.concatenate([s.WA[1, at_multiple(here, 128), 256:768], s.WA[1, at_multiple(512 + here, 128), 256:768]], axis=1)
                attn, mlp = (branch[at, :], got) if is_attention else (got, branch[at, :])
                branch[at, :] = (x + attn.astype(F32) + mlp.astype(F32)).astype(BF)

            s.A[2, at, :] = grad.astype(BF)

        scoped('last', loop)(8, last)
        outs = [
            pltpu.make_async_copy(branch.at[mine], s.o_out, s.fl.at[0]),
            pltpu.make_async_copy(s.A.at[2], s.o_ig, s.fl.at[1]),
        ]
        for cp in outs:
            cp.start()
        if is_attention:
            for j in range(2):
                s.VEC[4 + j : 5 + j, :] = jnp.sum(s.lnsum[j], axis=0, keepdims=True)
        if is_attention:
            for hop in range(2):
                copies = start_vectors(hop)
                scoped(f'reduce{8 + hop}', progress)(8 + hop)
                end_vectors(hop, copies)
        vx = to_other(s.VEC, s.VPART, s.vs.at[6], s.vr.at[6])
        vx.start()
        if is_attention:
            scoped('reduce10', progress)(10)
        scoped('finish', finish_all)()

        def split(first, size, half):
            return pl.ds(first, size) if extra > 1 else pl.ds(first + half * (size // 2), size // 2)

        def pieces(attention, half):
            wide = [s.o_qkv.at[:, pl.ds(1024 * k, 1024)] for k in range(3)] + [s.o_dense]
            if not attention:
                wide = [s.o_in.at[:, pl.ds(1024 * k, 1024)] for k in range(4)]
            parts = [(s.ACC.at[0, split(64 * k, 64, half)], to) for k, to in enumerate(wide)]
            return parts if attention else parts + [(s.ACC.at[0, split(256, 256, half)], s.o_outw)]

        sent, local = [], []
        for n, (src, dst) in enumerate(pieces(is_attention, 1 - own_half)):
            cp = to_other(src, dst, s.fs.at[n], s.fr.at[n])
            cp.start()
            sent.append(cp)
        for n, (src, dst) in enumerate(pieces(is_attention, own_half)):
            cp = pltpu.make_async_copy(src, dst, s.fl.at[2 + n])
            cp.start()
            local.append(cp)
        vx.wait()
        s.o_vec[0 if is_attention else 1] = s.VEC[...]
        s.o_vec[1 if is_attention else 0] = s.VPART[...]
        scoped('sent', wait_sent)()
        for cp in moves:
            cp.wait_send()
        for cp in outs + local:
            cp.wait()
        for cp in sent:
            cp.wait_send()
        for n, (src, dst) in enumerate(pieces(not is_attention, own_half)):
            to_other(src, dst, s.fs.at[n], s.fr.at[n]).wait_recv()

    pl.when(pr == 0)(lambda: role(True, attention_role, s.b_dense))
    pl.when(pr == 1)(lambda: role(False, feed_role, s.b_out))


def call(extra, *args):
    rows = 32 if extra == 1 else 64
    outw = 128 if extra == 1 else 256
    anywhere, vmem, smem = (pl.BlockSpec(memory_space=m) for m in (pl.ANY, pltpu.VMEM, pltpu.SMEM))
    shapes = [
        ((512, D), BF), ((SEQ, D), BF), ((rows, 3072), F32), ((rows, D), F32), ((rows, FF), F32), ((outw, D), F32), ((2, 8, D), F32),
    ]
    return pl.pallas_call(
        partial(kernel, extra),
        out_shape=[jax.ShapeDtypeStruct(*x) for x in shapes],
        in_specs=[anywhere, smem, vmem, vmem, anywhere, vmem, anywhere, vmem, anywhere, vmem, anywhere, vmem, anywhere],
        out_specs=[anywhere] * 6 + [vmem],
        scratch_shapes=[pltpu.VMEM(shape, kind) for _, shape, kind in SCRATCH]
        + [pltpu.SemaphoreType.DMA(shape) for _, shape in SEMS]
        + [pltpu.SemaphoreType.REGULAR],
        compiler_params=pltpu.CompilerParams(collective_id=0, has_side_effects=True, vmem_limit_bytes=VMEM_LIMIT),
        cost_estimate=pl.CostEstimate(flops=50 * 10**9, bytes_accessed=40 * 10**6, transcendentals=10**7),
    )(*args)


VMEM_LIMIT = 62 * 2**20


def deliver(count, *refs):
    big, vec, outs, small, held, sems = refs[:6], refs[6], refs[7:13], refs[13:19], refs[19:25], refs[25]
    take = [pltpu.make_async_copy(src, mid, sems.at[0, n]) for n, (src, mid) in enumerate(zip(big, held))]
    give = [pltpu.make_async_copy(mid, dst, sems.at[1, n]) for n, (mid, dst) in enumerate(zip(held, outs))]
    for cp in take:
        cp.start()
    place = lax.axis_index("dp") * 2 + lax.axis_index("pair")

    def tile(role, row, at):
        held = vec[role, :, at_multiple(128 * lax.rem(at, 8), 128)]
        return jnp.sum(jnp.where(sub == row + at // 8, held, 0.0), axis=0, keepdims=True)

    lane = lax.broadcasted_iota(jnp.int32, (1, 128), 1)
    sub = lax.broadcasted_iota(jnp.int32, (8, 128), 0)
    for out, (role, row, rows) in zip(small, ((0, 0, 3), (0, 3, 1), (1, 0, 4), (1, 4, 1), (0, 4, 1), (0, 5, 1))):
        size = rows * D // count
        at = place * size
        first, skip = at // 128, lax.rem(at, 128)
        turned = pltpu.roll(tile(role, row, first), lax.rem(128 - skip, 128), 1)
        if 128 % size:
            after = pltpu.roll(tile(role, row, jnp.minimum(first + 1, 8 * rows - 1)), lax.rem(128 - skip, 128), 1)
            turned = jnp.where(lane < 128 - skip, turned, after)
        out[...] = turned[:, 0:size]
    for one, other in zip(take, give):
        one.wait()
        other.start()
    for cp in give:
        cp.wait()


def swap(x, bit):
    return lax.ppermute(x, "dp", [(i, i ^ bit) for i in range(lax.axis_size("dp"))])


def halve(x, bit):
    half = x.shape[0] // 2
    up = (lax.axis_index("dp") // bit) % 2
    keep = lax.dynamic_slice_in_dim(x, up * half, half, 0)
    give = lax.dynamic_slice_in_dim(x, (1 - up) * half, half, 0)
    return keep + swap(give, bit)


def body(hidden, doc_lengths, ln_gain, ln_bias, qkv_weight, qkv_bias, dense_weight, dense_bias, fc_in_weight, fc_in_bias, fc_out_weight, fc_out_bias, cotangent):
    extra = lax.axis_size("dp") // INNER
    output, input_grad, qkv, dense, w_in, w_out, vec = call(
        extra, hidden, doc_lengths, ln_gain[None], ln_bias[None], qkv_weight, qkv_bias[None], dense_weight, dense_bias[None],
        fc_in_weight, fc_in_bias[None], fc_out_weight, fc_out_bias[None], cotangent,
    )
    dp, pair = lax.axis_index("dp"), lax.axis_index("pair")
    if extra > 1:
        bit = extra // 2
        while bit:
            qkv, dense, w_in, w_out = (halve(x, bit) for x in (qkv, dense, w_in, w_out))
            vec = vec + swap(vec, bit)
            bit //= 2
        qkv, dense, w_in, w_out = (
            lax.dynamic_slice_in_dim(x, pair * (x.shape[0] // 2), x.shape[0] // 2, 0) for x in (qkv, dense, w_in, w_out)
        )
    big = (output, input_grad, qkv, dense, w_in, w_out)
    count = lax.axis_size("dp") * 2
    sizes = (3072, D, FF, D, D, D)
    *big, qkv_b, dense_b, in_b, out_b, gain, shift = pl.pallas_call(
        partial(deliver, count),
        out_shape=[jax.ShapeDtypeStruct(x.shape, x.dtype) for x in big]
        + [jax.ShapeDtypeStruct((1, n // count), F32) for n in sizes],
        in_specs=[pl.BlockSpec(memory_space=pl.ANY)] * 6 + [pl.BlockSpec(memory_space=pltpu.VMEM)],
        out_specs=[pl.BlockSpec(memory_space=pl.ANY)] * 6 + [pl.BlockSpec(memory_space=pltpu.VMEM)] * 6,
        scratch_shapes=[pltpu.VMEM(x.shape, x.dtype) for x in big] + [pltpu.SemaphoreType.DMA((2, 6))],
    )(*big, vec)
    output, input_grad, qkv, dense, w_in, w_out = big
    qkv_b, dense_b, in_b, out_b, gain, shift = (x.reshape(-1) for x in (qkv_b, dense_b, in_b, out_b, gain, shift))
    return output, input_grad, qkv, qkv_b, dense, dense_b, w_in, in_b, w_out, out_b, gain, shift


def solution(mesh):
    rows = P("dp", None)
    shard, shard1 = P(("dp", "pair"), None), P(("dp", "pair"))
    return jax.shard_map(
        body,
        mesh=mesh,
        in_specs=(rows, rows) + (P(),) * 10 + (rows,),
        out_specs=(shard, rows, shard, shard1, shard, shard1, shard, shard1, shard, shard1, shard1, shard1),
        check_vma=False,
    )
```

```python
from functools import partial

import jax
import jax.numpy as jnp
import numpy as np
from jax import lax
from jax.experimental import pallas as pl
from jax.experimental.pallas import tpu as pltpu
from jax.sharding import PartitionSpec as P

F32, BF = jnp.float32, jnp.bfloat16
MESH = pl.DeviceIdType.MESH
EPS = 1e-05
SEQ, D, FF, HEAD, ROT, DOCS = 1024, 1024, 4096, 64, 16, 8
INNER = 16
W_ORDERS = ((1, 0, 2, 3), (0, 1, 2, 3))
O_ORDERS = ((1, 2, 0, 3), (2, 0, 1, 3))
QKV_ORDERS = ((2, 1, 0, 3), (0, 1, 2, 3), (0, 2, 1, 3))
LAGS = (1, 2, 3)


def dot(a, b):
    return lax.dot_general(a, b, (((1,), (0,)), ((), ())), preferred_element_type=F32)


def dot_t(a, b):
    return lax.dot_general(a, b, (((1,), (1,)), ((), ())), preferred_element_type=F32)


def t_dot(a, b):
    return lax.dot_general(a, b, (((0,), (0,)), ((), ())), preferred_element_type=F32)


def scoped(name, f):
    def g(*a, **k):
        with jax.named_scope(name):
            return f(*a, **k)
    return g


def loop(n, body, first=0):
    def step(i, c):
        body(i)
        return c

    lax.fori_loop(first, n, step, 0)


def at_multiple(start, size, of=None):
    return pl.ds(pl.multiple_of(start, of or size), size)


def xor(a, b):
    return a + b - 2 * a * b


class Scope:
    pass


SCRATCH = (
    ("A", (3, SEQ, D), BF),
    ("ACC", (2, SEQ, D), F32),
    ("WA", (2, D, 768), BF),
    ("WB", (D, D), BF),
    ("PD", (SEQ, 512), F32),
    ("GW", (16, 2, 2, 2, 2, 64, 256), BF),
    ("RW1", (16, 2, 2, 2, 64, 256), BF),
    ("RW2", (16, 2, 2, 64, 256), BF),
    ("RW3", (16, 2, 64, 256), BF),
    ("RW4", (16, 64, 256), BF),
    ("GO", (16, 256, D), BF),
    ("RO1", (2, 8, 2, 128, 512), BF),
    ("RO2", (2, SEQ, 512), BF),
    ("RO3", (SEQ, 512), BF),
    ("RO4", (2, 2, 128, 512), BF),
    ("gain", (1, D), F32),
    ("shift", (1, D), F32),
    ("b_first", (1, 4096), F32),
    ("b_last", (1, D), F32),
    ("bcol", (8, 4096), F32),
    ("bsum", (8, D), F32),
    ("lnsum", (2, 8, D), F32),
    ("VEC", (8, D), F32),
    ("VRECV", (6, 8, D), F32),
    ("VPART", (8, D), F32),
)
SEMS = (
    ("lsem", (2, 2)),
    ("hsem", (6,)),
    ("qsem", (2,)),
    ("ws", (4,)),
    ("wr", (8, 4)),
    ("os", (2, 4)),
    ("orr", (8, 2)),
    ("orr2", (2, 4)),
    ("orr3", (2, 2)),
    ("ds", (4,)),
    ("dr", (4, 4)),
    ("vs", (7,)),
    ("vr", (7,)),
    ("xs", (1,)),
    ("xr", (1,)),
    ("fs", (5,)),
    ("fr", (5,)),
    ("fl", (9,)),
    ("bsem", (4,)),
)
INPUTS = ("hidden", "lens", "h_gain", "h_shift", "w_qkv", "hb_qkv", "w_dense", "hb_dense", "w_in", "hb_in", "w_out", "hb_out", "cot")
OUTPUTS = ("o_out", "o_ig", "o_qkv", "o_dense", "o_in", "o_outw", "o_vec")


class Reducer:
    def __init__(self, s, extra):
        self.s, self.extra = s, extra
        dp = lax.axis_index("dp")
        inner = dp // extra
        self.dp, self.pr = dp, lax.axis_index("pair")
        self.bits = [inner % 2, (inner // 2) % 2, (inner // 4) % 2, inner // 8]
        step = [(1 - 2 * self.bits[b]) * (extra << b) for b in range(4)]
        self.partner = [dp + step[b] for b in range(4)]
        self.lines = ((self.partner[2], self.partner[3], dp + step[2] + step[3]), (self.partner[0], self.partner[1], dp + step[0] + step[1]))

    def to(self, src, dst, ss, rs, b):
        return pltpu.make_async_remote_copy(
            src_ref=src, dst_ref=dst, send_sem=ss, recv_sem=rs, device_id=(self.partner[b], self.pr), device_id_type=MESH
        )

    def wait_bytes(self, ref, sem, sent):
        cp = self.to(ref, ref, sem, sem, 0)
        cp.wait_send() if sent else cp.wait_recv()

    def w_half(self, order, st, u, bit):
        s = self.s
        left = [b for b in (3, 2, 1, 0) if b not in order[:st]]
        ref = (s.GW, s.RW1, s.RW2, s.RW3)[st]
        return ref.at[(u,) + (slice(None),) * left.index(order[st]) + (bit,)]

    def w_copy(self, order, st, u, k):
        s, b = self.s, order[st]
        dst = (s.RW1, s.RW2, s.RW3, s.RW4)[st].at[u]
        return self.to(self.w_half(order, st, u, 1 - self.bits[b]), dst, s.ws.at[st], s.wr.at[k, st], b)

    def w_wait(self, st, u, n, k):
        s = self.s
        self.wait_bytes((s.RW1, s.RW2, s.RW3, s.RW4)[st].at[pl.ds(u, n)], s.wr.at[k, st], False)

    def w_wait_sent(self, n):
        s = self.s
        for st, ref in enumerate((s.RW1, s.RW2, s.RW3, s.RW4)):
            self.wait_bytes(ref.at[pl.ds(0, n)], s.ws.at[st], True)

    def w_finish(self, order, st, u, k, cols):
        s, b = self.s, order[st]
        kept = self.w_half(order, st, u, self.bits[b])
        got = (s.RW1, s.RW2, s.RW3, s.RW4)[st].at[u]
        if st < 3:
            lead = got.shape[0]
            for i in range(lead):
                got[i] = (got[i].astype(F32) + kept[i].astype(F32)).astype(BF)
            self.w_copy(order, st + 1, u, k).start()
        else:
            total = got[...].astype(F32) + kept[...].astype(F32)
            for i, at in enumerate(cols):
                s.ACC[0, at_multiple(64 * (at // 1024), 64), at_multiple(lax.rem(at, 1024), 128)] = total[:, 128 * i : 128 * i + 128]

    def d_copies(self, st, gr):
        s, (x, y, zl, zh) = self.s, self.bits
        u = 12 + gr
        low, high = zl == gr % 2, zh == gr // 2

        def copy(src, dst, bit):
            return self.to(src, dst, s.ds.at[st], s.dr.at[gr, st], bit)

        if st == 0:
            return True, True, [
                copy(s.GW.at[u, 0, :, :, 1 - x], s.RW1.at[u, 0], 0), copy(s.GW.at[u, 1, :, 1 - y], s.RW1.at[u, 1], 1)
            ]
        if st == 1:
            return True, True, [
                copy(s.RW1.at[u, 0, :, 1 - y], s.RW2.at[u, 0], 1), copy(s.RW1.at[u, 1, :, 1 - x], s.RW2.at[u, 1], 0)
            ]
        if st == 2:
            return jnp.logical_not(low), low, [copy(s.RW2.at[u], self.d3(gr), 2)]
        return low & jnp.logical_not(high), low & high, [copy(self.d3(gr).at[j], s.RW4.at[pl.ds(12 + 2 * j, 2)], 3) for j in range(2)]

    def d3(self, gr):
        return self.s.RW3.at[pl.ds(12 + 2 * (gr // 2), 2)]

    def d_start(self, st, gr):
        sends, _, copies = self.d_copies(st, gr)

        @pl.when(sends)
        def _():
            for cp in copies:
                cp.start()

    def d_wait_sent(self):
        s, (x, y, zl, zh) = self.s, self.bits
        units = pl.ds(12, 4)
        for st, ref in enumerate((s.RW1.at[units], s.RW2.at[units], s.RW3.at[units], s.RW4.at[units])):
            self.wait_bytes(ref, s.ds.at[st], True)

    def d_finish(self, st, gr):
        s, (x, y, _, _) = self.s, self.bits
        u = 12 + gr
        _, takes, copies = self.d_copies(st, gr)

        @pl.when(takes)
        def _():
            self.wait_bytes((s.RW1.at[u], s.RW2.at[u], self.d3(gr), s.RW4.at[pl.ds(12, 4)])[st], s.dr.at[gr, st], False)
            if st == 0:
                for j in range(2):
                    s.RW1[u, 0, j] = (s.RW1[u, 0, j].astype(F32) + s.GW[u, 0, j, :, x].astype(F32)).astype(BF)
                    s.RW1[u, 1, j] = (s.RW1[u, 1, j].astype(F32) + s.GW[u, 1, j, y].astype(F32)).astype(BF)
            elif st == 1:
                s.RW2[u, 0] = (s.RW2[u, 0].astype(F32) + s.RW1[u, 0, :, y].astype(F32)).astype(BF)
                s.RW2[u, 1] = (s.RW2[u, 1].astype(F32) + s.RW1[u, 1, :, x].astype(F32)).astype(BF)
            elif st == 2:
                got = self.d3(gr)
                got[...] = (got[...].astype(F32) + s.RW2[u].astype(F32)).astype(BF)
            else:
                for j in range(4):
                    total = s.RW4[12 + j].astype(F32) + self.d3(gr)[j // 2, j % 2].astype(F32)
                    s.ACC[0, 192:256, 256 * j : 256 * j + 256] = total

        if st < 3:
            self.d_start(st + 1, gr)

    def chunk_of(self, c):
        return c % 2, (c // 2) % 2, c // 4

    def shard(self, c, x, y):
        a, b, _ = self.chunk_of(c)
        return x + 2 * y + 4 * xor(a, xor(x, y)) + 8 * xor(b, x)

    def ro2(self, n, c):
        return self.s.RO2.at[n, at_multiple(128 * c, 128)]

    def ro3(self, n, c):
        return self.s.RO3.at[at_multiple(512 * n + 128 * (c // 2), 128)]

    def o_shard(self, n, c, first, second):
        a, _, _ = self.chunk_of(c)
        p, q, r, _ = O_ORDERS[n]
        bit = {p: first, q: second, r: xor(a, xor(first, second))}
        return self.shard(c, bit[0], bit[1])

    def o_copies(self, n, st, c):
        s, own = self.s, self.bits
        a, b, h = self.chunk_of(c)
        p, q, r, _ = O_ORDERS[n]
        here = xor(a, xor(own[p], own[q])) == own[r]
        mine = here & (xor(b, own[0]) == own[3])

        def copy(src, dst, bit):
            come = s.orr.at[c, st] if st < 2 else s.orr2.at[n, c // 2] if st == 2 else s.orr3.at[n, h]
            return self.to(src, dst, s.os.at[n, st], come, bit)

        if st == 0:
            copies = []
            for k in range(2):
                src = s.GO.at[self.o_shard(n, c, 1 - own[p], k), at_multiple(128 * h, 128), pl.ds(512 * n, 512)]
                copies.append(copy(src, s.RO1.at[n, c, k], p))
            return True, True, copies
        if st == 1:
            return True, True, [copy(s.RO1.at[n, c, 1 - own[q]], self.ro2(n, c), q)]
        if st == 2:
            return jnp.logical_not(here), here, [copy(self.ro2(n, c), self.ro3(n, c), r)]
        return here & jnp.logical_not(mine), mine, [copy(self.ro3(n, c), s.RO4.at[n, h], 3)]

    def o_start(self, n, st, c):
        sends, _, copies = self.o_copies(n, st, c)

        @pl.when(sends)
        def _():
            for cp in copies:
                cp.start()

    def o_wait_sent(self):
        s = self.s
        for n in range(2):
            for st, ref in enumerate((s.RO1.at[n], s.RO2.at[n], s.RO3.at[pl.ds(512 * n, 512)], s.RO4.at[n])):
                self.wait_bytes(ref, s.os.at[n, st], True)

    def o_wait(self, st, c):
        s = self.s
        self.wait_bytes(s.RO1.at[:, c] if st == 0 else s.RO2.at[:, at_multiple(128 * c, 128)], s.orr.at[c, st], False)

    def o_finish(self, n, st, c):
        s, own = self.s, self.bits
        _, _, h = self.chunk_of(c)
        p, q, _, _ = O_ORDERS[n]
        lanes = pl.ds(512 * n, 512)
        _, takes, copies = self.o_copies(n, st, c)

        @pl.when(takes)
        def _():
            if st > 1:
                copies[0].wait_recv()
            if st == 0:
                for k in range(2):
                    kept = s.GO[self.o_shard(n, c, own[p], k), at_multiple(128 * h, 128), lanes]
                    s.RO1[n, c, k] = (s.RO1[n, c, k].astype(F32) + kept.astype(F32)).astype(BF)
            elif st == 1:
                got = self.ro2(n, c)
                got[...] = (got[...].astype(F32) + s.RO1[n, c, own[q]].astype(F32)).astype(BF)
            elif st == 2:
                got = self.ro3(n, c)
                got[...] = (got[...].astype(F32) + self.ro2(n, c)[...].astype(F32)).astype(BF)
            else:
                s.ACC[0, at_multiple(256 + 128 * h, 128), lanes] = s.RO4[n, h].astype(F32) + self.ro3(n, c)[...].astype(F32)

        if st < 3:
            self.o_start(n, st + 1, c)


def layer_norm(x, gain, shift):
    x = x.astype(F32)
    mean = jnp.mean(x, axis=1, keepdims=True)
    cen = x - mean
    inv = lax.rsqrt(jnp.mean(cen * cen, axis=1, keepdims=True) + EPS)
    return (cen * inv * gain + shift).astype(BF)


A1, A2, A3, A4, A5 = 0.254829592, -0.284496736, 1.421413741, -1.453152027, 1.061405429


def gelu_both(x):
    e = jnp.exp(-0.5 * (x * x))
    t = 1.0 / (1.0 + (0.3275911 * 0.7071067811865476) * jnp.abs(x))
    poly = ((((0.5 * A5) * t + (0.5 * A4)) * t + (0.5 * A3)) * t + (0.5 * A2)) * t + (0.5 * A1)
    q = poly * t * e
    cdf = jnp.where(x >= 0, 1.0 - q, q)
    return cdf, x * (e * 0.3989422804014327)


def load_inputs(s, first, last):
    hc = [pltpu.make_async_copy(s.hidden.at[pl.ds(256 * j, 256)], s.GO.at[12 + j], s.hsem.at[j]) for j in range(4)]
    gc = pltpu.make_async_copy(s.cot, s.A.at[1], s.hsem.at[4])
    n = first.shape[1]
    vectors = ((s.h_gain, s.gain), (s.h_shift, s.shift), (first, s.b_first.at[:, pl.ds(0, n)]), (last, s.b_last))
    vc = [pltpu.make_async_copy(src, dst, s.bsem.at[j]) for j, (src, dst) in enumerate(vectors)]
    for cp in hc + vc:
        cp.start()
    return hc, vc, gc


def column_sums(s):
    def tile(i):
        s.bsum[...] += jnp.sum(s.A[1, at_multiple(i * 256, 256), :].astype(F32).reshape(32, 8, D), axis=0)

    s.bsum[...] = jnp.zeros((8, D), F32)
    loop(4, tile)
    return jnp.sum(s.bsum[...], axis=0, keepdims=True)


def staged_rows(s, i):
    return s.GO[12 + i // 2, at_multiple(128 * lax.rem(i, 2), 128), :]


def feed_role(s, rs, enter):
    nb, g = s.A.at[0], s.A.at[1]
    dn, out = s.ACC.at[0], s.ACC.at[1]
    act, dpre = s.A.at[2, :, pl.ds(0, 512)], s.A.at[2, :, pl.ds(512, 512)]

    def units_at(c):
        return [256 * rs.shard(c, p % 2, p // 2) + 128 * (c // 4) for p in range(4)]

    def weights(c, slot):
        copies = []
        for p, at in enumerate(units_at(c)):
            cols = at_multiple(at, 128)
            copies.append(pltpu.make_async_copy(s.w_in.at[:, cols], s.WA.at[slot, :, pl.ds(128 * p, 128)], s.lsem.at[0, slot]))
            copies.append(pltpu.make_async_copy(s.w_out.at[cols, :], s.WB.at[at_multiple(512 * slot + 128 * p, 128)], s.lsem.at[1, slot]))
        return copies

    def weights_here(slot):
        pltpu.make_async_copy(s.w_in.at[:, pl.ds(0, 512)], s.WA.at[slot, :, pl.ds(0, 512)], s.lsem.at[0, slot]).wait()
        pltpu.make_async_copy(s.w_out.at[pl.ds(0, 512), :], s.WB.at[at_multiple(512 * slot, 512)], s.lsem.at[1, slot]).wait()

    hc, vc, gc = load_inputs(s, s.hb_in, s.hb_out)
    for cp in vc:
        cp.wait()

    def norm(i):
        at = at_multiple(i * 128, 128)
        nb[at, :] = layer_norm(staged_rows(s, i), s.gain[...], s.shift[...])
        dn[at, :] = jnp.zeros((128, D), F32)
        out[at, :] = jnp.zeros((128, D), F32)

    with jax.named_scope("norm"):
        for j in range(4):
            hc[j].wait()
            if j == 1:
                for cp in weights(0, 0):
                    cp.start()
                gc.start()
            loop(2 * j + 2, norm, 2 * j)
    gc.wait()
    enter()

    def progress(t):
        for st in (2, 1, 0):
            c = t - LAGS[st]

            @pl.when((c >= 0) & (c < 8))
            def _(st=st, c=c):
                rs.w_wait(st, 2 * c, 2, c)
                rs.w_finish(W_ORDERS[0], st, 2 * c, c, None)
                rs.w_finish(W_ORDERS[1], st, 2 * c + 1, c, None)
                if st < 2:
                    rs.o_wait(st, c)
                rs.o_finish(0, st, c)
                rs.o_finish(1, st, c)

    def chunk(c):
        slot = lax.rem(c, 2)

        @pl.when(c < 7)
        def _():
            for cp in weights(c + 1, 1 - slot):
                cp.start()

        weights_here(slot)
        win, wout = s.WA.at[slot, :, pl.ds(0, 512)], s.WB.at[at_multiple(512 * slot, 512)]
        places = units_at(c)
        bias = jnp.concatenate([s.b_first[:, at_multiple(at, 128)] for at in places], axis=1)
        bacc = jnp.zeros((8, 512), F32)
        for rt in range(2):
            rows = pl.ds(512 * rt, 512)
            s.PD[0:512, :] = dot(nb[rows, :], win[...]) + bias
            s.PD[512:1024, :] = dot_t(g[rows, :], wout[...])
            for q in range(4):
                r, r2, ro = pl.ds(128 * q, 128), pl.ds(512 + 128 * q, 128), pl.ds(512 * rt + 128 * q, 128)
                pre = s.PD[r, :]
                cdf, xphi = gelu_both(pre)
                act[ro, :] = (pre * cdf).astype(BF)
                dp = (s.PD[r2, :] * (cdf + xphi)).astype(BF)
                dpre[ro, :] = dp
                bacc = bacc + jnp.sum(dp.astype(F32).reshape(16, 8, 512), axis=0)
        for p, at in enumerate(places):
            s.bcol[:, at_multiple(at, 128)] = bacc[:, 128 * p : 128 * p + 128]
        for i in range(2):
            tile = t_dot(act[:, 256 * i : 256 * i + 256], g[...]).astype(BF)
            for p in range(2 * i, 2 * i + 2):
                s.GO[rs.shard(c, p % 2, p // 2), at_multiple(128 * (c // 4), 128), :] = tile[128 * (p % 2) : 128 * (p % 2) + 128]
        rs.o_start(0, 0, c)
        rs.o_start(1, 0, c)
        for q in range(4):
            tile = t_dot(nb[:, pl.ds(256 * q, 256)], dpre[...]).astype(BF)
            for i in range(2):
                s.GW[2 * c + i, q // 2, q % 2] = tile[:, 256 * i : 256 * i + 256].reshape(2, 2, 64, 256)
        rs.w_copy(W_ORDERS[0], 0, 2 * c, c).start()
        rs.w_copy(W_ORDERS[1], 0, 2 * c + 1, c).start()
        for h in range(4):
            part = pl.ds(256 * h, 256)
            out[part, :] += dot(act[part, :], wout[...])
            dn[part, :] += dot_t(dpre[part, :], win[...])
        scoped('reduce', progress)(c)

    loop(8, scoped('chunk', chunk))
    for j in range(4):
        s.VEC[j : j + 1, :] = jnp.sum(s.bcol[:, 1024 * j : 1024 * j + 1024], axis=0, keepdims=True)
    s.VEC[4:5, :] = column_sums(s)
    s.VEC[5:8, :] = jnp.zeros((3, D), F32)

    def finish_all():
        def units(c):
            places = units_at(c)
            rs.w_wait(3, 2 * c, 2, c)
            rs.w_finish(W_ORDERS[0], 3, 2 * c, c, places[:2])
            rs.w_finish(W_ORDERS[1], 3, 2 * c + 1, c, places[2:])
            rs.o_finish(0, 3, c)
            rs.o_finish(1, 3, c)

        loop(8, units)

    def wait_sent():
        rs.w_wait_sent(16)
        rs.o_wait_sent()

    return progress, finish_all, wait_sent


def attention_role(s, rs, enter):
    nb, g, dcT = s.A.at[0], s.A.at[1], s.A.at[2]
    dn, S1 = s.ACC.at[0], s.ACC.at[1]

    def weights(gr, slot):
        return [
            pltpu.make_async_copy(
                s.w_qkv.at[:, at_multiple(j * 1024 + gr * 256, 256)], s.WA.at[slot, :, pl.ds(256 * j, 256)], s.qsem.at[slot]
            )
            for j in range(3)
        ]

    hc, vc, gc = load_inputs(s, s.hb_qkv, s.hb_dense)
    for cp in weights(0, 0):
        cp.start()
    dc = pltpu.make_async_copy(s.w_dense, s.WB, s.lsem.at[1, 0])
    dc.start()
    gc.start()
    place = lax.broadcasted_iota(jnp.int32, (8, SEQ), 1)
    start = jnp.zeros((8, SEQ), jnp.int32)
    end = jnp.int32(0)
    for d in range(DOCS - 1):
        end = end + s.lens[0, d]
        start = jnp.where(place >= end, end, start)
    inv = np.float32(10000.0) ** (-(np.arange(0, ROT, 2, dtype=np.float32) / np.float32(ROT)))
    row = lax.broadcasted_iota(jnp.int32, (8, SEQ), 0)
    freq = jnp.zeros((8, SEQ), F32)
    for j in range(8):
        freq = jnp.where(row == j, float(inv[j]), freq)
    ang = (place - start).astype(F32) * freq
    co, si = jnp.cos(ang), jnp.sin(ang)
    one, zero = jnp.ones((48, SEQ), F32), jnp.zeros((48, SEQ), F32)
    for j, parts in enumerate(([co, co, one, co, co, one], [-si, si, zero, -si, si, zero])):
        table = jnp.concatenate(parts, axis=0).T
        for i in range(4):
            S1[768:1024, 256 * i + 128 * j : 256 * i + 128 * j + 128] = table[256 * i : 256 * i + 256]
    blocks = [(qb, kb) for qb in range(4) for kb in range(max(0, qb - 2), qb + 1)]

    def mask_at(qb, kb):
        n = blocks.index((qb, kb))
        return s.GO.at[8 + n // 4, :, pl.ds(256 * (n % 4), 256)]

    for qb, kb in blocks:
        kidx = lax.broadcasted_iota(jnp.int32, (256, 256), 0) + 256 * kb
        qidx = lax.broadcasted_iota(jnp.int32, (256, 256), 1) + 256 * qb
        st = start[0:1, 256 * qb : 256 * qb + 256]
        mask_at(qb, kb)[...] = jnp.where((kidx >= st) & (kidx <= qidx), 0.0, -1e9).astype(BF)
    for cp in vc:
        cp.wait()

    def norm(i):
        at = at_multiple(i * 128, 128)
        nb[at, :] = layer_norm(staged_rows(s, i), s.gain[...], s.shift[...])
        dn[at, :] = jnp.zeros((128, D), F32)

    with jax.named_scope("norm"):
        for j in range(4):
            hc[j].wait()
            loop(2 * j + 2, norm, 2 * j)
    gc.wait()
    dc.wait()
    enter()
    E = lambda qb, n: s.GO.at[n + 3 * (qb % 2)]
    DS = lambda n: s.GO.at[11 + n]
    kT, vT = s.GO.at[6], s.GO.at[7]
    query, key, value, d_query = (s.RO2.at[n, :, pl.ds(256 * k, 256)] for n in range(2) for k in range(2))
    lane = lax.broadcasted_iota(jnp.int32, (256, 256), 1)

    def turn(x, i, sign):
        cosines, sines = (S1[768:1024, at_multiple(256 * i + 128 * j, 128)] for j in range(2))
        low = lax.broadcasted_iota(jnp.int32, (256, 128), 1) % 64 < 8
        parts = []
        for j in range(x.shape[1] // 128):
            u = x[:, 128 * j : 128 * j + 128]
            a = jnp.where(low, pltpu.roll(u, 120, 1), pltpu.roll(u, 8, 1)) * sines
            parts.append(u * cosines + a if sign > 0 else u * cosines - a)
        return jnp.concatenate(parts, axis=1)

    def stack(x):
        zb = jnp.zeros_like(x)
        return jnp.concatenate([jnp.where((lane >= 64 * h) & (lane < 64 * h + 64), x, zb) for h in range(4)], axis=0)

    def diag(x):
        return jnp.concatenate([x[64 * h : 64 * h + 64, 256 * h : 256 * h + 256] for h in range(4)], axis=0)

    def rows4(x):
        return jnp.concatenate([jnp.broadcast_to(x[:, 256 * h : 256 * h + 256], (64, 256)) for h in range(4)], axis=0)

    def sum4(x):
        return jnp.concatenate([jnp.sum(x[64 * h : 64 * h + 64], axis=0, keepdims=True) for h in range(4)], axis=1)

    def finish(gr, st):
        @pl.when(gr >= 0)
        def _():
            rs.w_wait(st, 3 * gr, 3, gr)
            for j, order in enumerate(QKV_ORDERS):
                at = 1024 * j + 256 * gr
                rs.w_finish(order, st, 3 * gr + j, gr, (at, at + 128))
            rs.d_finish(st, gr)

    def group(gr):
        slot = lax.rem(gr, 2)

        @pl.when(gr < 3)
        def _():
            for cp in weights(gr + 1, 1 - slot):
                cp.start()

        pltpu.make_async_copy(s.w_qkv.at[:, pl.ds(0, 768)], s.WA.at[slot], s.qsem.at[slot]).wait()
        w = s.WA.at[slot]
        bq = jnp.concatenate([s.b_first[:, at_multiple(1024 * j + gr * 256, 256)] for j in range(3)], axis=1)

        with jax.named_scope("project"):
            for i in range(4):
                at = pl.ds(256 * i, 256)
                raw = dot(nb[at, :], w[...]) + bq
                query[at, :] = turn(raw[:, 0:256], i, 1).astype(BF) * BF(0.125)
                turned = turn(raw[:, 256:512], i, 1)
                key[at, :] = turned.astype(BF)
                kT[:, at] = turned.T.astype(BF)
                value[at, :] = raw[:, 512:768].astype(BF)
                vT[:, at] = raw[:, 512:768].T.astype(BF)
        crow = at_multiple(gr * 256, 256)
        for i in range(2):
            at = pl.ds(512 * i, 512)
            dcT[crow, at] = dot_t(s.WB[crow, :], g[at, :]).astype(BF)
        s.PD[...] = jnp.zeros((SEQ, 512), F32)

        def keys_of(qb):
            return list(range(max(0, qb - 2), qb + 1))

        def score(qb, q4):
            kbs = keys_of(qb)
            m = None
            for n, kb in enumerate(kbs):
                b = mask_at(qb, kb)[...].astype(F32)
                part = dot_t(key[pl.ds(256 * kb, 256), :], q4) + jnp.concatenate([b] * 4, axis=1)
                S1[pl.ds(256 * n, 256), :] = part
                top = jnp.max(part, axis=0, keepdims=True)
                m = top if m is None else jnp.maximum(m, top)
            return m

        def weigh(qb, n, m):
            e = jnp.exp(S1[pl.ds(256 * n, 256), :] - m)
            E(qb, n)[...] = e.astype(BF)
            return jnp.sum(e, axis=0, keepdims=True)

        def context(qb, total):
            kbs = keys_of(qb)
            nk = len(kbs)
            win, qs = pl.ds(256 * kbs[0], 256 * nk), pl.ds(256 * qb, 256)
            ev = s.GO[3 * (qb % 2) : 3 * (qb % 2) + nk].reshape(256 * nk, D)
            cx = dot(vT[:, win], ev)
            li = 1.0 / total
            lsel = rows4(li)
            cT = diag(cx) * lsel
            dcs = (dcT[crow, qs].astype(F32) * lsel).astype(BF).astype(F32)
            dcT[crow, qs] = cT.astype(BF)
            return sum4(cT * dcs), stack(dcs.T.astype(BF))

        def back(qb, q4, inner, dst):
            kbs = keys_of(qb)
            nk = len(kbs)
            win = pl.ds(256 * kbs[0], 256 * nk)
            ev = s.GO[3 * (qb % 2) : 3 * (qb % 2) + nk].reshape(256 * nk, D)
            s.PD[win, 256:512] += dot(ev, dst)
            for n, kb in enumerate(kbs):
                dP = dot_t(value[pl.ds(256 * kb, 256), :], dst)
                DS(n)[...] = (E(qb, n)[...].astype(F32) * (dP - inner)).astype(BF)
            s.PD[win, 0:256] += dot(s.GO[11 : 11 + nk].reshape(256 * nk, D), q4)

        def back_queries(qb):
            kbs = keys_of(qb)
            nk = len(kbs)
            dq = diag(dot(kT[:, pl.ds(256 * kbs[0], 256 * nk)], s.GO[11 : 11 + nk].reshape(256 * nk, D)))
            d_query[pl.ds(256 * qb, 256), :] = turn(dq.T * 0.125, qb, -1).astype(BF)

        with jax.named_scope("heads"):
            q4 = stack(query[0:256, :])
            inner, dst = context(0, weigh(0, 0, score(0, q4)))
            for qb in range(4):
                q4_after = None
                if qb < 3:
                    q4_after = stack(query[256 * qb + 256 : 256 * qb + 512, :])
                    m = score(qb + 1, q4_after)
                back(qb, q4, inner, dst)
                if qb < 3:
                    total = sum(weigh(qb + 1, n, m) for n in range(len(keys_of(qb + 1))))
                back_queries(qb)
                if qb < 3:
                    inner, dst = context(qb + 1, total)
                q4 = q4_after
        scoped('reduce', finish)(gr - 2, 1)
        for i in range(4):
            at = pl.ds(256 * i, 256)
            s.RO3[at, 0:256] = turn(s.PD[at, 0:256], i, -1).astype(BF)
        s.RO3[:, 256:512] = s.PD[:, 256:512].astype(BF)
        for q in range(4):
            tile = t_dot(nb[:, pl.ds(256 * q, 256)], jnp.concatenate([d_query[...], s.RO3[...]], axis=1)).astype(BF)
            for j in range(3):
                s.GW[3 * gr + j, q // 2, q % 2] = tile[:, 256 * j : 256 * j + 256].reshape(2, 2, 64, 256)
        for j, order in enumerate(QKV_ORDERS):
            rs.w_copy(order, 0, 3 * gr + j, gr).start()
        tile = dot(dcT[crow, :], g[...]).astype(BF)
        for j in range(4):
            s.GW[12 + gr, j // 2, j % 2] = tile[:, 256 * j : 256 * j + 256].reshape(2, 2, 64, 256)
        rs.d_start(0, gr)
        for j in range(3):
            s.bcol[:, at_multiple(1024 * j + gr * 256, 256)] = jnp.sum(
                (d_query[...] if j == 0 else s.RO3[:, 256 * j - 256 : 256 * j]).astype(F32).reshape(128, 8, 256), axis=0
            )

        with jax.named_scope("dnormed"):
            for i in range(4):
                at = pl.ds(256 * i, 256)
                dn[at, :] += dot_t(jnp.concatenate([d_query[at, :], s.RO3[at, :]], axis=1), w[...])
        scoped('reduce', finish)(gr - 2, 2)
        scoped('reduce', finish)(gr - 1, 0)

    loop(4, scoped('group', group))

    for i in range(4):
        at = pl.ds(256 * i, 256)
        S1[at, :] = t_dot(dcT[:, at], s.WB[...])
    for j in range(3):
        s.VEC[j : j + 1, :] = jnp.sum(s.bcol[:, 1024 * j : 1024 * j + 1024], axis=0, keepdims=True)
    s.VEC[3:4, :] = column_sums(s)
    s.VEC[6:8, :] = jnp.zeros((2, D), F32)

    def progress(t):
        if t == 7:
            finish(2, 1)
        if t == 9:
            finish(2, 2)
        if 8 <= t < 11:
            finish(3, t - 8)

    def finish_all():
        def units(gr):
            finish(gr, 3)

        loop(4, units)

    def wait_sent():
        rs.w_wait_sent(12)
        rs.d_wait_sent()

    return progress, finish_all, wait_sent


def kernel(extra, *refs):
    s = Scope()
    names = INPUTS + OUTPUTS + tuple(n for n, *_ in SCRATCH) + tuple(n for n, *_ in SEMS) + ("ready",)
    for n, r in zip(names, refs, strict=True):
        setattr(s, n, r)
    rs = Reducer(s, extra)
    pr, dp = rs.pr, rs.dp
    other = (dp, 1 - pr)
    barrier = pltpu.get_barrier_semaphore()
    for b in range(4):
        pl.semaphore_signal(barrier, inc=1, device_id=(rs.partner[b], pr), device_id_type=MESH)
    for line in rs.lines:
        pl.semaphore_signal(barrier, inc=1, device_id=(line[2], pr), device_id_type=MESH)
    pl.semaphore_signal(barrier, inc=1, device_id=other, device_id_type=MESH)
    enter = lambda: pl.semaphore_wait(barrier, 7)

    def to_other(src, dst, ss, sr):
        return pltpu.make_async_remote_copy(src_ref=src, dst_ref=dst, send_sem=ss, recv_sem=sr, device_id=other, device_id_type=MESH)

    def role(is_attention, run):
        progress, finish_all, wait_sent = run(s, rs, enter)
        own_half = 0 if is_attention else 1
        mine, theirs = pl.ds(512 * own_half, 512), pl.ds(512 * (1 - own_half), 512)
        if not is_attention:
            pl.semaphore_signal(s.ready, inc=1, device_id=other, device_id_type=MESH)
        hc = pltpu.make_async_copy(s.hidden, s.A.at[2], s.hsem.at[5])
        hc.start()
        branch = s.A.at[0]

        def pack(i):
            at = at_multiple(i * 128, 128)
            branch[at, :] = (s.ACC[1, at, :] + s.b_last[...]).astype(BF)
            s.WB[at, :] = s.ACC[0, at, :].astype(BF)

        scoped('pack', loop)(8, pack)
        if is_attention:
            pl.semaphore_wait(s.ready, 1)
        to_feed = (s.WA.at[1, pl.ds(0, 512), pl.ds(256, 512)], s.WA.at[1, pl.ds(512, 512), pl.ds(256, 512)], s.WA.at[0], s.WA.at[1, :, pl.ds(0, 256)])
        to_attention = tuple(s.RO1.at[n // 16, n // 2 % 8, n % 2] for n in range(24))
        give_feed = (branch.at[theirs, pl.ds(0, 512)], branch.at[theirs, pl.ds(512, 512)], s.WB.at[:, pl.ds(0, 768)], s.WB.at[:, pl.ds(768, 256)])
        give_attention = tuple(s.WB.at[pl.ds(128 * (n // 2), 128), pl.ds(512 * (n % 2), 512)] for n in range(16)) + tuple(
            branch.at[pl.ds(512 * (1 - own_half) + 128 * (n // 2), 128), pl.ds(512 * (n % 2), 512)] for n in range(8)
        )
        give, land = (give_feed, to_feed) if is_attention else (give_attention, to_attention)
        moves = [to_other(src, dst, s.xs.at[0], s.xr.at[0]) for src, dst in zip(give, land)]
        all_moves = to_other(s.WA, s.WA, s.xs.at[0], s.xr.at[0])
        for cp in moves:
            cp.start()
        def start_vectors(hop):
            copies = [
                pltpu.make_async_remote_copy(
                    src_ref=s.VEC, dst_ref=s.VRECV.at[3 * hop + k], send_sem=s.vs.at[3 * hop + k], recv_sem=s.vr.at[3 * hop + k],
                    device_id=(to, pr), device_id_type=MESH,
                )
                for k, to in enumerate(rs.lines[hop])
            ]
            for cp in copies:
                cp.start()
            return copies

        def end_vectors(hop, copies):
            for cp in copies:
                scoped('vec', cp.wait)()
            s.VEC[...] += s.VRECV[3 * hop] + s.VRECV[3 * hop + 1] + s.VRECV[3 * hop + 2]

        if is_attention:
            scoped('reduce7', progress)(7)
        else:
            copies = start_vectors(0)
        scoped('reduce8', progress)(8)
        hc.wait()
        scoped('moves', all_moves.wait_recv)()
        s.lnsum[...] = jnp.zeros((2, 8, D), F32)

        def last(i):
            at = at_multiple(i * 128, 128)
            x = s.A[2, at, :].astype(F32)
            mean = jnp.mean(x, axis=1, keepdims=True)
            cen = x - mean
            inv = lax.rsqrt(jnp.mean(cen * cen, axis=1, keepdims=True) + EPS)
            x_hat = cen * inv
            a = s.WB[at, :].astype(F32)
            if is_attention:
                b = jnp.concatenate([s.RO1[0, i, n] for n in range(2)], axis=1).astype(F32)
            else:
                b = jnp.concatenate([s.WA[0, at, :], s.WA[1, at, 0:256]], axis=1).astype(F32)
            dnv = (a + b).astype(BF).astype(F32)
            e = dnv * s.gain[...]
            grad = s.A[1, at, :].astype(F32) + inv * (
                e - jnp.mean(e, axis=1, keepdims=True) - x_hat * jnp.mean(e * x_hat, axis=1, keepdims=True)
            )
            if is_attention:
                s.lnsum[0] += jnp.sum((dnv * x_hat).reshape(16, 8, D), axis=0)
                s.lnsum[1] += jnp.sum(dnv.reshape(16, 8, D), axis=0)

            @pl.when(i // 4 == own_half)
            def _():
                if is_attention:
                    got = jnp.concatenate([s.RO1[1, lax.rem(i, 4), n] for n in range(2)], axis=1)
                else:
                    here = 128 * lax.rem(i, 4)
                    got = jnp.concatenate([s.WA[1, at_multiple(here, 128), 256:768], s.WA[1, at_multiple(512 + here, 128), 256:768]], axis=1)
                attn, mlp = (branch[at, :], got) if is_attention else (got, branch[at, :])
                branch[at, :] = (x + attn.astype(F32) + mlp.astype(F32)).astype(BF)

            s.A[2, at, :] = grad.astype(BF)

        scoped('last', loop)(8, last)
        outs = [
            pltpu.make_async_copy(branch.at[mine], s.o_out, s.fl.at[0]),
            pltpu.make_async_copy(s.A.at[2], s.o_ig, s.fl.at[1]),
        ]
        for cp in outs:
            cp.start()
        if is_attention:
            for j in range(2):
                s.VEC[4 + j : 5 + j, :] = jnp.sum(s.lnsum[j], axis=0, keepdims=True)
        if is_attention:
            copies = start_vectors(0)
            scoped('reduce9', progress)(9)
            end_vectors(0, copies)
            copies = start_vectors(1)
            scoped('reduce10', progress)(10)
        else:
            end_vectors(0, copies)
            copies = start_vectors(1)
            for t in range(9, 8 + LAGS[2]):
                scoped(f'reduce{t}', progress)(t)
        scoped('finish', finish_all)()
        end_vectors(1, copies)
        vx = to_other(s.VEC, s.VPART, s.vs.at[6], s.vr.at[6])
        vx.start()

        def split(first, size, half):
            return pl.ds(first, size) if extra > 1 else pl.ds(first + half * (size // 2), size // 2)

        def pieces(attention, half):
            wide = [s.o_qkv.at[:, pl.ds(1024 * k, 1024)] for k in range(3)] + [s.o_dense]
            if not attention:
                wide = [s.o_in.at[:, pl.ds(1024 * k, 1024)] for k in range(4)]
            parts = [(s.ACC.at[0, split(64 * k, 64, half)], to) for k, to in enumerate(wide)]
            return parts if attention else parts + [(s.ACC.at[0, split(256, 256, half)], s.o_outw)]

        sent, local = [], []
        for n, (src, dst) in enumerate(pieces(is_attention, 1 - own_half)):
            cp = to_other(src, dst, s.fs.at[n], s.fr.at[n])
            cp.start()
            sent.append(cp)
        for n, (src, dst) in enumerate(pieces(is_attention, own_half)):
            cp = pltpu.make_async_copy(src, dst, s.fl.at[2 + n])
            cp.start()
            local.append(cp)
        vx.wait()
        for n, (src, k) in enumerate(((s.VEC, own_half), (s.VPART, 1 - own_half))):
            cp = pltpu.make_async_copy(src, s.o_vec.at[k], s.fl.at[7 + n])
            cp.start()
            local.append(cp)
        scoped('sent', wait_sent)()
        all_moves.wait_send()
        for cp in outs + local:
            cp.wait()
        for cp in sent:
            cp.wait_send()
        for n, (src, dst) in enumerate(pieces(not is_attention, own_half)):
            to_other(src, dst, s.fs.at[n], s.fr.at[n]).wait_recv()

    pl.when(pr == 0)(lambda: role(True, attention_role))
    pl.when(pr == 1)(lambda: role(False, feed_role))


def call(extra, *args):
    rows = 32 if extra == 1 else 64
    outw = 128 if extra == 1 else 256
    anywhere, smem = (pl.BlockSpec(memory_space=m) for m in (pl.ANY, pltpu.SMEM))
    shapes = [
        ((512, D), BF), ((SEQ, D), BF), ((rows, 3072), F32), ((rows, D), F32), ((rows, FF), F32), ((outw, D), F32), ((2, 8, D), F32),
    ]
    return pl.pallas_call(
        partial(kernel, extra),
        out_shape=[jax.ShapeDtypeStruct(*x) for x in shapes],
        in_specs=[anywhere, smem] + [anywhere] * 11,
        out_specs=[anywhere] * 7,
        scratch_shapes=[pltpu.VMEM(shape, kind) for _, shape, kind in SCRATCH]
        + [pltpu.SemaphoreType.DMA(shape) for _, shape in SEMS]
        + [pltpu.SemaphoreType.REGULAR],
        compiler_params=pltpu.CompilerParams(collective_id=0, has_side_effects=True, vmem_limit_bytes=VMEM_LIMIT),
        cost_estimate=pl.CostEstimate(flops=50 * 10**9, bytes_accessed=40 * 10**6, transcendentals=10**7),
    )(*args)


VMEM_LIMIT = 62 * 2**20


def deliver(count, *refs):
    big, vec, outs, small, held, sems = refs[:6], refs[6], refs[7:13], refs[13:19], refs[19:25], refs[25]
    take = [pltpu.make_async_copy(src, mid, sems.at[0, n]) for n, (src, mid) in enumerate(zip(big, held))]
    give = [pltpu.make_async_copy(mid, dst, sems.at[1, n]) for n, (mid, dst) in enumerate(zip(held, outs))]
    for cp in take:
        cp.start()
    place = lax.axis_index("dp") * 2 + lax.axis_index("pair")

    def tile(role, row, at):
        held = vec[role, :, at_multiple(128 * lax.rem(at, 8), 128)]
        return jnp.sum(jnp.where(sub == row + at // 8, held, 0.0), axis=0, keepdims=True)

    lane = lax.broadcasted_iota(jnp.int32, (1, 128), 1)
    sub = lax.broadcasted_iota(jnp.int32, (8, 128), 0)
    for out, (role, row, rows) in zip(small, ((0, 0, 3), (0, 3, 1), (1, 0, 4), (1, 4, 1), (0, 4, 1), (0, 5, 1))):
        size = rows * D // count
        at = place * size
        first, skip = at // 128, lax.rem(at, 128)
        turned = pltpu.roll(tile(role, row, first), lax.rem(128 - skip, 128), 1)
        if 128 % size:
            after = pltpu.roll(tile(role, row, jnp.minimum(first + 1, 8 * rows - 1)), lax.rem(128 - skip, 128), 1)
            turned = jnp.where(lane < 128 - skip, turned, after)
        out[...] = turned[:, 0:size]
    for one, other in zip(take, give):
        one.wait()
        other.start()
    for cp in give:
        cp.wait()


def swap(x, bit):
    return lax.ppermute(x, "dp", [(i, i ^ bit) for i in range(lax.axis_size("dp"))])


def halve(x, bit):
    half = x.shape[0] // 2
    up = (lax.axis_index("dp") // bit) % 2
    keep = lax.dynamic_slice_in_dim(x, up * half, half, 0)
    give = lax.dynamic_slice_in_dim(x, (1 - up) * half, half, 0)
    return keep + swap(give, bit)


def body(hidden, doc_lengths, ln_gain, ln_bias, qkv_weight, qkv_bias, dense_weight, dense_bias, fc_in_weight, fc_in_bias, fc_out_weight, fc_out_bias, cotangent):
    extra = lax.axis_size("dp") // INNER
    output, input_grad, qkv, dense, w_in, w_out, vec = call(
        extra, hidden, doc_lengths, ln_gain[None], ln_bias[None], qkv_weight, qkv_bias[None], dense_weight, dense_bias[None],
        fc_in_weight, fc_in_bias[None], fc_out_weight, fc_out_bias[None], cotangent,
    )
    dp, pair = lax.axis_index("dp"), lax.axis_index("pair")
    if extra > 1:
        bit = extra // 2
        while bit:
            qkv, dense, w_in, w_out = (halve(x, bit) for x in (qkv, dense, w_in, w_out))
            vec = vec + swap(vec, bit)
            bit //= 2
        qkv, dense, w_in, w_out = (
            lax.dynamic_slice_in_dim(x, pair * (x.shape[0] // 2), x.shape[0] // 2, 0) for x in (qkv, dense, w_in, w_out)
        )
    big = (output, input_grad, qkv, dense, w_in, w_out)
    count = lax.axis_size("dp") * 2
    sizes = (3072, D, FF, D, D, D)
    *big, qkv_b, dense_b, in_b, out_b, gain, shift = pl.pallas_call(
        partial(deliver, count),
        out_shape=[jax.ShapeDtypeStruct(x.shape, x.dtype) for x in big]
        + [jax.ShapeDtypeStruct((1, n // count), F32) for n in sizes],
        in_specs=[pl.BlockSpec(memory_space=pl.ANY)] * 6 + [pl.BlockSpec(memory_space=pltpu.VMEM)],
        out_specs=[pl.BlockSpec(memory_space=pl.ANY)] * 6 + [pl.BlockSpec(memory_space=pltpu.VMEM)] * 6,
        scratch_shapes=[pltpu.VMEM(x.shape, x.dtype) for x in big] + [pltpu.SemaphoreType.DMA((2, 6))],
    )(*big, vec)
    output, input_grad, qkv, dense, w_in, w_out = big
    qkv_b, dense_b, in_b, out_b, gain, shift = (x.reshape(-1) for x in (qkv_b, dense_b, in_b, out_b, gain, shift))
    return output, input_grad, qkv, qkv_b, dense, dense_b, w_in, in_b, w_out, out_b, gain, shift


def solution(mesh):
    rows = P("dp", None)
    shard, shard1 = P(("dp", "pair"), None), P(("dp", "pair"))
    return jax.shard_map(
        body,
        mesh=mesh,
        in_specs=(rows, rows) + (P(),) * 10 + (rows,),
        out_specs=(shard, rows, shard, shard1, shard, shard1, shard, shard1, shard, shard1, shard1, shard1),
        check_vma=False,
    )
```

```python
from functools import partial

import jax
import jax.numpy as jnp
import numpy as np
from jax import lax
from jax.experimental import pallas as pl
from jax.experimental.pallas import tpu as pltpu
from jax.sharding import PartitionSpec as P

F32, BF = jnp.float32, jnp.bfloat16
MESH = pl.DeviceIdType.MESH
EPS = 1e-05
SEQ, D, FF, HEAD, ROT, DOCS = 1024, 1024, 4096, 64, 16, 8
INNER = 16
W_ORDERS = ((1, 0, 2, 3), (0, 1, 2, 3))
O_ORDERS = ((1, 2, 0, 3), (2, 0, 1, 3))
QKV_ORDERS = ((2, 1, 0, 3), (0, 1, 2, 3), (0, 2, 1, 3))
LAGS = (1, 2, 3)


def dot(a, b):
    return lax.dot_general(a, b, (((1,), (0,)), ((), ())), preferred_element_type=F32)


def dot_t(a, b):
    return lax.dot_general(a, b, (((1,), (1,)), ((), ())), preferred_element_type=F32)


def t_dot(a, b):
    return lax.dot_general(a, b, (((0,), (0,)), ((), ())), preferred_element_type=F32)


def scoped(name, f):
    def g(*a, **k):
        with jax.named_scope(name):
            return f(*a, **k)
    return g


def loop(n, body, first=0):
    def step(i, c):
        body(i)
        return c

    lax.fori_loop(first, n, step, 0)


def at_multiple(start, size, of=None):
    return pl.ds(pl.multiple_of(start, of or size), size)


def xor(a, b):
    return a + b - 2 * a * b


class Scope:
    pass


SCRATCH = (
    ("A", (3, SEQ, D), BF),
    ("ACC", (2, SEQ, D), F32),
    ("WA", (2, D, 768), BF),
    ("WB", (D, D), BF),
    ("PD", (SEQ, 512), F32),
    ("GW", (16, 2, 2, 2, 2, 64, 256), BF),
    ("RW1", (16, 2, 2, 2, 64, 256), BF),
    ("RW2", (16, 2, 2, 64, 256), BF),
    ("RW3", (16, 2, 64, 256), BF),
    ("RW4", (16, 64, 256), BF),
    ("GO", (16, 256, D), BF),
    ("RO1", (2, 8, 2, 128, 512), BF),
    ("RO2", (2, SEQ, 512), BF),
    ("RO3", (SEQ, 512), BF),
    ("RO4", (2, 2, 128, 512), BF),
    ("gain", (1, D), F32),
    ("shift", (1, D), F32),
    ("b_first", (1, 4096), F32),
    ("b_last", (1, D), F32),
    ("bcol", (8, 4096), F32),
    ("bsum", (8, D), F32),
    ("lnsum", (2, 8, D), F32),
    ("VEC", (8, D), F32),
    ("VRECV", (6, 8, D), F32),
    ("VPART", (8, D), F32),
)
SEMS = (
    ("lsem", (2, 2)),
    ("hsem", (6,)),
    ("qsem", (2,)),
    ("ws", (4,)),
    ("wr", (8, 4)),
    ("os", (2, 4)),
    ("orr", (8, 2)),
    ("orr2", (2, 4)),
    ("orr3", (2, 2)),
    ("ds", (4,)),
    ("dr", (4, 4)),
    ("vs", (7,)),
    ("vr", (7,)),
    ("xs", (1,)),
    ("xr", (1,)),
    ("fs", (5,)),
    ("fr", (5,)),
    ("fl", (9,)),
    ("bsem", (4,)),
)
INPUTS = ("hidden", "lens", "h_gain", "h_shift", "w_qkv", "hb_qkv", "w_dense", "hb_dense", "w_in", "hb_in", "w_out", "hb_out", "cot")
OUTPUTS = ("o_out", "o_ig", "o_qkv", "o_dense", "o_in", "o_outw", "o_vec")


class Reducer:
    def __init__(self, s, extra):
        self.s, self.extra = s, extra
        dp = lax.axis_index("dp")
        inner = dp // extra
        self.dp, self.pr = dp, lax.axis_index("pair")
        self.bits = [inner % 2, (inner // 2) % 2, (inner // 4) % 2, inner // 8]
        step = [(1 - 2 * self.bits[b]) * (extra << b) for b in range(4)]
        self.partner = [dp + step[b] for b in range(4)]
        self.lines = ((self.partner[2], self.partner[3], dp + step[2] + step[3]), (self.partner[0], self.partner[1], dp + step[0] + step[1]))

    def to(self, src, dst, ss, rs, b):
        return pltpu.make_async_remote_copy(
            src_ref=src, dst_ref=dst, send_sem=ss, recv_sem=rs, device_id=(self.partner[b], self.pr), device_id_type=MESH
        )

    def wait_bytes(self, ref, sem, sent):
        cp = self.to(ref, ref, sem, sem, 0)
        cp.wait_send() if sent else cp.wait_recv()

    def w_half(self, order, st, u, bit):
        s = self.s
        left = [b for b in (3, 2, 1, 0) if b not in order[:st]]
        ref = (s.GW, s.RW1, s.RW2, s.RW3)[st]
        return ref.at[(u,) + (slice(None),) * left.index(order[st]) + (bit,)]

    def w_copy(self, order, st, u, k):
        s, b = self.s, order[st]
        dst = (s.RW1, s.RW2, s.RW3, s.RW4)[st].at[u]
        return self.to(self.w_half(order, st, u, 1 - self.bits[b]), dst, s.ws.at[st], s.wr.at[k, st], b)

    def w_wait(self, st, u, n, k):
        s = self.s
        self.wait_bytes((s.RW1, s.RW2, s.RW3, s.RW4)[st].at[pl.ds(u, n)], s.wr.at[k, st], False)

    def w_wait_sent(self, n):
        s = self.s
        for st, ref in enumerate((s.RW1, s.RW2, s.RW3, s.RW4)):
            self.wait_bytes(ref.at[pl.ds(0, n)], s.ws.at[st], True)

    def w_finish(self, order, st, u, k, cols):
        s, b = self.s, order[st]
        kept = self.w_half(order, st, u, self.bits[b])
        got = (s.RW1, s.RW2, s.RW3, s.RW4)[st].at[u]
        if st < 3:
            lead = got.shape[0]
            for i in range(lead):
                got[i] = (got[i].astype(F32) + kept[i].astype(F32)).astype(BF)
            self.w_copy(order, st + 1, u, k).start()
        else:
            total = got[...].astype(F32) + kept[...].astype(F32)
            for i, at in enumerate(cols):
                s.ACC[0, at_multiple(64 * (at // 1024), 64), at_multiple(lax.rem(at, 1024), 128)] = total[:, 128 * i : 128 * i + 128]

    def d_copies(self, st, gr):
        s, (x, y, zl, zh) = self.s, self.bits
        u = 12 + gr
        low, high = zl == gr % 2, zh == gr // 2

        def copy(src, dst, bit):
            return self.to(src, dst, s.ds.at[st], s.dr.at[gr, st], bit)

        if st == 0:
            return True, True, [
                copy(s.GW.at[u, 0, :, :, 1 - x], s.RW1.at[u, 0], 0), copy(s.GW.at[u, 1, :, 1 - y], s.RW1.at[u, 1], 1)
            ]
        if st == 1:
            return True, True, [
                copy(s.RW1.at[u, 0, :, 1 - y], s.RW2.at[u, 0], 1), copy(s.RW1.at[u, 1, :, 1 - x], s.RW2.at[u, 1], 0)
            ]
        if st == 2:
            return jnp.logical_not(low), low, [copy(s.RW2.at[u], self.d3(gr), 2)]
        return low & jnp.logical_not(high), low & high, [copy(self.d3(gr).at[j], s.RW4.at[pl.ds(12 + 2 * j, 2)], 3) for j in range(2)]

    def d3(self, gr):
        return self.s.RW3.at[pl.ds(12 + 2 * (gr // 2), 2)]

    def d_start(self, st, gr):
        sends, _, copies = self.d_copies(st, gr)

        @pl.when(sends)
        def _():
            for cp in copies:
                cp.start()

    def d_wait_sent(self):
        s, (x, y, zl, zh) = self.s, self.bits
        units = pl.ds(12, 4)
        for st, ref in enumerate((s.RW1.at[units], s.RW2.at[units], s.RW3.at[units], s.RW4.at[units])):
            self.wait_bytes(ref, s.ds.at[st], True)

    def d_finish(self, st, gr):
        s, (x, y, _, _) = self.s, self.bits
        u = 12 + gr
        _, takes, copies = self.d_copies(st, gr)

        @pl.when(takes)
        def _():
            self.wait_bytes((s.RW1.at[u], s.RW2.at[u], self.d3(gr), s.RW4.at[pl.ds(12, 4)])[st], s.dr.at[gr, st], False)
            if st == 0:
                for j in range(2):
                    s.RW1[u, 0, j] = (s.RW1[u, 0, j].astype(F32) + s.GW[u, 0, j, :, x].astype(F32)).astype(BF)
                    s.RW1[u, 1, j] = (s.RW1[u, 1, j].astype(F32) + s.GW[u, 1, j, y].astype(F32)).astype(BF)
            elif st == 1:
                s.RW2[u, 0] = (s.RW2[u, 0].astype(F32) + s.RW1[u, 0, :, y].astype(F32)).astype(BF)
                s.RW2[u, 1] = (s.RW2[u, 1].astype(F32) + s.RW1[u, 1, :, x].astype(F32)).astype(BF)
            elif st == 2:
                got = self.d3(gr)
                got[...] = (got[...].astype(F32) + s.RW2[u].astype(F32)).astype(BF)
            else:
                for j in range(4):
                    total = s.RW4[12 + j].astype(F32) + self.d3(gr)[j // 2, j % 2].astype(F32)
                    s.ACC[0, 192:256, 256 * j : 256 * j + 256] = total

        if st < 3:
            self.d_start(st + 1, gr)

    def chunk_of(self, c):
        return c % 2, (c // 2) % 2, c // 4

    def shard(self, c, x, y):
        a, b, _ = self.chunk_of(c)
        return x + 2 * y + 4 * xor(a, xor(x, y)) + 8 * xor(b, x)

    def ro2(self, n, c):
        return self.s.RO2.at[n, at_multiple(128 * c, 128)]

    def ro3(self, n, c):
        return self.s.RO3.at[at_multiple(512 * n + 128 * (c // 2), 128)]

    def o_shard(self, n, c, first, second):
        a, _, _ = self.chunk_of(c)
        p, q, r, _ = O_ORDERS[n]
        bit = {p: first, q: second, r: xor(a, xor(first, second))}
        return self.shard(c, bit[0], bit[1])

    def o_copies(self, n, st, c):
        s, own = self.s, self.bits
        a, b, h = self.chunk_of(c)
        p, q, r, _ = O_ORDERS[n]
        here = xor(a, xor(own[p], own[q])) == own[r]
        mine = here & (xor(b, own[0]) == own[3])

        def copy(src, dst, bit):
            come = s.orr.at[c, st] if st < 2 else s.orr2.at[n, c // 2] if st == 2 else s.orr3.at[n, h]
            return self.to(src, dst, s.os.at[n, st], come, bit)

        if st == 0:
            copies = []
            for k in range(2):
                src = s.GO.at[self.o_shard(n, c, 1 - own[p], k), at_multiple(128 * h, 128), pl.ds(512 * n, 512)]
                copies.append(copy(src, s.RO1.at[n, c, k], p))
            return True, True, copies
        if st == 1:
            return True, True, [copy(s.RO1.at[n, c, 1 - own[q]], self.ro2(n, c), q)]
        if st == 2:
            return jnp.logical_not(here), here, [copy(self.ro2(n, c), self.ro3(n, c), r)]
        return here & jnp.logical_not(mine), mine, [copy(self.ro3(n, c), s.RO4.at[n, h], 3)]

    def o_start(self, n, st, c):
        sends, _, copies = self.o_copies(n, st, c)

        @pl.when(sends)
        def _():
            for cp in copies:
                cp.start()

    def o_wait_sent(self):
        s = self.s
        for n in range(2):
            for st, ref in enumerate((s.RO1.at[n], s.RO2.at[n], s.RO3.at[pl.ds(512 * n, 512)], s.RO4.at[n])):
                self.wait_bytes(ref, s.os.at[n, st], True)

    def o_wait(self, st, c):
        s = self.s
        self.wait_bytes(s.RO1.at[:, c] if st == 0 else s.RO2.at[:, at_multiple(128 * c, 128)], s.orr.at[c, st], False)

    def o_finish(self, n, st, c):
        s, own = self.s, self.bits
        _, _, h = self.chunk_of(c)
        p, q, _, _ = O_ORDERS[n]
        lanes = pl.ds(512 * n, 512)
        _, takes, copies = self.o_copies(n, st, c)

        @pl.when(takes)
        def _():
            if st > 1:
                copies[0].wait_recv()
            if st == 0:
                for k in range(2):
                    kept = s.GO[self.o_shard(n, c, own[p], k), at_multiple(128 * h, 128), lanes]
                    s.RO1[n, c, k] = (s.RO1[n, c, k].astype(F32) + kept.astype(F32)).astype(BF)
            elif st == 1:
                got = self.ro2(n, c)
                got[...] = (got[...].astype(F32) + s.RO1[n, c, own[q]].astype(F32)).astype(BF)
            elif st == 2:
                got = self.ro3(n, c)
                got[...] = (got[...].astype(F32) + self.ro2(n, c)[...].astype(F32)).astype(BF)
            else:
                s.ACC[0, at_multiple(256 + 128 * h, 128), lanes] = s.RO4[n, h].astype(F32) + self.ro3(n, c)[...].astype(F32)

        if st < 3:
            self.o_start(n, st + 1, c)


def layer_norm(x, gain, shift):
    x = x.astype(F32)
    mean = jnp.mean(x, axis=1, keepdims=True)
    cen = x - mean
    inv = lax.rsqrt(jnp.mean(cen * cen, axis=1, keepdims=True) + EPS)
    return (cen * inv * gain + shift).astype(BF)


A1, A2, A3, A4, A5 = 0.254829592, -0.284496736, 1.421413741, -1.453152027, 1.061405429


def gelu_both(x):
    e = jnp.exp(-0.5 * (x * x))
    t = 1.0 / (1.0 + (0.3275911 * 0.7071067811865476) * jnp.abs(x))
    poly = ((((0.5 * A5) * t + (0.5 * A4)) * t + (0.5 * A3)) * t + (0.5 * A2)) * t + (0.5 * A1)
    q = poly * t * e
    cdf = jnp.where(x >= 0, 1.0 - q, q)
    return cdf, x * (e * 0.3989422804014327)


def load_inputs(s, first, last):
    hc = [pltpu.make_async_copy(s.hidden.at[pl.ds(256 * j, 256)], s.GO.at[12 + j], s.hsem.at[j]) for j in range(4)]
    gc = pltpu.make_async_copy(s.cot, s.A.at[1], s.hsem.at[4])
    n = first.shape[1]
    vectors = ((s.h_gain, s.gain), (s.h_shift, s.shift), (first, s.b_first.at[:, pl.ds(0, n)]), (last, s.b_last))
    vc = [pltpu.make_async_copy(src, dst, s.bsem.at[j]) for j, (src, dst) in enumerate(vectors)]
    for cp in hc + vc:
        cp.start()
    return hc, vc, gc


def column_sums(s):
    def tile(i):
        s.bsum[...] += jnp.sum(s.A[1, at_multiple(i * 256, 256), :].astype(F32).reshape(32, 8, D), axis=0)

    s.bsum[...] = jnp.zeros((8, D), F32)
    loop(4, tile)
    return jnp.sum(s.bsum[...], axis=0, keepdims=True)


def staged_rows(s, i):
    return s.GO[12 + i // 2, at_multiple(128 * lax.rem(i, 2), 128), :]


def feed_role(s, rs, enter):
    nb, g = s.A.at[0], s.A.at[1]
    dn, out = s.ACC.at[0], s.ACC.at[1]
    act, dpre = s.A.at[2, :, pl.ds(0, 512)], s.A.at[2, :, pl.ds(512, 512)]

    def units_at(c):
        return [256 * rs.shard(c, p % 2, p // 2) + 128 * (c // 4) for p in range(4)]

    def weights(c, slot):
        copies = []
        for p, at in enumerate(units_at(c)):
            cols = at_multiple(at, 128)
            copies.append(pltpu.make_async_copy(s.w_in.at[:, cols], s.WA.at[slot, :, pl.ds(128 * p, 128)], s.lsem.at[0, slot]))
            copies.append(pltpu.make_async_copy(s.w_out.at[cols, :], s.WB.at[at_multiple(512 * slot + 128 * p, 128)], s.lsem.at[1, slot]))
        return copies

    def weights_here(slot):
        pltpu.make_async_copy(s.w_in.at[:, pl.ds(0, 512)], s.WA.at[slot, :, pl.ds(0, 512)], s.lsem.at[0, slot]).wait()
        pltpu.make_async_copy(s.w_out.at[pl.ds(0, 512), :], s.WB.at[at_multiple(512 * slot, 512)], s.lsem.at[1, slot]).wait()

    hc, vc, gc = load_inputs(s, s.hb_in, s.hb_out)
    for cp in vc:
        cp.wait()

    def norm(i):
        at = at_multiple(i * 128, 128)
        nb[at, :] = layer_norm(staged_rows(s, i), s.gain[...], s.shift[...])
        dn[at, :] = jnp.zeros((128, D), F32)
        out[at, :] = jnp.zeros((128, D), F32)

    with jax.named_scope("norm"):
        for j in range(4):
            hc[j].wait()
            if j == 1:
                for cp in weights(0, 0):
                    cp.start()
                gc.start()
            loop(2 * j + 2, norm, 2 * j)
    gc.wait()
    enter()

    def progress(t):
        for st in (2, 1, 0):
            c = t - LAGS[st]

            @pl.when((c >= 0) & (c < 8))
            def _(st=st, c=c):
                rs.w_wait(st, 2 * c, 2, c)
                rs.w_finish(W_ORDERS[0], st, 2 * c, c, None)
                rs.w_finish(W_ORDERS[1], st, 2 * c + 1, c, None)
                if st < 2:
                    rs.o_wait(st, c)
                rs.o_finish(0, st, c)
                rs.o_finish(1, st, c)

    def chunk(c):
        slot = lax.rem(c, 2)

        @pl.when((c < 7) & (c != 1))
        def _():
            for cp in weights(c + 1, 1 - slot):
                cp.start()

        weights_here(slot)
        win, wout = s.WA.at[slot, :, pl.ds(0, 512)], s.WB.at[at_multiple(512 * slot, 512)]
        places = units_at(c)
        bias = jnp.concatenate([s.b_first[:, at_multiple(at, 128)] for at in places], axis=1)
        bacc = jnp.zeros((8, 512), F32)
        for rt in range(2):
            rows = pl.ds(512 * rt, 512)
            s.PD[0:512, :] = dot(nb[rows, :], win[...]) + bias
            s.PD[512:1024, :] = dot_t(g[rows, :], wout[...])
            for q in range(4):
                r, r2, ro = pl.ds(128 * q, 128), pl.ds(512 + 128 * q, 128), pl.ds(512 * rt + 128 * q, 128)
                pre = s.PD[r, :]
                cdf, xphi = gelu_both(pre)
                act[ro, :] = (pre * cdf).astype(BF)
                dp = (s.PD[r2, :] * (cdf + xphi)).astype(BF)
                dpre[ro, :] = dp
                bacc = bacc + jnp.sum(dp.astype(F32).reshape(16, 8, 512), axis=0)
        for p, at in enumerate(places):
            s.bcol[:, at_multiple(at, 128)] = bacc[:, 128 * p : 128 * p + 128]
        for i in range(2):
            tile = t_dot(act[:, 256 * i : 256 * i + 256], g[...]).astype(BF)
            for p in range(2 * i, 2 * i + 2):
                s.GO[rs.shard(c, p % 2, p // 2), at_multiple(128 * (c // 4), 128), :] = tile[128 * (p % 2) : 128 * (p % 2) + 128]
        rs.o_start(0, 0, c)
        rs.o_start(1, 0, c)
        for q in range(4):
            tile = t_dot(nb[:, pl.ds(256 * q, 256)], dpre[...]).astype(BF)
            for i in range(2):
                s.GW[2 * c + i, q // 2, q % 2] = tile[:, 256 * i : 256 * i + 256].reshape(2, 2, 64, 256)
        rs.w_copy(W_ORDERS[0], 0, 2 * c, c).start()
        rs.w_copy(W_ORDERS[1], 0, 2 * c + 1, c).start()

        @pl.when(c == 0)
        def _():
            def keep(i):
                at = at_multiple(256 * i, 256)
                for k in range(4):
                    s.GW[8 + k, i // 2, i % 2] = s.A[2, at, 256 * k : 256 * k + 256].reshape(2, 2, 64, 256)

            loop(4, keep)

        @pl.when(c == 1)
        def _():
            def kept(h):
                part = at_multiple(256 * h, 256)
                for i in range(2):
                    out[part, :] += dot(s.GW[8 + i, h // 2, h % 2].reshape(256, 256), s.WB[256 * i : 256 * i + 256, :])
                    dn[part, :] += dot_t(s.GW[10 + i, h // 2, h % 2].reshape(256, 256), s.WA[0, :, 256 * i : 256 * i + 256])

            loop(4, kept)
            for cp in weights(2, 0):
                cp.start()

        @pl.when(c > 0)
        def _():
            for h in range(4):
                part = pl.ds(256 * h, 256)
                out[part, :] += dot(act[part, :], wout[...])
                dn[part, :] += dot_t(dpre[part, :], win[...])

        scoped('reduce', progress)(c)

    loop(8, scoped('chunk', chunk))
    for j in range(4):
        s.VEC[j : j + 1, :] = jnp.sum(s.bcol[:, 1024 * j : 1024 * j + 1024], axis=0, keepdims=True)
    s.VEC[4:5, :] = column_sums(s)
    s.VEC[5:8, :] = jnp.zeros((3, D), F32)

    def finish_all():
        def units(c):
            places = units_at(c)
            rs.w_wait(3, 2 * c, 2, c)
            rs.w_finish(W_ORDERS[0], 3, 2 * c, c, places[:2])
            rs.w_finish(W_ORDERS[1], 3, 2 * c + 1, c, places[2:])
            rs.o_finish(0, 3, c)
            rs.o_finish(1, 3, c)

        loop(8, units)

    def wait_sent():
        rs.w_wait_sent(16)
        rs.o_wait_sent()

    return progress, finish_all, wait_sent


def attention_role(s, rs, enter):
    nb, g, dcT = s.A.at[0], s.A.at[1], s.A.at[2]
    dn, S1 = s.ACC.at[0], s.ACC.at[1]

    def weights(gr, slot):
        return [
            pltpu.make_async_copy(
                s.w_qkv.at[:, at_multiple(j * 1024 + gr * 256, 256)], s.WA.at[slot, :, pl.ds(256 * j, 256)], s.qsem.at[slot]
            )
            for j in range(3)
        ]

    hc, vc, gc = load_inputs(s, s.hb_qkv, s.hb_dense)
    for cp in weights(0, 0):
        cp.start()
    dc = pltpu.make_async_copy(s.w_dense, s.WB, s.lsem.at[1, 0])
    dc.start()
    gc.start()
    place = lax.broadcasted_iota(jnp.int32, (8, SEQ), 1)
    start = jnp.zeros((8, SEQ), jnp.int32)
    end = jnp.int32(0)
    for d in range(DOCS - 1):
        end = end + s.lens[0, d]
        start = jnp.where(place >= end, end, start)
    inv = np.float32(10000.0) ** (-(np.arange(0, ROT, 2, dtype=np.float32) / np.float32(ROT)))
    row = lax.broadcasted_iota(jnp.int32, (8, SEQ), 0)
    freq = jnp.zeros((8, SEQ), F32)
    for j in range(8):
        freq = jnp.where(row == j, float(inv[j]), freq)
    ang = (place - start).astype(F32) * freq
    co, si = jnp.cos(ang), jnp.sin(ang)
    one, zero = jnp.ones((48, SEQ), F32), jnp.zeros((48, SEQ), F32)
    for j, parts in enumerate(([co, co, one, co, co, one], [-si, si, zero, -si, si, zero])):
        table = jnp.concatenate(parts, axis=0).T
        for i in range(4):
            S1[768:1024, 256 * i + 128 * j : 256 * i + 128 * j + 128] = table[256 * i : 256 * i + 256]
    blocks = [(qb, kb) for qb in range(4) for kb in range(max(0, qb - 2), qb + 1)]

    def mask_at(qb, kb):
        n = blocks.index((qb, kb))
        return s.GO.at[8 + n // 4, :, pl.ds(256 * (n % 4), 256)]

    for qb, kb in blocks:
        kidx = lax.broadcasted_iota(jnp.int32, (256, 256), 0) + 256 * kb
        qidx = lax.broadcasted_iota(jnp.int32, (256, 256), 1) + 256 * qb
        st = start[0:1, 256 * qb : 256 * qb + 256]
        mask_at(qb, kb)[...] = jnp.where((kidx >= st) & (kidx <= qidx), 0.0, -1e9).astype(BF)
    for cp in vc:
        cp.wait()

    def norm(i):
        at = at_multiple(i * 128, 128)
        nb[at, :] = layer_norm(staged_rows(s, i), s.gain[...], s.shift[...])
        dn[at, :] = jnp.zeros((128, D), F32)

    with jax.named_scope("norm"):
        for j in range(4):
            hc[j].wait()
            loop(2 * j + 2, norm, 2 * j)
    gc.wait()
    dc.wait()
    enter()
    E = lambda qb, n: s.GO.at[n + 3 * (qb % 2)]
    DS = lambda n: s.GO.at[11 + n]
    kT, vT = s.GO.at[6], s.GO.at[7]
    query, key, value, d_query = (s.RO2.at[n, :, pl.ds(256 * k, 256)] for n in range(2) for k in range(2))
    lane = lax.broadcasted_iota(jnp.int32, (256, 256), 1)

    def turn(x, i, sign):
        cosines, sines = (S1[768:1024, at_multiple(256 * i + 128 * j, 128)] for j in range(2))
        low = lax.broadcasted_iota(jnp.int32, (256, 128), 1) % 64 < 8
        parts = []
        for j in range(x.shape[1] // 128):
            u = x[:, 128 * j : 128 * j + 128]
            a = jnp.where(low, pltpu.roll(u, 120, 1), pltpu.roll(u, 8, 1)) * sines
            parts.append(u * cosines + a if sign > 0 else u * cosines - a)
        return jnp.concatenate(parts, axis=1)

    def stack(x):
        zb = jnp.zeros_like(x)
        return jnp.concatenate([jnp.where((lane >= 64 * h) & (lane < 64 * h + 64), x, zb) for h in range(4)], axis=0)

    def diag(x):
        return jnp.concatenate([x[64 * h : 64 * h + 64, 256 * h : 256 * h + 256] for h in range(4)], axis=0)

    def rows4(x):
        return jnp.concatenate([jnp.broadcast_to(x[:, 256 * h : 256 * h + 256], (64, 256)) for h in range(4)], axis=0)

    def sum4(x):
        return jnp.concatenate([jnp.sum(x[64 * h : 64 * h + 64], axis=0, keepdims=True) for h in range(4)], axis=1)

    def finish(gr, st):
        @pl.when(gr >= 0)
        def _():
            rs.w_wait(st, 3 * gr, 3, gr)
            for j, order in enumerate(QKV_ORDERS):
                at = 1024 * j + 256 * gr
                rs.w_finish(order, st, 3 * gr + j, gr, (at, at + 128))
            rs.d_finish(st, gr)

    def group(gr):
        slot = lax.rem(gr, 2)

        @pl.when(gr < 3)
        def _():
            for cp in weights(gr + 1, 1 - slot):
                cp.start()

        pltpu.make_async_copy(s.w_qkv.at[:, pl.ds(0, 768)], s.WA.at[slot], s.qsem.at[slot]).wait()
        w = s.WA.at[slot]
        bq = jnp.concatenate([s.b_first[:, at_multiple(1024 * j + gr * 256, 256)] for j in range(3)], axis=1)

        with jax.named_scope("project"):
            for i in range(4):
                at = pl.ds(256 * i, 256)
                raw = dot(nb[at, :], w[...]) + bq
                query[at, :] = turn(raw[:, 0:256], i, 1).astype(BF) * BF(0.125)
                turned = turn(raw[:, 256:512], i, 1)
                key[at, :] = turned.astype(BF)
                kT[:, at] = turned.T.astype(BF)
                value[at, :] = raw[:, 512:768].astype(BF)
                vT[:, at] = raw[:, 512:768].T.astype(BF)
        crow = at_multiple(gr * 256, 256)
        for i in range(2):
            at = pl.ds(512 * i, 512)
            dcT[crow, at] = dot_t(s.WB[crow, :], g[at, :]).astype(BF)
        s.PD[...] = jnp.zeros((SEQ, 512), F32)

        def keys_of(qb):
            return list(range(max(0, qb - 2), qb + 1))

        def score(qb, q4):
            kbs = keys_of(qb)
            m = None
            for n, kb in enumerate(kbs):
                b = mask_at(qb, kb)[...].astype(F32)
                part = dot_t(key[pl.ds(256 * kb, 256), :], q4) + jnp.concatenate([b] * 4, axis=1)
                S1[pl.ds(256 * n, 256), :] = part
                top = jnp.max(part, axis=0, keepdims=True)
                m = top if m is None else jnp.maximum(m, top)
            return m

        def weigh(qb, n, m):
            e = jnp.exp(S1[pl.ds(256 * n, 256), :] - m)
            E(qb, n)[...] = e.astype(BF)
            return jnp.sum(e, axis=0, keepdims=True)

        def context(qb, total):
            kbs = keys_of(qb)
            nk = len(kbs)
            win, qs = pl.ds(256 * kbs[0], 256 * nk), pl.ds(256 * qb, 256)
            ev = s.GO[3 * (qb % 2) : 3 * (qb % 2) + nk].reshape(256 * nk, D)
            cx = dot(vT[:, win], ev)
            li = 1.0 / total
            lsel = rows4(li)
            cT = diag(cx) * lsel
            dcs = (dcT[crow, qs].astype(F32) * lsel).astype(BF).astype(F32)
            dcT[crow, qs] = cT.astype(BF)
            return sum4(cT * dcs), stack(dcs.T.astype(BF))

        def back(qb, q4, inner, dst):
            kbs = keys_of(qb)
            nk = len(kbs)
            win = pl.ds(256 * kbs[0], 256 * nk)
            ev = s.GO[3 * (qb % 2) : 3 * (qb % 2) + nk].reshape(256 * nk, D)
            s.PD[win, 256:512] += dot(ev, dst)
            for n, kb in enumerate(kbs):
                dP = dot_t(value[pl.ds(256 * kb, 256), :], dst)
                DS(n)[...] = (E(qb, n)[...].astype(F32) * (dP - inner)).astype(BF)
            s.PD[win, 0:256] += dot(s.GO[11 : 11 + nk].reshape(256 * nk, D), q4)

        def back_queries(qb):
            kbs = keys_of(qb)
            nk = len(kbs)
            dq = diag(dot(kT[:, pl.ds(256 * kbs[0], 256 * nk)], s.GO[11 : 11 + nk].reshape(256 * nk, D)))
            d_query[pl.ds(256 * qb, 256), :] = turn(dq.T * 0.125, qb, -1).astype(BF)

        with jax.named_scope("heads"):
            q4 = stack(query[0:256, :])
            inner, dst = context(0, weigh(0, 0, score(0, q4)))
            for qb in range(4):
                q4_after = None
                if qb < 3:
                    q4_after = stack(query[256 * qb + 256 : 256 * qb + 512, :])
                    m = score(qb + 1, q4_after)
                back(qb, q4, inner, dst)
                if qb < 3:
                    total = sum(weigh(qb + 1, n, m) for n in range(len(keys_of(qb + 1))))
                back_queries(qb)
                if qb < 3:
                    inner, dst = context(qb + 1, total)
                q4 = q4_after
        scoped('reduce', finish)(gr - 2, 1)
        for i in range(4):
            at = pl.ds(256 * i, 256)
            s.RO3[at, 0:256] = turn(s.PD[at, 0:256], i, -1).astype(BF)
        s.RO3[:, 256:512] = s.PD[:, 256:512].astype(BF)
        for q in range(4):
            tile = t_dot(nb[:, pl.ds(256 * q, 256)], jnp.concatenate([d_query[...], s.RO3[...]], axis=1)).astype(BF)
            for j in range(3):
                s.GW[3 * gr + j, q // 2, q % 2] = tile[:, 256 * j : 256 * j + 256].reshape(2, 2, 64, 256)
        for j, order in enumerate(QKV_ORDERS):
            rs.w_copy(order, 0, 3 * gr + j, gr).start()
        tile = dot(dcT[crow, :], g[...]).astype(BF)
        for j in range(4):
            s.GW[12 + gr, j // 2, j % 2] = tile[:, 256 * j : 256 * j + 256].reshape(2, 2, 64, 256)
        rs.d_start(0, gr)
        for j in range(3):
            s.bcol[:, at_multiple(1024 * j + gr * 256, 256)] = jnp.sum(
                (d_query[...] if j == 0 else s.RO3[:, 256 * j - 256 : 256 * j]).astype(F32).reshape(128, 8, 256), axis=0
            )

        with jax.named_scope("dnormed"):
            for i in range(4):
                at = pl.ds(256 * i, 256)
                dn[at, :] += dot_t(jnp.concatenate([d_query[at, :], s.RO3[at, :]], axis=1), w[...])
        scoped('reduce', finish)(gr - 2, 2)
        scoped('reduce', finish)(gr - 1, 0)

    loop(4, scoped('group', group))

    for i in range(4):
        at = pl.ds(256 * i, 256)
        S1[at, :] = t_dot(dcT[:, at], s.WB[...])
    for j in range(3):
        s.VEC[j : j + 1, :] = jnp.sum(s.bcol[:, 1024 * j : 1024 * j + 1024], axis=0, keepdims=True)
    s.VEC[3:4, :] = column_sums(s)
    s.VEC[6:8, :] = jnp.zeros((2, D), F32)

    def progress(t):
        if t == 7:
            finish(2, 1)
        if t == 9:
            finish(2, 2)
        if 8 <= t < 11:
            finish(3, t - 8)

    def finish_all():
        def units(gr):
            finish(gr, 3)

        loop(4, units)

    def wait_sent():
        rs.w_wait_sent(12)
        rs.d_wait_sent()

    return progress, finish_all, wait_sent


def kernel(extra, *refs):
    s = Scope()
    names = INPUTS + OUTPUTS + tuple(n for n, *_ in SCRATCH) + tuple(n for n, *_ in SEMS) + ("ready",)
    for n, r in zip(names, refs, strict=True):
        setattr(s, n, r)
    rs = Reducer(s, extra)
    pr, dp = rs.pr, rs.dp
    other = (dp, 1 - pr)
    barrier = pltpu.get_barrier_semaphore()
    for b in range(4):
        pl.semaphore_signal(barrier, inc=1, device_id=(rs.partner[b], pr), device_id_type=MESH)
    for line in rs.lines:
        pl.semaphore_signal(barrier, inc=1, device_id=(line[2], pr), device_id_type=MESH)
    pl.semaphore_signal(barrier, inc=1, device_id=other, device_id_type=MESH)
    enter = lambda: pl.semaphore_wait(barrier, 7)

    def to_other(src, dst, ss, sr):
        return pltpu.make_async_remote_copy(src_ref=src, dst_ref=dst, send_sem=ss, recv_sem=sr, device_id=other, device_id_type=MESH)

    def role(is_attention, run):
        progress, finish_all, wait_sent = run(s, rs, enter)
        own_half = 0 if is_attention else 1
        mine, theirs = pl.ds(512 * own_half, 512), pl.ds(512 * (1 - own_half), 512)
        if not is_attention:
            pl.semaphore_signal(s.ready, inc=1, device_id=other, device_id_type=MESH)
        hc = pltpu.make_async_copy(s.hidden, s.A.at[2], s.hsem.at[5])
        hc.start()
        branch = s.A.at[0]

        def pack(i):
            at = at_multiple(i * 128, 128)
            branch[at, :] = (s.ACC[1, at, :] + s.b_last[...]).astype(BF)
            s.WB[at, :] = s.ACC[0, at, :].astype(BF)

        scoped('pack', loop)(8, pack)
        if is_attention:
            pl.semaphore_wait(s.ready, 1)
        to_feed = (s.WA.at[1, pl.ds(0, 512), pl.ds(256, 512)], s.WA.at[1, pl.ds(512, 512), pl.ds(256, 512)], s.WA.at[0], s.WA.at[1, :, pl.ds(0, 256)])
        to_attention = tuple(s.RO1.at[n // 16, n // 2 % 8, n % 2] for n in range(24))
        give_feed = (branch.at[theirs, pl.ds(0, 512)], branch.at[theirs, pl.ds(512, 512)], s.WB.at[:, pl.ds(0, 768)], s.WB.at[:, pl.ds(768, 256)])
        give_attention = tuple(s.WB.at[pl.ds(128 * (n // 2), 128), pl.ds(512 * (n % 2), 512)] for n in range(16)) + tuple(
            branch.at[pl.ds(512 * (1 - own_half) + 128 * (n // 2), 128), pl.ds(512 * (n % 2), 512)] for n in range(8)
        )
        give, land = (give_feed, to_feed) if is_attention else (give_attention, to_attention)
        moves = [to_other(src, dst, s.xs.at[0], s.xr.at[0]) for src, dst in zip(give, land)]
        all_moves = to_other(s.WA, s.WA, s.xs.at[0], s.xr.at[0])
        for cp in moves:
            cp.start()
        def start_vectors(hop):
            copies = [
                pltpu.make_async_remote_copy(
                    src_ref=s.VEC, dst_ref=s.VRECV.at[3 * hop + k], send_sem=s.vs.at[3 * hop + k], recv_sem=s.vr.at[3 * hop + k],
                    device_id=(to, pr), device_id_type=MESH,
                )
                for k, to in enumerate(rs.lines[hop])
            ]
            for cp in copies:
                cp.start()
            return copies

        def end_vectors(hop, copies):
            for cp in copies:
                scoped('vec', cp.wait)()
            s.VEC[...] += s.VRECV[3 * hop] + s.VRECV[3 * hop + 1] + s.VRECV[3 * hop + 2]

        if is_attention:
            scoped('reduce7', progress)(7)
        else:
            copies = start_vectors(0)
        scoped('reduce8', progress)(8)
        hc.wait()
        scoped('moves', all_moves.wait_recv)()
        s.lnsum[...] = jnp.zeros((2, 8, D), F32)

        def last(i):
            at = at_multiple(i * 128, 128)
            x = s.A[2, at, :].astype(F32)
            mean = jnp.mean(x, axis=1, keepdims=True)
            cen = x - mean
            inv = lax.rsqrt(jnp.mean(cen * cen, axis=1, keepdims=True) + EPS)
            x_hat = cen * inv
            a = s.WB[at, :].astype(F32)
            if is_attention:
                b = jnp.concatenate([s.RO1[0, i, n] for n in range(2)], axis=1).astype(F32)
            else:
                b = jnp.concatenate([s.WA[0, at, :], s.WA[1, at, 0:256]], axis=1).astype(F32)
            dnv = (a + b).astype(BF).astype(F32)
            e = dnv * s.gain[...]
            grad = s.A[1, at, :].astype(F32) + inv * (
                e - jnp.mean(e, axis=1, keepdims=True) - x_hat * jnp.mean(e * x_hat, axis=1, keepdims=True)
            )
            if is_attention:
                s.lnsum[0] += jnp.sum((dnv * x_hat).reshape(16, 8, D), axis=0)
                s.lnsum[1] += jnp.sum(dnv.reshape(16, 8, D), axis=0)

            @pl.when(i // 4 == own_half)
            def _():
                if is_attention:
                    got = jnp.concatenate([s.RO1[1, lax.rem(i, 4), n] for n in range(2)], axis=1)
                else:
                    here = 128 * lax.rem(i, 4)
                    got = jnp.concatenate([s.WA[1, at_multiple(here, 128), 256:768], s.WA[1, at_multiple(512 + here, 128), 256:768]], axis=1)
                attn, mlp = (branch[at, :], got) if is_attention else (got, branch[at, :])
                branch[at, :] = (x + attn.astype(F32) + mlp.astype(F32)).astype(BF)

            s.A[2, at, :] = grad.astype(BF)

        scoped('last', loop)(8, last)
        outs = [
            pltpu.make_async_copy(branch.at[mine], s.o_out, s.fl.at[0]),
            pltpu.make_async_copy(s.A.at[2], s.o_ig, s.fl.at[1]),
        ]
        for cp in outs:
            cp.start()
        if is_attention:
            for j in range(2):
                s.VEC[4 + j : 5 + j, :] = jnp.sum(s.lnsum[j], axis=0, keepdims=True)
        if is_attention:
            copies = start_vectors(0)
            scoped('reduce9', progress)(9)
            end_vectors(0, copies)
            copies = start_vectors(1)
            scoped('reduce10', progress)(10)
        else:
            end_vectors(0, copies)
            copies = start_vectors(1)
            for t in range(9, 8 + LAGS[2]):
                scoped(f'reduce{t}', progress)(t)
        scoped('finish', finish_all)()
        end_vectors(1, copies)
        vx = to_other(s.VEC, s.VPART, s.vs.at[6], s.vr.at[6])
        vx.start()

        def split(first, size, half):
            return pl.ds(first, size) if extra > 1 else pl.ds(first + half * (size // 2), size // 2)

        def pieces(attention, half):
            wide = [s.o_qkv.at[:, pl.ds(1024 * k, 1024)] for k in range(3)] + [s.o_dense]
            if not attention:
                wide = [s.o_in.at[:, pl.ds(1024 * k, 1024)] for k in range(4)]
            parts = [(s.ACC.at[0, split(64 * k, 64, half)], to) for k, to in enumerate(wide)]
            return parts if attention else parts + [(s.ACC.at[0, split(256, 256, half)], s.o_outw)]

        sent, local = [], []
        for n, (src, dst) in enumerate(pieces(is_attention, 1 - own_half)):
            cp = to_other(src, dst, s.fs.at[n], s.fr.at[n])
            cp.start()
            sent.append(cp)
        for n, (src, dst) in enumerate(pieces(is_attention, own_half)):
            cp = pltpu.make_async_copy(src, dst, s.fl.at[2 + n])
            cp.start()
            local.append(cp)
        vx.wait()
        for n, (src, k) in enumerate(((s.VEC, own_half), (s.VPART, 1 - own_half))):
            cp = pltpu.make_async_copy(src, s.o_vec.at[k], s.fl.at[7 + n])
            cp.start()
            local.append(cp)
        scoped('sent', wait_sent)()
        all_moves.wait_send()
        for cp in outs + local:
            cp.wait()
        for cp in sent:
            cp.wait_send()
        for n, (src, dst) in enumerate(pieces(not is_attention, own_half)):
            to_other(src, dst, s.fs.at[n], s.fr.at[n]).wait_recv()

    pl.when(pr == 0)(lambda: role(True, attention_role))
    pl.when(pr == 1)(lambda: role(False, feed_role))


def call(extra, *args):
    rows = 32 if extra == 1 else 64
    outw = 128 if extra == 1 else 256
    anywhere, smem = (pl.BlockSpec(memory_space=m) for m in (pl.ANY, pltpu.SMEM))
    shapes = [
        ((512, D), BF), ((SEQ, D), BF), ((rows, 3072), F32), ((rows, D), F32), ((rows, FF), F32), ((outw, D), F32), ((2, 8, D), F32),
    ]
    return pl.pallas_call(
        partial(kernel, extra),
        out_shape=[jax.ShapeDtypeStruct(*x) for x in shapes],
        in_specs=[anywhere, smem] + [anywhere] * 11,
        out_specs=[anywhere] * 7,
        scratch_shapes=[pltpu.VMEM(shape, kind) for _, shape, kind in SCRATCH]
        + [pltpu.SemaphoreType.DMA(shape) for _, shape in SEMS]
        + [pltpu.SemaphoreType.REGULAR],
        compiler_params=pltpu.CompilerParams(collective_id=0, has_side_effects=True, vmem_limit_bytes=VMEM_LIMIT),
        cost_estimate=pl.CostEstimate(flops=50 * 10**9, bytes_accessed=40 * 10**6, transcendentals=10**7),
    )(*args)


VMEM_LIMIT = 62 * 2**20


def deliver(count, *refs):
    big, vec, outs, small, held, sems = refs[:6], refs[6], refs[7:13], refs[13:19], refs[19:25], refs[25]
    take = [pltpu.make_async_copy(src, mid, sems.at[0, n]) for n, (src, mid) in enumerate(zip(big, held))]
    give = [pltpu.make_async_copy(mid, dst, sems.at[1, n]) for n, (mid, dst) in enumerate(zip(held, outs))]
    for cp in take:
        cp.start()
    place = lax.axis_index("dp") * 2 + lax.axis_index("pair")

    def tile(role, row, at):
        held = vec[role, :, at_multiple(128 * lax.rem(at, 8), 128)]
        return jnp.sum(jnp.where(sub == row + at // 8, held, 0.0), axis=0, keepdims=True)

    lane = lax.broadcasted_iota(jnp.int32, (1, 128), 1)
    sub = lax.broadcasted_iota(jnp.int32, (8, 128), 0)
    for out, (role, row, rows) in zip(small, ((0, 0, 3), (0, 3, 1), (1, 0, 4), (1, 4, 1), (0, 4, 1), (0, 5, 1))):
        size = rows * D // count
        at = place * size
        first, skip = at // 128, lax.rem(at, 128)
        turned = pltpu.roll(tile(role, row, first), lax.rem(128 - skip, 128), 1)
        if 128 % size:
            after = pltpu.roll(tile(role, row, jnp.minimum(first + 1, 8 * rows - 1)), lax.rem(128 - skip, 128), 1)
            turned = jnp.where(lane < 128 - skip, turned, after)
        out[...] = turned[:, 0:size]
    for one, other in zip(take, give):
        one.wait()
        other.start()
    for cp in give:
        cp.wait()


def swap(x, bit):
    return lax.ppermute(x, "dp", [(i, i ^ bit) for i in range(lax.axis_size("dp"))])


def halve(x, bit):
    half = x.shape[0] // 2
    up = (lax.axis_index("dp") // bit) % 2
    keep = lax.dynamic_slice_in_dim(x, up * half, half, 0)
    give = lax.dynamic_slice_in_dim(x, (1 - up) * half, half, 0)
    return keep + swap(give, bit)


def body(hidden, doc_lengths, ln_gain, ln_bias, qkv_weight, qkv_bias, dense_weight, dense_bias, fc_in_weight, fc_in_bias, fc_out_weight, fc_out_bias, cotangent):
    extra = lax.axis_size("dp") // INNER
    output, input_grad, qkv, dense, w_in, w_out, vec = call(
        extra, hidden, doc_lengths, ln_gain[None], ln_bias[None], qkv_weight, qkv_bias[None], dense_weight, dense_bias[None],
        fc_in_weight, fc_in_bias[None], fc_out_weight, fc_out_bias[None], cotangent,
    )
    dp, pair = lax.axis_index("dp"), lax.axis_index("pair")
    if extra > 1:
        bit = extra // 2
        while bit:
            qkv, dense, w_in, w_out = (halve(x, bit) for x in (qkv, dense, w_in, w_out))
            vec = vec + swap(vec, bit)
            bit //= 2
        qkv, dense, w_in, w_out = (
            lax.dynamic_slice_in_dim(x, pair * (x.shape[0] // 2), x.shape[0] // 2, 0) for x in (qkv, dense, w_in, w_out)
        )
    big = (output, input_grad, qkv, dense, w_in, w_out)
    count = lax.axis_size("dp") * 2
    sizes = (3072, D, FF, D, D, D)
    *big, qkv_b, dense_b, in_b, out_b, gain, shift = pl.pallas_call(
        partial(deliver, count),
        out_shape=[jax.ShapeDtypeStruct(x.shape, x.dtype) for x in big]
        + [jax.ShapeDtypeStruct((1, n // count), F32) for n in sizes],
        in_specs=[pl.BlockSpec(memory_space=pl.ANY)] * 6 + [pl.BlockSpec(memory_space=pltpu.VMEM)],
        out_specs=[pl.BlockSpec(memory_space=pl.ANY)] * 6 + [pl.BlockSpec(memory_space=pltpu.VMEM)] * 6,
        scratch_shapes=[pltpu.VMEM(x.shape, x.dtype) for x in big] + [pltpu.SemaphoreType.DMA((2, 6))],
    )(*big, vec)
    output, input_grad, qkv, dense, w_in, w_out = big
    qkv_b, dense_b, in_b, out_b, gain, shift = (x.reshape(-1) for x in (qkv_b, dense_b, in_b, out_b, gain, shift))
    return output, input_grad, qkv, qkv_b, dense, dense_b, w_in, in_b, w_out, out_b, gain, shift


def solution(mesh):
    rows = P("dp", None)
    shard, shard1 = P(("dp", "pair"), None), P(("dp", "pair"))
    return jax.shard_map(
        body,
        mesh=mesh,
        in_specs=(rows, rows) + (P(),) * 10 + (rows,),
        out_specs=(shard, rows, shard, shard1, shard, shard1, shard, shard1, shard, shard1, shard1, shard1),
        check_vma=False,
    )
```

```python
from functools import partial

import jax
import jax.numpy as jnp
import numpy as np
from jax import lax
from jax.experimental import pallas as pl
from jax.experimental.pallas import tpu as pltpu
from jax.sharding import PartitionSpec as P

F32, BF = jnp.float32, jnp.bfloat16
MESH = pl.DeviceIdType.MESH
EPS = 1e-05
SEQ, D, FF, HEAD, ROT, DOCS = 1024, 1024, 4096, 64, 16, 8
INNER = 16
W_ORDERS = ((1, 0, 2, 3), (0, 1, 2, 3))
O_ORDERS = ((1, 2, 0, 3), (2, 0, 1, 3))
QKV_ORDERS = ((2, 1, 0, 3), (0, 1, 2, 3), (0, 2, 1, 3))
LAGS = (1, 2, 3)


def dot(a, b):
    return lax.dot_general(a, b, (((1,), (0,)), ((), ())), preferred_element_type=F32)


def dot_t(a, b):
    return lax.dot_general(a, b, (((1,), (1,)), ((), ())), preferred_element_type=F32)


def t_dot(a, b):
    return lax.dot_general(a, b, (((0,), (0,)), ((), ())), preferred_element_type=F32)


def scoped(name, f):
    def g(*a, **k):
        with jax.named_scope(name):
            return f(*a, **k)
    return g


def loop(n, body, first=0):
    def step(i, c):
        body(i)
        return c

    lax.fori_loop(first, n, step, 0)


def at_multiple(start, size, of=None):
    return pl.ds(pl.multiple_of(start, of or size), size)


def xor(a, b):
    return a + b - 2 * a * b


class Scope:
    pass


SCRATCH = (
    ("A", (3, SEQ, D), BF),
    ("ACC", (2, SEQ, D), F32),
    ("WA", (2, D, 768), BF),
    ("WB", (D, D), BF),
    ("PD", (SEQ, 512), F32),
    ("GW", (16, 2, 2, 2, 2, 64, 256), BF),
    ("RW1", (16, 2, 2, 2, 64, 256), BF),
    ("RW2", (16, 2, 2, 64, 256), BF),
    ("RW3", (16, 2, 64, 256), BF),
    ("RW4", (16, 64, 256), BF),
    ("GO", (16, 256, D), BF),
    ("RO1", (2, 8, 2, 128, 512), BF),
    ("RO2", (2, SEQ, 512), BF),
    ("RO3", (SEQ, 512), BF),
    ("RO4", (2, 2, 128, 512), BF),
    ("gain", (1, D), F32),
    ("shift", (1, D), F32),
    ("b_first", (1, 4096), F32),
    ("b_last", (1, D), F32),
    ("bcol", (8, 4096), F32),
    ("bsum", (8, D), F32),
    ("lnsum", (2, 8, D), F32),
    ("VEC", (8, D), F32),
    ("VRECV", (6, 8, D), F32),
    ("VPART", (8, D), F32),
)
SEMS = (
    ("lsem", (2, 2)),
    ("hsem", (6,)),
    ("qsem", (2,)),
    ("ws", (4,)),
    ("wr", (8, 4)),
    ("os", (2, 4)),
    ("orr", (8, 2)),
    ("orr2", (2, 4)),
    ("orr3", (2, 2)),
    ("ds", (4,)),
    ("dr", (4, 4)),
    ("vs", (7,)),
    ("vr", (7,)),
    ("xs", (1,)),
    ("xr", (1,)),
    ("fs", (5,)),
    ("fr", (5,)),
    ("fl", (9,)),
    ("bsem", (4,)),
)
INPUTS = ("hidden", "lens", "h_gain", "h_shift", "w_qkv", "hb_qkv", "w_dense", "hb_dense", "w_in", "hb_in", "w_out", "hb_out", "cot")
OUTPUTS = ("o_out", "o_ig", "o_qkv", "o_dense", "o_in", "o_outw", "o_vec")


class Reducer:
    def __init__(self, s, extra):
        self.s, self.extra = s, extra
        dp = lax.axis_index("dp")
        inner = dp // extra
        self.dp, self.pr = dp, lax.axis_index("pair")
        self.bits = [inner % 2, (inner // 2) % 2, (inner // 4) % 2, inner // 8]
        step = [(1 - 2 * self.bits[b]) * (extra << b) for b in range(4)]
        self.partner = [dp + step[b] for b in range(4)]
        self.lines = ((self.partner[2], self.partner[3], dp + step[2] + step[3]), (self.partner[0], self.partner[1], dp + step[0] + step[1]))

    def to(self, src, dst, ss, rs, b):
        return pltpu.make_async_remote_copy(
            src_ref=src, dst_ref=dst, send_sem=ss, recv_sem=rs, device_id=(self.partner[b], self.pr), device_id_type=MESH
        )

    def wait_bytes(self, ref, sem, sent):
        cp = self.to(ref, ref, sem, sem, 0)
        cp.wait_send() if sent else cp.wait_recv()

    def w_half(self, order, st, u, bit):
        s = self.s
        left = [b for b in (3, 2, 1, 0) if b not in order[:st]]
        ref = (s.GW, s.RW1, s.RW2, s.RW3)[st]
        return ref.at[(u,) + (slice(None),) * left.index(order[st]) + (bit,)]

    def w_copy(self, order, st, u, k):
        s, b = self.s, order[st]
        dst = (s.RW1, s.RW2, s.RW3, s.RW4)[st].at[u]
        return self.to(self.w_half(order, st, u, 1 - self.bits[b]), dst, s.ws.at[st], s.wr.at[k, st], b)

    def w_wait(self, st, u, n, k):
        s = self.s
        self.wait_bytes((s.RW1, s.RW2, s.RW3, s.RW4)[st].at[pl.ds(u, n)], s.wr.at[k, st], False)

    def w_wait_sent(self, n):
        s = self.s
        for st, ref in enumerate((s.RW1, s.RW2, s.RW3, s.RW4)):
            self.wait_bytes(ref.at[pl.ds(0, n)], s.ws.at[st], True)

    def w_finish(self, order, st, u, k, cols):
        s, b = self.s, order[st]
        kept = self.w_half(order, st, u, self.bits[b])
        got = (s.RW1, s.RW2, s.RW3, s.RW4)[st].at[u]
        if st < 3:
            lead = got.shape[0]
            for i in range(lead):
                got[i] = (got[i].astype(F32) + kept[i].astype(F32)).astype(BF)
            self.w_copy(order, st + 1, u, k).start()
        else:
            total = got[...].astype(F32) + kept[...].astype(F32)
            for i, at in enumerate(cols):
                s.ACC[0, at_multiple(64 * (at // 1024), 64), at_multiple(lax.rem(at, 1024), 128)] = total[:, 128 * i : 128 * i + 128]

    def d_copies(self, st, gr):
        s, (x, y, zl, zh) = self.s, self.bits
        u = 12 + gr
        low, high = zl == gr % 2, zh == gr // 2

        def copy(src, dst, bit):
            return self.to(src, dst, s.ds.at[st], s.dr.at[gr, st], bit)

        if st == 0:
            return True, True, [
                copy(s.GW.at[u, 0, :, :, 1 - x], s.RW1.at[u, 0], 0), copy(s.GW.at[u, 1, :, 1 - y], s.RW1.at[u, 1], 1)
            ]
        if st == 1:
            return True, True, [
                copy(s.RW1.at[u, 0, :, 1 - y], s.RW2.at[u, 0], 1), copy(s.RW1.at[u, 1, :, 1 - x], s.RW2.at[u, 1], 0)
            ]
        if st == 2:
            return jnp.logical_not(low), low, [copy(s.RW2.at[u], self.d3(gr), 2)]
        return low & jnp.logical_not(high), low & high, [copy(self.d3(gr).at[j], s.RW4.at[pl.ds(12 + 2 * j, 2)], 3) for j in range(2)]

    def d3(self, gr):
        return self.s.RW3.at[pl.ds(12 + 2 * (gr // 2), 2)]

    def d_start(self, st, gr):
        sends, _, copies = self.d_copies(st, gr)

        @pl.when(sends)
        def _():
            for cp in copies:
                cp.start()

    def d_wait_sent(self):
        s, (x, y, zl, zh) = self.s, self.bits
        units = pl.ds(12, 4)
        for st, ref in enumerate((s.RW1.at[units], s.RW2.at[units], s.RW3.at[units], s.RW4.at[units])):
            self.wait_bytes(ref, s.ds.at[st], True)

    def d_finish(self, st, gr):
        s, (x, y, _, _) = self.s, self.bits
        u = 12 + gr
        _, takes, copies = self.d_copies(st, gr)

        @pl.when(takes)
        def _():
            self.wait_bytes((s.RW1.at[u], s.RW2.at[u], self.d3(gr), s.RW4.at[pl.ds(12, 4)])[st], s.dr.at[gr, st], False)
            if st == 0:
                for j in range(2):
                    s.RW1[u, 0, j] = (s.RW1[u, 0, j].astype(F32) + s.GW[u, 0, j, :, x].astype(F32)).astype(BF)
                    s.RW1[u, 1, j] = (s.RW1[u, 1, j].astype(F32) + s.GW[u, 1, j, y].astype(F32)).astype(BF)
            elif st == 1:
                s.RW2[u, 0] = (s.RW2[u, 0].astype(F32) + s.RW1[u, 0, :, y].astype(F32)).astype(BF)
                s.RW2[u, 1] = (s.RW2[u, 1].astype(F32) + s.RW1[u, 1, :, x].astype(F32)).astype(BF)
            elif st == 2:
                got = self.d3(gr)
                got[...] = (got[...].astype(F32) + s.RW2[u].astype(F32)).astype(BF)
            else:
                for j in range(4):
                    total = s.RW4[12 + j].astype(F32) + self.d3(gr)[j // 2, j % 2].astype(F32)
                    s.ACC[0, 192:256, 256 * j : 256 * j + 256] = total

        if st < 3:
            self.d_start(st + 1, gr)

    def chunk_of(self, c):
        return c % 2, (c // 2) % 2, c // 4

    def shard(self, c, x, y):
        a, b, _ = self.chunk_of(c)
        return x + 2 * y + 4 * xor(a, xor(x, y)) + 8 * xor(b, x)

    def ro2(self, n, c):
        return self.s.RO2.at[n, at_multiple(128 * c, 128)]

    def ro3(self, n, c):
        return self.s.RO3.at[at_multiple(512 * n + 128 * (c // 2), 128)]

    def o_shard(self, n, c, first, second):
        a, _, _ = self.chunk_of(c)
        p, q, r, _ = O_ORDERS[n]
        bit = {p: first, q: second, r: xor(a, xor(first, second))}
        return self.shard(c, bit[0], bit[1])

    def o_copies(self, n, st, c):
        s, own = self.s, self.bits
        a, b, h = self.chunk_of(c)
        p, q, r, _ = O_ORDERS[n]
        here = xor(a, xor(own[p], own[q])) == own[r]
        mine = here & (xor(b, own[0]) == own[3])

        def copy(src, dst, bit):
            come = s.orr.at[c, st] if st < 2 else s.orr2.at[n, c // 2] if st == 2 else s.orr3.at[n, h]
            return self.to(src, dst, s.os.at[n, st], come, bit)

        if st == 0:
            copies = []
            for k in range(2):
                src = s.GO.at[self.o_shard(n, c, 1 - own[p], k), at_multiple(128 * h, 128), pl.ds(512 * n, 512)]
                copies.append(copy(src, s.RO1.at[n, c, k], p))
            return True, True, copies
        if st == 1:
            return True, True, [copy(s.RO1.at[n, c, 1 - own[q]], self.ro2(n, c), q)]
        if st == 2:
            return jnp.logical_not(here), here, [copy(self.ro2(n, c), self.ro3(n, c), r)]
        return here & jnp.logical_not(mine), mine, [copy(self.ro3(n, c), s.RO4.at[n, h], 3)]

    def o_start(self, n, st, c):
        sends, _, copies = self.o_copies(n, st, c)

        @pl.when(sends)
        def _():
            for cp in copies:
                cp.start()

    def o_wait_sent(self):
        s = self.s
        for n in range(2):
            for st, ref in enumerate((s.RO1.at[n], s.RO2.at[n], s.RO3.at[pl.ds(512 * n, 512)], s.RO4.at[n])):
                self.wait_bytes(ref, s.os.at[n, st], True)

    def o_wait(self, st, c):
        s = self.s
        self.wait_bytes(s.RO1.at[:, c] if st == 0 else s.RO2.at[:, at_multiple(128 * c, 128)], s.orr.at[c, st], False)

    def o_finish(self, n, st, c):
        s, own = self.s, self.bits
        _, _, h = self.chunk_of(c)
        p, q, _, _ = O_ORDERS[n]
        lanes = pl.ds(512 * n, 512)
        _, takes, copies = self.o_copies(n, st, c)

        @pl.when(takes)
        def _():
            if st > 1:
                copies[0].wait_recv()
            if st == 0:
                for k in range(2):
                    kept = s.GO[self.o_shard(n, c, own[p], k), at_multiple(128 * h, 128), lanes]
                    s.RO1[n, c, k] = (s.RO1[n, c, k].astype(F32) + kept.astype(F32)).astype(BF)
            elif st == 1:
                got = self.ro2(n, c)
                got[...] = (got[...].astype(F32) + s.RO1[n, c, own[q]].astype(F32)).astype(BF)
            elif st == 2:
                got = self.ro3(n, c)
                got[...] = (got[...].astype(F32) + self.ro2(n, c)[...].astype(F32)).astype(BF)
            else:
                s.ACC[0, at_multiple(256 + 128 * h, 128), lanes] = s.RO4[n, h].astype(F32) + self.ro3(n, c)[...].astype(F32)

        if st < 3:
            self.o_start(n, st + 1, c)


def layer_norm(x, gain, shift):
    x = x.astype(F32)
    mean = jnp.mean(x, axis=1, keepdims=True)
    cen = x - mean
    inv = lax.rsqrt(jnp.mean(cen * cen, axis=1, keepdims=True) + EPS)
    return (cen * inv * gain + shift).astype(BF)


A1, A2, A3, A4, A5 = 0.254829592, -0.284496736, 1.421413741, -1.453152027, 1.061405429


def gelu_both(x):
    e = jnp.exp(-0.5 * (x * x))
    t = 1.0 / (1.0 + (0.3275911 * 0.7071067811865476) * jnp.abs(x))
    poly = ((((0.5 * A5) * t + (0.5 * A4)) * t + (0.5 * A3)) * t + (0.5 * A2)) * t + (0.5 * A1)
    q = poly * t * e
    cdf = jnp.where(x >= 0, 1.0 - q, q)
    return cdf, x * (e * 0.3989422804014327)


def load_inputs(s, first, last):
    hc = [pltpu.make_async_copy(s.hidden.at[pl.ds(256 * j, 256)], s.GO.at[12 + j], s.hsem.at[j]) for j in range(4)]
    gc = pltpu.make_async_copy(s.cot, s.A.at[1], s.hsem.at[4])
    n = first.shape[1]
    vectors = ((s.h_gain, s.gain), (s.h_shift, s.shift), (first, s.b_first.at[:, pl.ds(0, n)]), (last, s.b_last))
    vc = [pltpu.make_async_copy(src, dst, s.bsem.at[j]) for j, (src, dst) in enumerate(vectors)]
    for cp in hc + vc:
        cp.start()
    return hc, vc, gc


def column_sums(s):
    def tile(i):
        s.bsum[...] += jnp.sum(s.A[1, at_multiple(i * 256, 256), :].astype(F32).reshape(32, 8, D), axis=0)

    s.bsum[...] = jnp.zeros((8, D), F32)
    loop(4, tile)
    return jnp.sum(s.bsum[...], axis=0, keepdims=True)


def staged_rows(s, i):
    return s.GO[12 + i // 2, at_multiple(128 * lax.rem(i, 2), 128), :]


def feed_role(s, rs, enter):
    nb, g = s.A.at[0], s.A.at[1]
    dn, out = s.ACC.at[0], s.ACC.at[1]
    act, dpre = s.A.at[2, :, pl.ds(0, 512)], s.A.at[2, :, pl.ds(512, 512)]

    def units_at(c):
        return [256 * rs.shard(c, p % 2, p // 2) + 128 * (c // 4) for p in range(4)]

    def weights(c, slot):
        copies = []
        for p, at in enumerate(units_at(c)):
            cols = at_multiple(at, 128)
            copies.append(pltpu.make_async_copy(s.w_in.at[:, cols], s.WA.at[slot, :, pl.ds(128 * p, 128)], s.lsem.at[0, slot]))
            copies.append(pltpu.make_async_copy(s.w_out.at[cols, :], s.WB.at[at_multiple(512 * slot + 128 * p, 128)], s.lsem.at[1, slot]))
        return copies

    def weights_here(slot):
        pltpu.make_async_copy(s.w_in.at[:, pl.ds(0, 512)], s.WA.at[slot, :, pl.ds(0, 512)], s.lsem.at[0, slot]).wait()
        pltpu.make_async_copy(s.w_out.at[pl.ds(0, 512), :], s.WB.at[at_multiple(512 * slot, 512)], s.lsem.at[1, slot]).wait()

    hc, vc, gc = load_inputs(s, s.hb_in, s.hb_out)
    for cp in vc:
        cp.wait()

    def norm(i):
        at = at_multiple(i * 128, 128)
        nb[at, :] = layer_norm(staged_rows(s, i), s.gain[...], s.shift[...])
        dn[at, :] = jnp.zeros((128, D), F32)
        out[at, :] = jnp.zeros((128, D), F32)

    with jax.named_scope("norm"):
        for j in range(4):
            hc[j].wait()
            if j == 1:
                for cp in weights(0, 0):
                    cp.start()
                gc.start()
            loop(2 * j + 2, norm, 2 * j)
    gc.wait()
    enter()

    def progress(t):
        for st in (2, 1, 0):
            c = t - LAGS[st]

            @pl.when((c >= 0) & (c < 8))
            def _(st=st, c=c):
                rs.w_wait(st, 2 * c, 2, c)
                rs.w_finish(W_ORDERS[0], st, 2 * c, c, None)
                rs.w_finish(W_ORDERS[1], st, 2 * c + 1, c, None)
                if st < 2:
                    rs.o_wait(st, c)
                rs.o_finish(0, st, c)
                rs.o_finish(1, st, c)

    def chunk(c):
        slot = lax.rem(c, 2)

        @pl.when((c < 7) & (c != 1))
        def _():
            for cp in weights(c + 1, 1 - slot):
                cp.start()

        weights_here(slot)
        win, wout = s.WA.at[slot, :, pl.ds(0, 512)], s.WB.at[at_multiple(512 * slot, 512)]
        places = units_at(c)
        bias = jnp.concatenate([s.b_first[:, at_multiple(at, 128)] for at in places], axis=1)
        bacc = jnp.zeros((8, 512), F32)
        for rt in range(2):
            rows = pl.ds(512 * rt, 512)
            s.PD[0:512, :] = dot(nb[rows, :], win[...]) + bias
            s.PD[512:1024, :] = dot_t(g[rows, :], wout[...])
            for q in range(4):
                r, r2, ro = pl.ds(128 * q, 128), pl.ds(512 + 128 * q, 128), pl.ds(512 * rt + 128 * q, 128)
                pre = s.PD[r, :]
                cdf, xphi = gelu_both(pre)
                act[ro, :] = (pre * cdf).astype(BF)
                dp = (s.PD[r2, :] * (cdf + xphi)).astype(BF)
                dpre[ro, :] = dp
                bacc = bacc + jnp.sum(dp.astype(F32).reshape(16, 8, 512), axis=0)
        for p, at in enumerate(places):
            s.bcol[:, at_multiple(at, 128)] = bacc[:, 128 * p : 128 * p + 128]
        for i in range(2):
            tile = t_dot(act[:, 256 * i : 256 * i + 256], g[...]).astype(BF)
            for p in range(2 * i, 2 * i + 2):
                s.GO[rs.shard(c, p % 2, p // 2), at_multiple(128 * (c // 4), 128), :] = tile[128 * (p % 2) : 128 * (p % 2) + 128]
        rs.o_start(0, 0, c)
        rs.o_start(1, 0, c)
        for q in range(4):
            tile = t_dot(nb[:, pl.ds(256 * q, 256)], dpre[...]).astype(BF)
            for i in range(2):
                s.GW[2 * c + i, q // 2, q % 2] = tile[:, 256 * i : 256 * i + 256].reshape(2, 2, 64, 256)
        rs.w_copy(W_ORDERS[0], 0, 2 * c, c).start()
        rs.w_copy(W_ORDERS[1], 0, 2 * c + 1, c).start()

        @pl.when(c == 0)
        def _():
            def keep(i):
                at = at_multiple(256 * i, 256)
                for k in range(4):
                    s.GW[8 + k, i // 2, i % 2] = s.A[2, at, 256 * k : 256 * k + 256].reshape(2, 2, 64, 256)

            loop(4, keep)

        @pl.when(c == 1)
        def _():
            def kept(h):
                part = at_multiple(256 * h, 256)
                for i in range(2):
                    out[part, :] += dot(s.GW[8 + i, h // 2, h % 2].reshape(256, 256), s.WB[256 * i : 256 * i + 256, :])
                    dn[part, :] += dot_t(s.GW[10 + i, h // 2, h % 2].reshape(256, 256), s.WA[0, :, 256 * i : 256 * i + 256])

            loop(4, kept)
            for cp in weights(2, 0):
                cp.start()

        @pl.when(c > 0)
        def _():
            for h in range(4):
                part = pl.ds(256 * h, 256)
                out[part, :] += dot(act[part, :], wout[...])
                dn[part, :] += dot_t(dpre[part, :], win[...])

        scoped('reduce', progress)(c)

    loop(8, scoped('chunk', chunk))
    for j in range(4):
        s.VEC[j : j + 1, :] = jnp.sum(s.bcol[:, 1024 * j : 1024 * j + 1024], axis=0, keepdims=True)
    s.VEC[4:5, :] = column_sums(s)
    s.VEC[5:8, :] = jnp.zeros((3, D), F32)

    def finish_all():
        def units(c):
            places = units_at(c)
            rs.w_wait(3, 2 * c, 2, c)
            rs.w_finish(W_ORDERS[0], 3, 2 * c, c, places[:2])
            rs.w_finish(W_ORDERS[1], 3, 2 * c + 1, c, places[2:])
            rs.o_finish(0, 3, c)
            rs.o_finish(1, 3, c)

        loop(8, units)

    def wait_sent():
        rs.w_wait_sent(16)
        rs.o_wait_sent()

    return progress, finish_all, wait_sent


def attention_role(s, rs, enter):
    nb, g, dcT = s.A.at[0], s.A.at[1], s.A.at[2]
    dn, S1 = s.ACC.at[0], s.ACC.at[1]

    def weights(gr, slot):
        return [
            pltpu.make_async_copy(
                s.w_qkv.at[:, at_multiple(j * 1024 + gr * 256, 256)], s.WA.at[slot, :, pl.ds(256 * j, 256)], s.qsem.at[slot]
            )
            for j in range(3)
        ]

    hc, vc, gc = load_inputs(s, s.hb_qkv, s.hb_dense)
    for cp in weights(0, 0):
        cp.start()
    dc = pltpu.make_async_copy(s.w_dense, s.WB, s.lsem.at[1, 0])
    dc.start()
    gc.start()
    place = lax.broadcasted_iota(jnp.int32, (8, SEQ), 1)
    start = jnp.zeros((8, SEQ), jnp.int32)
    end = jnp.int32(0)
    for d in range(DOCS - 1):
        end = end + s.lens[0, d]
        start = jnp.where(place >= end, end, start)
    inv = np.float32(10000.0) ** (-(np.arange(0, ROT, 2, dtype=np.float32) / np.float32(ROT)))
    row = lax.broadcasted_iota(jnp.int32, (8, SEQ), 0)
    freq = jnp.zeros((8, SEQ), F32)
    for j in range(8):
        freq = jnp.where(row == j, float(inv[j]), freq)
    ang = (place - start).astype(F32) * freq
    co, si = jnp.cos(ang), jnp.sin(ang)
    one, zero = jnp.ones((48, SEQ), F32), jnp.zeros((48, SEQ), F32)
    for j, parts in enumerate(([co, co, one, co, co, one], [-si, si, zero, -si, si, zero])):
        table = jnp.concatenate(parts, axis=0).T
        for i in range(4):
            S1[768:1024, 256 * i + 128 * j : 256 * i + 128 * j + 128] = table[256 * i : 256 * i + 256]
    blocks = [(qb, kb) for qb in range(4) for kb in range(max(0, qb - 2), qb + 1)]

    def mask_at(qb, kb):
        n = blocks.index((qb, kb))
        return s.GO.at[8 + n // 4, :, pl.ds(256 * (n % 4), 256)]

    for qb, kb in blocks:
        kidx = lax.broadcasted_iota(jnp.int32, (256, 256), 0) + 256 * kb
        qidx = lax.broadcasted_iota(jnp.int32, (256, 256), 1) + 256 * qb
        st = start[0:1, 256 * qb : 256 * qb + 256]
        mask_at(qb, kb)[...] = jnp.where((kidx >= st) & (kidx <= qidx), 0.0, -1e9).astype(BF)
    for cp in vc:
        cp.wait()

    def norm(i):
        at = at_multiple(i * 128, 128)
        nb[at, :] = layer_norm(staged_rows(s, i), s.gain[...], s.shift[...])
        dn[at, :] = jnp.zeros((128, D), F32)

    with jax.named_scope("norm"):
        for j in range(4):
            hc[j].wait()
            loop(2 * j + 2, norm, 2 * j)
    gc.wait()
    dc.wait()
    enter()
    E = lambda qb, n: s.GO.at[n + 3 * (qb % 2)]
    DS = lambda n: s.GO.at[11 + n]
    kT, vT = s.GO.at[6], s.GO.at[7]
    query, key, value, d_query = (s.RO2.at[n, :, pl.ds(256 * k, 256)] for n in range(2) for k in range(2))
    lane = lax.broadcasted_iota(jnp.int32, (256, 256), 1)

    def turn(x, i, sign):
        cosines, sines = (S1[768:1024, at_multiple(256 * i + 128 * j, 128)] for j in range(2))
        low = lax.broadcasted_iota(jnp.int32, (256, 128), 1) % 64 < 8
        parts = []
        for j in range(x.shape[1] // 128):
            u = x[:, 128 * j : 128 * j + 128]
            a = jnp.where(low, pltpu.roll(u, 120, 1), pltpu.roll(u, 8, 1)) * sines
            parts.append(u * cosines + a if sign > 0 else u * cosines - a)
        return jnp.concatenate(parts, axis=1)

    def stack(x):
        zb = jnp.zeros_like(x)
        return jnp.concatenate([jnp.where((lane >= 64 * h) & (lane < 64 * h + 64), x, zb) for h in range(4)], axis=0)

    def diag(x):
        return jnp.concatenate([x[64 * h : 64 * h + 64, 256 * h : 256 * h + 256] for h in range(4)], axis=0)

    def rows4(x):
        return jnp.concatenate([jnp.broadcast_to(x[:, 256 * h : 256 * h + 256], (64, 256)) for h in range(4)], axis=0)

    def sum4(x):
        return jnp.concatenate([jnp.sum(x[64 * h : 64 * h + 64], axis=0, keepdims=True) for h in range(4)], axis=1)

    def finish(gr, st):
        @pl.when(gr >= 0)
        def _():
            rs.w_wait(st, 3 * gr, 3, gr)
            for j, order in enumerate(QKV_ORDERS):
                at = 1024 * j + 256 * gr
                rs.w_finish(order, st, 3 * gr + j, gr, (at, at + 128))
            rs.d_finish(st, gr)

    def group(gr):
        slot = lax.rem(gr, 2)

        @pl.when(gr < 3)
        def _():
            for cp in weights(gr + 1, 1 - slot):
                cp.start()

        pltpu.make_async_copy(s.w_qkv.at[:, pl.ds(0, 768)], s.WA.at[slot], s.qsem.at[slot]).wait()
        w = s.WA.at[slot]
        bq = jnp.concatenate([s.b_first[:, at_multiple(1024 * j + gr * 256, 256)] for j in range(3)], axis=1)

        with jax.named_scope("project"):
            for i in range(4):
                at = pl.ds(256 * i, 256)
                raw = dot(nb[at, :], w[...]) + bq
                query[at, :] = turn(raw[:, 0:256], i, 1).astype(BF) * BF(0.125)
                turned = turn(raw[:, 256:512], i, 1)
                key[at, :] = turned.astype(BF)
                kT[:, at] = turned.T.astype(BF)
                value[at, :] = raw[:, 512:768].astype(BF)
                vT[:, at] = raw[:, 512:768].T.astype(BF)
        crow = at_multiple(gr * 256, 256)
        for i in range(2):
            at = pl.ds(512 * i, 512)
            dcT[crow, at] = dot_t(s.WB[crow, :], g[at, :]).astype(BF)
        s.PD[...] = jnp.zeros((SEQ, 512), F32)

        def keys_of(qb):
            return list(range(max(0, qb - 2), qb + 1))

        def score(qb, q4):
            kbs = keys_of(qb)
            m = None
            for n, kb in enumerate(kbs):
                b = mask_at(qb, kb)[...].astype(F32)
                part = dot_t(key[pl.ds(256 * kb, 256), :], q4) + jnp.concatenate([b] * 4, axis=1)
                S1[pl.ds(256 * n, 256), :] = part
                top = jnp.max(part, axis=0, keepdims=True)
                m = top if m is None else jnp.maximum(m, top)
            return m

        def weigh(qb, n, m):
            e = jnp.exp(S1[pl.ds(256 * n, 256), :] - m)
            E(qb, n)[...] = e.astype(BF)
            return jnp.sum(e, axis=0, keepdims=True)

        def context(qb, total):
            kbs = keys_of(qb)
            nk = len(kbs)
            win, qs = pl.ds(256 * kbs[0], 256 * nk), pl.ds(256 * qb, 256)
            ev = s.GO[3 * (qb % 2) : 3 * (qb % 2) + nk].reshape(256 * nk, D)
            cx = dot(vT[:, win], ev)
            li = 1.0 / total
            lsel = rows4(li)
            cT = diag(cx) * lsel
            dcs = (dcT[crow, qs].astype(F32) * lsel).astype(BF).astype(F32)
            dcT[crow, qs] = cT.astype(BF)
            return sum4(cT * dcs), stack(dcs.T.astype(BF))

        def back(qb, q4, inner, dst):
            kbs = keys_of(qb)
            nk = len(kbs)
            win = pl.ds(256 * kbs[0], 256 * nk)
            ev = s.GO[3 * (qb % 2) : 3 * (qb % 2) + nk].reshape(256 * nk, D)
            s.PD[win, 256:512] += dot(ev, dst)
            for n, kb in enumerate(kbs):
                dP = dot_t(value[pl.ds(256 * kb, 256), :], dst)
                DS(n)[...] = (E(qb, n)[...].astype(F32) * (dP - inner)).astype(BF)
            s.PD[win, 0:256] += dot(s.GO[11 : 11 + nk].reshape(256 * nk, D), q4)

        def back_queries(qb):
            kbs = keys_of(qb)
            nk = len(kbs)
            dq = diag(dot(kT[:, pl.ds(256 * kbs[0], 256 * nk)], s.GO[11 : 11 + nk].reshape(256 * nk, D)))
            d_query[pl.ds(256 * qb, 256), :] = turn(dq.T * 0.125, qb, -1).astype(BF)

        with jax.named_scope("heads"):
            q4 = stack(query[0:256, :])
            inner, dst = context(0, weigh(0, 0, score(0, q4)))
            for qb in range(4):
                q4_after = None
                if qb < 3:
                    q4_after = stack(query[256 * qb + 256 : 256 * qb + 512, :])
                    m = score(qb + 1, q4_after)
                back(qb, q4, inner, dst)
                if qb < 3:
                    total = sum(weigh(qb + 1, n, m) for n in range(len(keys_of(qb + 1))))
                back_queries(qb)
                if qb < 3:
                    inner, dst = context(qb + 1, total)
                q4 = q4_after
        scoped('reduce', finish)(gr - 2, 1)
        for i in range(4):
            at = pl.ds(256 * i, 256)
            s.RO3[at, 0:256] = turn(s.PD[at, 0:256], i, -1).astype(BF)
        s.RO3[:, 256:512] = s.PD[:, 256:512].astype(BF)
        for q in range(4):
            tile = t_dot(nb[:, pl.ds(256 * q, 256)], jnp.concatenate([d_query[...], s.RO3[...]], axis=1)).astype(BF)
            for j in range(3):
                s.GW[3 * gr + j, q // 2, q % 2] = tile[:, 256 * j : 256 * j + 256].reshape(2, 2, 64, 256)
        for j, order in enumerate(QKV_ORDERS):
            rs.w_copy(order, 0, 3 * gr + j, gr).start()
        tile = dot(dcT[crow, :], g[...]).astype(BF)
        for j in range(4):
            s.GW[12 + gr, j // 2, j % 2] = tile[:, 256 * j : 256 * j + 256].reshape(2, 2, 64, 256)
        rs.d_start(0, gr)
        for j in range(3):
            s.bcol[:, at_multiple(1024 * j + gr * 256, 256)] = jnp.sum(
                (d_query[...] if j == 0 else s.RO3[:, 256 * j - 256 : 256 * j]).astype(F32).reshape(128, 8, 256), axis=0
            )

        with jax.named_scope("dnormed"):
            for i in range(4):
                at = pl.ds(256 * i, 256)
                dn[at, :] += dot_t(jnp.concatenate([d_query[at, :], s.RO3[at, :]], axis=1), w[...])
        scoped('reduce', finish)(gr - 2, 2)
        scoped('reduce', finish)(gr - 1, 0)

    loop(4, scoped('group', group))

    for i in range(4):
        at = pl.ds(256 * i, 256)
        S1[at, :] = t_dot(dcT[:, at], s.WB[...])
    for j in range(3):
        s.VEC[j : j + 1, :] = jnp.sum(s.bcol[:, 1024 * j : 1024 * j + 1024], axis=0, keepdims=True)
    s.VEC[3:4, :] = column_sums(s)
    s.VEC[6:8, :] = jnp.zeros((2, D), F32)

    def progress(t):
        if t == 7:
            finish(2, 1)
        if t == 9:
            finish(2, 2)
        if 8 <= t < 11:
            finish(3, t - 8)

    def finish_all():
        def units(gr):
            finish(gr, 3)

        loop(4, units)

    def wait_sent():
        rs.w_wait_sent(12)
        rs.d_wait_sent()

    return progress, finish_all, wait_sent


def kernel(extra, *refs):
    s = Scope()
    names = INPUTS + OUTPUTS + tuple(n for n, *_ in SCRATCH) + tuple(n for n, *_ in SEMS) + ("ready",)
    for n, r in zip(names, refs, strict=True):
        setattr(s, n, r)
    rs = Reducer(s, extra)
    pr, dp = rs.pr, rs.dp
    other = (dp, 1 - pr)
    barrier = pltpu.get_barrier_semaphore()
    for b in range(4):
        pl.semaphore_signal(barrier, inc=1, device_id=(rs.partner[b], pr), device_id_type=MESH)
    for line in rs.lines:
        pl.semaphore_signal(barrier, inc=1, device_id=(line[2], pr), device_id_type=MESH)
    pl.semaphore_signal(barrier, inc=1, device_id=other, device_id_type=MESH)
    enter = lambda: pl.semaphore_wait(barrier, 7)

    def to_other(src, dst, ss, sr):
        return pltpu.make_async_remote_copy(src_ref=src, dst_ref=dst, send_sem=ss, recv_sem=sr, device_id=other, device_id_type=MESH)

    def role(is_attention, run):
        progress, finish_all, wait_sent = run(s, rs, enter)
        own_half = 0 if is_attention else 1
        mine, theirs = pl.ds(512 * own_half, 512), pl.ds(512 * (1 - own_half), 512)
        if not is_attention:
            pl.semaphore_signal(s.ready, inc=1, device_id=other, device_id_type=MESH)
        hc = pltpu.make_async_copy(s.hidden, s.A.at[2], s.hsem.at[5])
        hc.start()
        branch = s.A.at[0]

        def pack(i):
            at = at_multiple(i * 128, 128)
            branch[at, :] = (s.ACC[1, at, :] + s.b_last[...]).astype(BF)
            s.WB[at, :] = s.ACC[0, at, :].astype(BF)

        scoped('pack', loop)(8, pack)
        if is_attention:
            pl.semaphore_wait(s.ready, 1)
        to_feed = (s.WA.at[1, pl.ds(0, 512), pl.ds(256, 512)], s.WA.at[1, pl.ds(512, 512), pl.ds(256, 512)], s.WA.at[0], s.WA.at[1, :, pl.ds(0, 256)])
        to_attention = tuple(s.RO1.at[n // 16, n // 2 % 8, n % 2] for n in range(24))
        give_feed = (branch.at[theirs, pl.ds(0, 512)], branch.at[theirs, pl.ds(512, 512)], s.WB.at[:, pl.ds(0, 768)], s.WB.at[:, pl.ds(768, 256)])
        give_attention = tuple(s.WB.at[pl.ds(128 * (n // 2), 128), pl.ds(512 * (n % 2), 512)] for n in range(16)) + tuple(
            branch.at[pl.ds(512 * (1 - own_half) + 128 * (n // 2), 128), pl.ds(512 * (n % 2), 512)] for n in range(8)
        )
        give, land = (give_feed, to_feed) if is_attention else (give_attention, to_attention)
        moves = [to_other(src, dst, s.xs.at[0], s.xr.at[0]) for src, dst in zip(give, land)]
        all_moves = to_other(s.WA, s.WA, s.xs.at[0], s.xr.at[0])
        for cp in moves:
            cp.start()
        def start_vectors(hop):
            copies = [
                pltpu.make_async_remote_copy(
                    src_ref=s.VEC, dst_ref=s.VRECV.at[3 * hop + k], send_sem=s.vs.at[3 * hop + k], recv_sem=s.vr.at[3 * hop + k],
                    device_id=(to, pr), device_id_type=MESH,
                )
                for k, to in enumerate(rs.lines[hop])
            ]
            for cp in copies:
                cp.start()
            return copies

        def end_vectors(hop, copies):
            for cp in copies:
                scoped('vec', cp.wait)()
            s.VEC[...] += s.VRECV[3 * hop] + s.VRECV[3 * hop + 1] + s.VRECV[3 * hop + 2]

        if is_attention:
            scoped('reduce7', progress)(7)
        else:
            copies = start_vectors(0)
        scoped('reduce8', progress)(8)
        hc.wait()
        scoped('moves', all_moves.wait_recv)()
        s.lnsum[...] = jnp.zeros((2, 8, D), F32)

        def last(i):
            at = at_multiple(i * 128, 128)
            x = s.A[2, at, :].astype(F32)
            mean = jnp.mean(x, axis=1, keepdims=True)
            cen = x - mean
            inv = lax.rsqrt(jnp.mean(cen * cen, axis=1, keepdims=True) + EPS)
            x_hat = cen * inv
            a = s.WB[at, :].astype(F32)
            if is_attention:
                b = jnp.concatenate([s.RO1[0, i, n] for n in range(2)], axis=1).astype(F32)
            else:
                b = jnp.concatenate([s.WA[0, at, :], s.WA[1, at, 0:256]], axis=1).astype(F32)
            dnv = (a + b).astype(BF).astype(F32)
            e = dnv * s.gain[...]
            grad = s.A[1, at, :].astype(F32) + inv * (
                e - jnp.mean(e, axis=1, keepdims=True) - x_hat * jnp.mean(e * x_hat, axis=1, keepdims=True)
            )
            if is_attention:
                s.lnsum[0] += jnp.sum((dnv * x_hat).reshape(16, 8, D), axis=0)
                s.lnsum[1] += jnp.sum(dnv.reshape(16, 8, D), axis=0)

            @pl.when(i // 4 == own_half)
            def _():
                if is_attention:
                    got = jnp.concatenate([s.RO1[1, lax.rem(i, 4), n] for n in range(2)], axis=1)
                else:
                    here = 128 * lax.rem(i, 4)
                    got = jnp.concatenate([s.WA[1, at_multiple(here, 128), 256:768], s.WA[1, at_multiple(512 + here, 128), 256:768]], axis=1)
                attn, mlp = (branch[at, :], got) if is_attention else (got, branch[at, :])
                branch[at, :] = (x + attn.astype(F32) + mlp.astype(F32)).astype(BF)

            s.A[2, at, :] = grad.astype(BF)

        scoped('last', loop)(8, last)
        outs = [
            pltpu.make_async_copy(branch.at[mine], s.o_out, s.fl.at[0]),
            pltpu.make_async_copy(s.A.at[2], s.o_ig, s.fl.at[1]),
        ]
        for cp in outs:
            cp.start()
        if is_attention:
            for j in range(2):
                s.VEC[4 + j : 5 + j, :] = jnp.sum(s.lnsum[j], axis=0, keepdims=True)
        if is_attention:
            copies = start_vectors(0)
            scoped('reduce9', progress)(9)
            scoped('reduce10', progress)(10)
            end_vectors(0, copies)
            copies = start_vectors(1)
        else:
            end_vectors(0, copies)
            copies = start_vectors(1)
            for t in range(9, 8 + LAGS[2]):
                scoped(f'reduce{t}', progress)(t)
        scoped('finish', finish_all)()
        end_vectors(1, copies)
        vx = to_other(s.VEC, s.VPART, s.vs.at[6], s.vr.at[6])
        vx.start()

        def split(first, size, half):
            return pl.ds(first, size) if extra > 1 else pl.ds(first + half * (size // 2), size // 2)

        def pieces(attention, half):
            wide = [s.o_qkv.at[:, pl.ds(1024 * k, 1024)] for k in range(3)] + [s.o_dense]
            if not attention:
                wide = [s.o_in.at[:, pl.ds(1024 * k, 1024)] for k in range(4)]
            parts = [(s.ACC.at[0, split(64 * k, 64, half)], to) for k, to in enumerate(wide)]
            return parts if attention else parts + [(s.ACC.at[0, split(256, 256, half)], s.o_outw)]

        sent, local = [], []
        for n, (src, dst) in enumerate(pieces(is_attention, 1 - own_half)):
            cp = to_other(src, dst, s.fs.at[n], s.fr.at[n])
            cp.start()
            sent.append(cp)
        for n, (src, dst) in enumerate(pieces(is_attention, own_half)):
            cp = pltpu.make_async_copy(src, dst, s.fl.at[2 + n])
            cp.start()
            local.append(cp)
        vx.wait()
        for n, (src, k) in enumerate(((s.VEC, own_half), (s.VPART, 1 - own_half))):
            cp = pltpu.make_async_copy(src, s.o_vec.at[k], s.fl.at[7 + n])
            cp.start()
            local.append(cp)
        scoped('sent', wait_sent)()
        all_moves.wait_send()
        for cp in outs + local:
            cp.wait()
        for cp in sent:
            cp.wait_send()
        for n, (src, dst) in enumerate(pieces(not is_attention, own_half)):
            to_other(src, dst, s.fs.at[n], s.fr.at[n]).wait_recv()

    pl.when(pr == 0)(lambda: role(True, attention_role))
    pl.when(pr == 1)(lambda: role(False, feed_role))


def call(extra, *args):
    rows = 32 if extra == 1 else 64
    outw = 128 if extra == 1 else 256
    anywhere, smem = (pl.BlockSpec(memory_space=m) for m in (pl.ANY, pltpu.SMEM))
    shapes = [
        ((512, D), BF), ((SEQ, D), BF), ((rows, 3072), F32), ((rows, D), F32), ((rows, FF), F32), ((outw, D), F32), ((2, 8, D), F32),
    ]
    return pl.pallas_call(
        partial(kernel, extra),
        out_shape=[jax.ShapeDtypeStruct(*x) for x in shapes],
        in_specs=[anywhere, smem] + [anywhere] * 11,
        out_specs=[anywhere] * 7,
        scratch_shapes=[pltpu.VMEM(shape, kind) for _, shape, kind in SCRATCH]
        + [pltpu.SemaphoreType.DMA(shape) for _, shape in SEMS]
        + [pltpu.SemaphoreType.REGULAR],
        compiler_params=pltpu.CompilerParams(collective_id=0, has_side_effects=True, vmem_limit_bytes=VMEM_LIMIT),
        cost_estimate=pl.CostEstimate(flops=50 * 10**9, bytes_accessed=40 * 10**6, transcendentals=10**7),
    )(*args)


VMEM_LIMIT = 62 * 2**20


def deliver(count, *refs):
    big, vec, outs, small, held, sems = refs[:6], refs[6], refs[7:13], refs[13:19], refs[19:25], refs[25]
    take = [pltpu.make_async_copy(src, mid, sems.at[0, n]) for n, (src, mid) in enumerate(zip(big, held))]
    give = [pltpu.make_async_copy(mid, dst, sems.at[1, n]) for n, (mid, dst) in enumerate(zip(held, outs))]
    for cp in take:
        cp.start()
    place = lax.axis_index("dp") * 2 + lax.axis_index("pair")

    def tile(role, row, at):
        held = vec[role, :, at_multiple(128 * lax.rem(at, 8), 128)]
        return jnp.sum(jnp.where(sub == row + at // 8, held, 0.0), axis=0, keepdims=True)

    lane = lax.broadcasted_iota(jnp.int32, (1, 128), 1)
    sub = lax.broadcasted_iota(jnp.int32, (8, 128), 0)
    for out, (role, row, rows) in zip(small, ((0, 0, 3), (0, 3, 1), (1, 0, 4), (1, 4, 1), (0, 4, 1), (0, 5, 1))):
        size = rows * D // count
        at = place * size
        first, skip = at // 128, lax.rem(at, 128)
        turned = pltpu.roll(tile(role, row, first), lax.rem(128 - skip, 128), 1)
        if 128 % size:
            after = pltpu.roll(tile(role, row, jnp.minimum(first + 1, 8 * rows - 1)), lax.rem(128 - skip, 128), 1)
            turned = jnp.where(lane < 128 - skip, turned, after)
        out[...] = turned[:, 0:size]
    for one, other in zip(take, give):
        one.wait()
        other.start()
    for cp in give:
        cp.wait()


def swap(x, bit):
    return lax.ppermute(x, "dp", [(i, i ^ bit) for i in range(lax.axis_size("dp"))])


def halve(x, bit):
    half = x.shape[0] // 2
    up = (lax.axis_index("dp") // bit) % 2
    keep = lax.dynamic_slice_in_dim(x, up * half, half, 0)
    give = lax.dynamic_slice_in_dim(x, (1 - up) * half, half, 0)
    return keep + swap(give, bit)


def body(hidden, doc_lengths, ln_gain, ln_bias, qkv_weight, qkv_bias, dense_weight, dense_bias, fc_in_weight, fc_in_bias, fc_out_weight, fc_out_bias, cotangent):
    extra = lax.axis_size("dp") // INNER
    output, input_grad, qkv, dense, w_in, w_out, vec = call(
        extra, hidden, doc_lengths, ln_gain[None], ln_bias[None], qkv_weight, qkv_bias[None], dense_weight, dense_bias[None],
        fc_in_weight, fc_in_bias[None], fc_out_weight, fc_out_bias[None], cotangent,
    )
    dp, pair = lax.axis_index("dp"), lax.axis_index("pair")
    if extra > 1:
        bit = extra // 2
        while bit:
            qkv, dense, w_in, w_out = (halve(x, bit) for x in (qkv, dense, w_in, w_out))
            vec = vec + swap(vec, bit)
            bit //= 2
        qkv, dense, w_in, w_out = (
            lax.dynamic_slice_in_dim(x, pair * (x.shape[0] // 2), x.shape[0] // 2, 0) for x in (qkv, dense, w_in, w_out)
        )
    big = (output, input_grad, qkv, dense, w_in, w_out)
    count = lax.axis_size("dp") * 2
    sizes = (3072, D, FF, D, D, D)
    *big, qkv_b, dense_b, in_b, out_b, gain, shift = pl.pallas_call(
        partial(deliver, count),
        out_shape=[jax.ShapeDtypeStruct(x.shape, x.dtype) for x in big]
        + [jax.ShapeDtypeStruct((1, n // count), F32) for n in sizes],
        in_specs=[pl.BlockSpec(memory_space=pl.ANY)] * 6 + [pl.BlockSpec(memory_space=pltpu.VMEM)],
        out_specs=[pl.BlockSpec(memory_space=pl.ANY)] * 6 + [pl.BlockSpec(memory_space=pltpu.VMEM)] * 6,
        scratch_shapes=[pltpu.VMEM(x.shape, x.dtype) for x in big] + [pltpu.SemaphoreType.DMA((2, 6))],
    )(*big, vec)
    output, input_grad, qkv, dense, w_in, w_out = big
    qkv_b, dense_b, in_b, out_b, gain, shift = (x.reshape(-1) for x in (qkv_b, dense_b, in_b, out_b, gain, shift))
    return output, input_grad, qkv, qkv_b, dense, dense_b, w_in, in_b, w_out, out_b, gain, shift


def solution(mesh):
    rows = P("dp", None)
    shard, shard1 = P(("dp", "pair"), None), P(("dp", "pair"))
    return jax.shard_map(
        body,
        mesh=mesh,
        in_specs=(rows, rows) + (P(),) * 10 + (rows,),
        out_specs=(shard, rows, shard, shard1, shard, shard1, shard, shard1, shard, shard1, shard1, shard1),
        check_vma=False,
    )
```
